512 devices in a mesh: seq: 64 (over y, z), chan: 8 (over x, core).
Axes of the slice: x: 4, y: 4, z: 16, core: 2. Of those that a mesh axis runs over, the one named last changes fastest.
Arguments:
- x1: bfloat16 [8192, 4096], P('seq', 'chan'), may hold values from -6 to 6
- x2: bfloat16 [8192, 4096], P('seq', 'chan'), may hold values from -6 to 6
- value: bfloat16 [8192, 4096], P('seq', 'chan'), may hold values from -6 to 6
- out_grad: bfloat16 [8192, 4096], P('seq', 'chan'), may hold values from -6 to 6
- short_weight: float32 [3, 4096], P(None, 'chan'), may hold values from -3.5 to 3.5
- coef: float32 [64, 4096], P(None, 'chan'), may hold values from -0.75 to 0.75
- rate: float32 [64], replicated, may hold values from 0.2 to 273.06667, as said below
Outputs:
- layer_output: bfloat16 [8192, 4096], P('seq', 'chan')
- grad_x1: bfloat16 [8192, 4096], P('seq', 'chan')
- grad_value: bfloat16 [8192, 4096], P('seq', 'chan')
- grad_coef: float32 [64, 4096], P(None, 'chan')
- grad_rate: float32 [64], replicated
The draws below stay inside these ranges and needn't reach their ends.
Inputs may be any that keep to these rules, and one draw needn't show every extreme that they name: `rate`: decay rates of the basis functions, per 8192 positions.
All inputs are finite; a program needn't handle non-finite values.
Results may differ from the reference program's by a relative error of at most 0.011.
Values may be sent and summed in bfloat16 or wider, within the bound.
No kernel may reach another device: no remote copies, remote signals or barrier semaphores. Data moves between devices by JAX's collectives and lax.ppermute only.
A program may use at most 64 MiB of HBM per device.

```python
import math
import jax
import jax.numpy as jnp
from jax import lax

D = 4096
SHORT_LEN = 3
ORDER = 64
SEQ_LEN = 8192


def draw_rate(key, part):
    key = jax.random.fold_in(key, 11)
    key_order, key_slow, key_fast = jax.random.split(key, 3)
    order = jax.random.permutation(key_order, jnp.arange(ORDER, dtype=jnp.int32))
    slow_count = ORDER // 2
    slow = order < slow_count
    slow_rate = jnp.exp(jax.random.uniform(key_slow, (ORDER,), jnp.float32, math.log(0.2), math.log(2.0)))
    fast_rate = jnp.exp(jax.random.uniform(key_fast, (ORDER,), jnp.float32, math.log(SEQ_LEN / 256.0), math.log(SEQ_LEN / 30.0)))
    return jnp.where(slow, slow_rate, fast_rate).astype(jnp.float32)


def block_scale(rng, extent, shards, low, high):
    factor_of, own = 1.0, jax.random.fold_in(rng, 6)
    for dim, blocks in shards:
        steps = jnp.exp(jax.random.uniform(jax.random.fold_in(own, dim), (blocks,), jnp.float32, low / len(shards), high / len(shards)))
        factor_of = factor_of * jnp.repeat(steps, extent[dim] // blocks).reshape([-1 if axis == dim else 1 for axis in range(len(extent))])
    return factor_of


def scatter_about(key, shape, scale, bound, cuts=(), kind=jnp.bfloat16):
    level = block_scale(key, shape, cuts, -0.22, 0.18) if cuts else 1.0
    values = jax.random.normal(key, shape, jnp.float32) * scale * level
    return jnp.minimum(jnp.maximum(values, -bound), bound).astype(kind)


def setup_inputs(seed: int = 0) -> dict:
    seeds = jax.random.split(jax.random.key(seed), 8)
    x1 = scatter_about(seeds[0], (SEQ_LEN, D), 1.0, 6.0, ((0, 64), (1, 8)))
    x2 = scatter_about(seeds[1], (SEQ_LEN, D), 1.0, 6.0, ((0, 64), (1, 8)))
    value = scatter_about(seeds[2], (SEQ_LEN, D), 1.0, 6.0, ((0, 64), (1, 8)))
    out_grad = scatter_about(seeds[3], (SEQ_LEN, D), 1.0, 6.0, ((0, 64), (1, 8)))
    short_weight = scatter_about(seeds[4], (SHORT_LEN, D), SHORT_LEN ** -0.5, 3.5, ((1, 8),), jnp.float32)
    coef = scatter_about(seeds[5], (ORDER, D), ORDER ** -0.5, 0.75, ((1, 8),), jnp.float32)
    rate = draw_rate(jax.random.fold_in(seeds[7], 71), 0)
    return dict(x1=x1, x2=x2, value=value, out_grad=out_grad, short_weight=short_weight, coef=coef, rate=rate)


def basis_pair(rate, length):
    position = jnp.arange(length, dtype=jnp.int32)
    index = jnp.arange(rate.shape[0], dtype=jnp.int32)
    cycles = (index // 2 + 1) * (index // 2 + 1)
    turned = position[:, None] * cycles[None, :] % length
    angle = 2.0 * math.pi / length * turned.astype(jnp.float32)
    wave = jnp.where(index[None, :] % 2 == 0, jnp.cos(angle), jnp.sin(angle))
    scaled = position.astype(jnp.float32)[:, None] / length
    envelope = jnp.sqrt(2.0 * rate / length)[None, :] * jnp.exp(-rate[None, :] * scaled)
    phi = envelope * wave
    psi = (0.5 / rate[None, :] - scaled) * phi
    return (phi, psi)

def reference(x1, x2, value, out_grad, short_weight, coef, rate):
    length = x1.shape[0]
    width = x1.shape[1]
    total = 2 * length
    taps = short_weight.shape[0]
    block = math.gcd(width, 512)
    count = width // block
    phi, psi = basis_pair(rate, length)
    highest = lax.Precision.HIGHEST

    def one_block(number):
        start = number * block

        def take(array):
            return lax.dynamic_slice_in_dim(array, start, block, 1)
        first = take(x1).astype(jnp.float32)
        second = take(x2).astype(jnp.float32)
        stream = take(value).astype(jnp.float32)
        cotangent = take(out_grad).astype(jnp.float32)
        weights = take(short_weight)
        mixing = take(coef)
        padded = jnp.concatenate([jnp.zeros((taps - 1, block), jnp.float32), stream], axis=0)
        mixed = weights[0][None, :] * padded[taps - 1:taps - 1 + length]
        for shift_k in range(1, taps):
            mixed = mixed + weights[shift_k][None, :] * padded[taps - 1 - shift_k:taps - 1 - shift_k + length]
        gated = (first * mixed).astype(jnp.bfloat16)
        grad_conv = (cotangent * second).astype(jnp.bfloat16)
        kernel = jnp.dot(phi, mixing, precision=highest)
        spec_u = jnp.fft.rfft(gated.astype(jnp.float32), n=total, axis=0)
        spec_d = jnp.fft.rfft(grad_conv.astype(jnp.float32), n=total, axis=0)
        spec_h = jnp.fft.rfft(kernel, n=total, axis=0)
        conv = jnp.fft.irfft(spec_u * spec_h, n=total, axis=0)[:length]
        grad_gated = jnp.fft.irfft(jnp.conj(spec_h) * spec_d, n=total, axis=0)[:length]
        grad_filter = jnp.fft.irfft(jnp.conj(spec_u) * spec_d, n=total, axis=0)[:length]
        out_y = (second * conv).astype(jnp.bfloat16)
        out_x1 = (grad_gated * mixed).astype(jnp.bfloat16)
        grad_mixed = grad_gated * first
        dpadded = jnp.concatenate([grad_mixed, jnp.zeros((taps - 1, block), jnp.float32)], axis=0)
        back = weights[0][None, :] * dpadded[0:length]
        for shift_k in range(1, taps):
            back = back + weights[shift_k][None, :] * dpadded[shift_k:shift_k + length]
        out_value = back.astype(jnp.bfloat16)
        coef_part = jnp.dot(phi.T, grad_filter, precision=highest) * length ** (-0.5)
        rate_part = lax.optimization_barrier(jnp.sum(psi * jnp.dot(grad_filter, mixing.T, precision=highest), axis=0))
        return (out_y, out_x1, out_value, coef_part, rate_part)
    result = lax.map(one_block, jnp.arange(count, dtype=jnp.int32))

    def unblock(array):
        return jnp.transpose(array, (1, 0, 2)).reshape(array.shape[1], width)
    grad_rate = lax.optimization_barrier(jnp.sum(result[4], axis=0)) * (length * width) ** (-0.5)
    return (unblock(result[0]), unblock(result[1]), unblock(result[2]), unblock(result[3]), grad_rate)
```

```python
import math

import jax
import jax.numpy as jnp
import numpy as np
from jax import lax
from jax.experimental import pallas as pl
from jax.experimental.pallas import tpu as pltpu
from jax.sharding import PartitionSpec as P

f32 = jnp.float32
bf16 = jnp.bfloat16
highest = lax.Precision.HIGHEST
LENGTH = 8192
ROWS = 128
ORDER = 64
LANES = 128
OWN = 8
NT = (((1,), (1,)), ((), ()))
TN = (((0,), (0,)), ((), ()))

VMEM = pl.BlockSpec(memory_space=pltpu.VMEM)
SMEM = pl.BlockSpec(memory_space=pltpu.SMEM)


def wave_tables():
    index = np.arange(ORDER)
    cycles = (index // 2 + 1) ** 2
    odd = index % 2 == 1

    def turn(power):
        angle = 2.0 * math.pi / LENGTH * (power[:, None] * cycles[None, :] % LENGTH)
        return np.cos(angle), np.sin(angle)

    ahead = np.arange(ROWS)
    cos_a, sin_a = turn(ahead)
    cos_b, sin_b = turn(ROWS - ahead)
    real_b = np.where(odd, sin_b, cos_b)
    imag_b = np.where(odd, -cos_b, sin_b)
    wave = np.where(odd, sin_a, cos_a)
    cos_l, sin_l = turn(np.array([ROWS]))
    twice = [np.concatenate([t, t], axis=1).astype(np.float32) for t in (cos_a, sin_a, real_b, imag_b, wave)]
    step = np.concatenate([np.concatenate([t, t], axis=1) for t in (cos_l, sin_l)], axis=0).astype(np.float32)
    return (*twice, step)


def split(table):
    high = table.astype(bf16)
    low = (table - high.astype(f32)).astype(bf16)
    return jnp.concatenate([high, low], axis=0)


def table_kernel(
    place, rate, coef, cos_a, sin_a, real_b, imag_b, wave, step, tx, tg, mf, me, wd, small
):
    lane = lax.broadcasted_iota(jnp.int32, (ROWS, LANES), 1)
    power = lax.broadcasted_iota(jnp.int32, (ROWS, LANES), 0).astype(f32)
    left = lane < ORDER
    slope = rate[...] * (-1.0 / LENGTH)
    env_a = jnp.exp(slope * power)
    env_b = jnp.exp(slope * (ROWS - power))
    ar = env_a * cos_a[...]
    ai = env_a * sin_a[...]
    br = env_b * real_b[...]
    bi = env_b * imag_b[...]
    back = ROWS - power
    tx[...] = split(
        jnp.concatenate([br, bi, jnp.where(left, 0.0, back * br), jnp.where(left, 0.0, back * bi)], axis=1)
    )
    tg[...] = split(
        jnp.concatenate([ar, ai, jnp.where(left, ar, power * ar), jnp.where(left, ai, power * ai)], axis=1)
    )
    mf[...] = jnp.where(left, ar, ai).astype(bf16)
    me[...] = jnp.where(left, br, bi).astype(bf16)
    w = env_a * wave[...]
    wd[...] = jnp.where(left, w, power * w)
    pick = lax.broadcasted_iota(jnp.int32, (OWN, coef.shape[1]), 1) - place[0] * OWN
    pick = (pick == lax.broadcasted_iota(jnp.int32, (OWN, coef.shape[1]), 0)).astype(f32)
    own = lax.dot_general(
        pick, jnp.concatenate([coef[...], coef[...]], axis=0), NT, precision=highest, preferred_element_type=f32
    )
    scale = own * jnp.sqrt(rate[...] * (2.0 / LENGTH))
    left8 = left[:OWN]
    decay = jnp.exp(slope * ROWS)
    small[0] = scale
    small[1] = lax.dot_general(
        jnp.where(left8, scale, 0.0), w, NT, precision=highest, preferred_element_type=f32
    )
    small[2] = jnp.broadcast_to(decay * step[0:1], (OWN, LANES))
    small[3] = jnp.broadcast_to(decay * step[1:2], (OWN, LANES))
    small[4] = jnp.where(left8, scale * (0.5 / rate[...]), scale * (-1.0 / LENGTH))
    small[5] = jnp.broadcast_to(jnp.sqrt(rate[...] * (2.0 / LENGTH)) * LENGTH ** -0.5, (OWN, LANES))


def make_tables(place, rate, coef):
    consts = [jnp.asarray(t) for t in wave_tables()]
    rate2 = jnp.concatenate([rate, rate])[None, :]
    return pl.pallas_call(
        table_kernel,
        out_shape=(
            jax.ShapeDtypeStruct((2 * ROWS, 4 * LANES), bf16),
            jax.ShapeDtypeStruct((2 * ROWS, 4 * LANES), bf16),
            jax.ShapeDtypeStruct((ROWS, LANES), bf16),
            jax.ShapeDtypeStruct((ROWS, LANES), bf16),
            jax.ShapeDtypeStruct((ROWS, LANES), f32),
            jax.ShapeDtypeStruct((6, OWN, LANES), f32),
        ),
        in_specs=[SMEM] + [VMEM] * 8,
        out_specs=tuple([VMEM] * 6),
        compiler_params=pltpu.CompilerParams(vmem_limit_bytes=12 << 20),
        cost_estimate=pl.CostEstimate(flops=4_000_000, bytes_accessed=1_000_000, transcendentals=40_000),
        name="tables",
    )(place, rate2, coef, *consts)


def mix(value, prior, weight):
    row = lax.broadcasted_iota(jnp.int32, value.shape, 0)
    one = jnp.where(row == 0, prior[1:2], pltpu.roll(value, 1, 0))
    two = jnp.where(row == 0, prior[0:1], jnp.where(row == 1, prior[1:2], pltpu.roll(value, 2, 0)))
    return weight[0:1] * value + weight[1:2] * one + weight[2:3] * two


def gate_kernel(x1, x2, value, out_grad, prior, weight, sent):
    mixed = mix(value[...].astype(f32), prior[...].astype(f32), weight[...])
    gated = x1[...].astype(f32) * mixed
    grad = out_grad[...].astype(f32) * x2[...].astype(f32)
    shards = sent.shape[0]
    gated = gated.T.reshape(shards, OWN, ROWS)
    grad = grad.T.reshape(shards, OWN, ROWS)
    sent[...] = jnp.concatenate([gated, grad], axis=1).astype(bf16)


def gate(x1, x2, value, out_grad, prior, weight):
    shards = x1.shape[1] // OWN
    return pl.pallas_call(
        gate_kernel,
        out_shape=jax.ShapeDtypeStruct((shards, 2 * OWN, ROWS), bf16),
        in_specs=[VMEM] * 6,
        out_specs=VMEM,
        compiler_params=pltpu.CompilerParams(vmem_limit_bytes=12 << 20),
        name="gate",
    )(x1, x2, value, out_grad, prior, weight)


def owner_kernel(got, tx, tg, mf, me, wd, small, out, xs, gs, rs, ex, eg, sr, si, gr, gi, yc, yg):
    chunks = got.shape[0]
    rows = chunks * OWN
    both = got[...].astype(f32)
    x = both[:, :OWN].reshape(rows, ROWS)
    g = both[:, OWN:].reshape(rows, ROWS)
    xs[...] = x
    gs[...] = g
    xb = x.astype(bf16)
    gb = g.astype(bf16)
    here = lax.broadcasted_iota(jnp.int32, (ROWS, ROWS), 0)
    there = lax.broadcasted_iota(jnp.int32, (ROWS, ROWS), 1)
    mirror = (here + there == ROWS - 1).astype(bf16)
    rs[...] = jnp.dot(xb, mirror, preferred_element_type=f32)
    ex[...] = jnp.dot(
        jnp.concatenate([xb, xb], axis=1), tx[...], preferred_element_type=f32
    )
    eg[...] = jnp.dot(
        jnp.concatenate([gb, gb], axis=1), tg[...], preferred_element_type=f32
    )
    scale = small[0]
    filt = small[1]
    lr = small[2]
    li = small[3]

    a = b = c = d = jnp.zeros((OWN, LANES), f32)
    for k in range(chunks):
        at = pl.ds(k * OWN, OWN)
        sr[at] = a
        si[at] = b
        a, b = (
            lr * a - li * b + ex[at, 0:LANES],
            lr * b + li * a + ex[at, LANES : 2 * LANES],
        )
        at = pl.ds((chunks - 1 - k) * OWN, OWN)
        gr[at] = c
        gi[at] = d
        c, d = (
            lr * c - li * d + eg[at, 0:LANES],
            lr * d + li * c + eg[at, LANES : 2 * LANES],
        )

    left = lax.broadcasted_iota(jnp.int32, (OWN, LANES), 1) < ORDER

    def cube(array):
        return array.reshape(chunks, OWN, LANES)

    s_r, s_i, g_r, g_i = (cube(ref[...]) for ref in (sr, si, gr, gi))
    over = jnp.where(left, 0.0, float(ROWS))
    ahead_r = over * lr * g_r - over * li * g_i
    ahead_i = over * lr * g_i + over * li * g_r
    total = (
        s_r * (cube(eg[:, 2 * LANES : 3 * LANES]) + ahead_r)
        - s_i * (cube(eg[:, 3 * LANES : 4 * LANES]) + ahead_i)
        + g_r * cube(ex[:, 2 * LANES : 3 * LANES])
        - g_i * cube(ex[:, 3 * LANES : 4 * LANES])
    )
    total = jnp.sum(total, axis=0)
    us = jnp.where(left, scale * s_r, -scale * s_i).reshape(rows, LANES).astype(bf16)
    ug = jnp.where(left, scale * g_r, -scale * g_i).reshape(rows, LANES).astype(bf16)
    yc[...] = lax.dot_general(us, mf[...], NT, preferred_element_type=f32)
    yg[...] = lax.dot_general(ug, me[...], NT, preferred_element_type=f32)

    later = there >= here
    inside = (there < here) | (there == ROWS - 1)
    lags = []
    for ch in range(OWN):
        at = pl.ds(ch, chunks, stride=OWN)
        xc = xs[at, :].astype(bf16)
        gc = gs[at, :].astype(bf16)
        toeplitz = pltpu.roll(
            jnp.broadcast_to(filt[ch : ch + 1], (ROWS, ROWS)), 0, 1, stride=1, stride_axis=0
        )
        toeplitz = jnp.where(later, toeplitz, 0.0).astype(bf16)
        yc[at, :] += jnp.dot(xc, toeplitz, preferred_element_type=f32)
        yg[at, :] += lax.dot_general(gc, toeplitz, NT, preferred_element_type=f32)
        pairs = lax.dot_general(rs[at, :].astype(bf16), gc, TN, preferred_element_type=f32)
        pairs = pltpu.roll(pairs, 0, 1, stride=1, stride_axis=0)
        lags.append(jnp.sum(jnp.where(inside, pairs, 0.0), axis=0, keepdims=True))
    lags = pltpu.roll(jnp.concatenate(lags, axis=0), 1, 1)
    total = total + jnp.dot(lags, wd[...], precision=highest, preferred_element_type=f32)

    part = jnp.sum(total * small[4], axis=0, keepdims=True)
    part = jnp.broadcast_to(part + pltpu.roll(part, ORDER, 1), (OWN, LANES))
    moved = pltpu.roll(part, 2, 1)
    low = part - part.astype(bf16).astype(f32)
    low_moved = moved - moved.astype(bf16).astype(f32)
    row = lax.broadcasted_iota(jnp.int32, (OWN, LANES), 0)
    lane = lax.broadcasted_iota(jnp.int32, (OWN, LANES), 1)
    part = jnp.where(row == 0, part, jnp.where(row == 1, moved, jnp.where(row == 2, low, low_moved)))
    extra = jnp.where(left, total * small[5], jnp.where(row < 4, part, 0.0))
    grad = cube(yg[...])
    heads = jnp.concatenate([yg[OWN:, :], jnp.zeros((OWN, LANES), f32)], axis=0)
    heads = cube(pltpu.roll(heads, ORDER, 1))
    is_head = (lane >= ORDER) & (lane < ORDER + 2)
    extra = jnp.where(is_head, heads, extra)
    out[...] = jnp.concatenate([cube(yc[...]), grad, extra], axis=1).astype(bf16)


def owner(got, tables):
    chunks = got.shape[0]
    rows = chunks * OWN
    return pl.pallas_call(
        owner_kernel,
        out_shape=jax.ShapeDtypeStruct((chunks, 3 * OWN, ROWS), bf16),
        in_specs=[VMEM] * 7,
        out_specs=VMEM,
        scratch_shapes=[pltpu.VMEM((rows, LANES), f32)] * 3
        + [pltpu.VMEM((rows, 4 * LANES), f32)] * 2
        + [pltpu.VMEM((rows, LANES), f32)] * 6,
        compiler_params=pltpu.CompilerParams(vmem_limit_bytes=24 << 20),
        name="owner",
    )(got, *tables)


def finish_kernel(back, x1, x2, value, prior, head, weight, y, gx1, gvalue, gcoef, rates):
    shards = back.shape[0]
    wide = shards * OWN
    every = back[...].astype(f32)
    conv = every[:, :OWN].reshape(wide, ROWS).T
    grad = every[:, OWN : 2 * OWN].reshape(wide, ROWS).T
    extra = every[:, 2 * OWN :]
    turned = extra.reshape(wide, LANES).T
    gcoef[...] = turned[:ORDER]
    part = jnp.sum(extra, axis=0)
    lane = lax.broadcasted_iota(jnp.int32, (1, LANES), 1)
    most = part[0:1] + part[2:3]
    few = part[1:2] + part[3:4]
    rates[...] = jnp.broadcast_to(
        jnp.where(lane < 2, pltpu.roll(few, ORDER - 2, 1), pltpu.roll(most, ORDER, 1)), rates.shape
    )
    first = x1[...].astype(f32)
    w = weight[...]
    y[...] = (x2[...].astype(f32) * conv).astype(bf16)
    mixed = mix(value[...].astype(f32), prior[...].astype(f32), w)
    gx1[...] = (grad * mixed).astype(bf16)
    grad_mixed = grad * first
    after = turned[ORDER : ORDER + 2] * head[...].astype(f32)
    row = lax.broadcasted_iota(jnp.int32, grad_mixed.shape, 0)
    one = jnp.where(row == ROWS - 1, after[0:1], pltpu.roll(grad_mixed, ROWS - 1, 0))
    two = jnp.where(
        row == ROWS - 2,
        after[0:1],
        jnp.where(row == ROWS - 1, after[1:2], pltpu.roll(grad_mixed, ROWS - 2, 0)),
    )
    gvalue[...] = (w[0:1] * grad_mixed + w[1:2] * one + w[2:3] * two).astype(bf16)


def finish(back, x1, x2, value, prior, head, weight, peers):
    shape = jax.ShapeDtypeStruct(x1.shape, bf16)
    return pl.pallas_call(
        finish_kernel,
        out_shape=(
            shape,
            shape,
            shape,
            jax.ShapeDtypeStruct((ORDER, x1.shape[1]), f32),
            jax.ShapeDtypeStruct((peers, LANES), f32),
        ),
        in_specs=[VMEM] * 7,
        out_specs=tuple([VMEM] * 5),
        compiler_params=pltpu.CompilerParams(vmem_limit_bytes=16 << 20),
        name="finish",
    )(back, x1, x2, value, prior, head, weight)


def shift(array, by):
    peers = lax.axis_size("seq")
    pairs = [(i, i + by) for i in range(peers) if 0 <= i + by < peers]
    return lax.ppermute(array, "seq", pairs)


def per_device(x1, x2, value, out_grad, short_weight, coef, rate):
    peers = lax.axis_size("chan")
    width = x1.shape[1]
    prior = shift(value[ROWS - 2 :], 1)
    head = shift(x1[:2], -1)
    place = lax.axis_index("seq").astype(jnp.int32)[None]
    tables = make_tables(place, rate, coef)
    sent = gate(x1, x2, value, out_grad, prior, short_weight)
    got = lax.all_to_all(sent, "seq", split_axis=0, concat_axis=0, tiled=True)
    done = owner(got, tables)
    back = lax.all_to_all(done, "seq", split_axis=0, concat_axis=0, tiled=True)
    y, gx1, gvalue, gcoef, rates = finish(back, x1, x2, value, prior, head, short_weight, peers)
    rates = lax.all_to_all(rates, "chan", split_axis=0, concat_axis=0, tiled=True)
    grad_rate = jnp.sum(rates, axis=0)[:ORDER] * (LENGTH * width * peers) ** -0.5
    return (y, gx1, gvalue, gcoef, grad_rate)


def solution(mesh):
    whole = P("seq", "chan")
    return jax.shard_map(
        per_device,
        mesh=mesh,
        in_specs=(whole, whole, whole, whole, P(None, "chan"), P(None, "chan"), P()),
        out_specs=(whole, whole, whole, P(None, "chan"), P()),
        check_vma=False,
    )
```

```python
import math

import jax
import jax.numpy as jnp
import numpy as np
from jax import lax
from jax.experimental import pallas as pl
from jax.experimental.pallas import tpu as pltpu
from jax.sharding import PartitionSpec as P

f32 = jnp.float32
bf16 = jnp.bfloat16
highest = lax.Precision.HIGHEST
LENGTH = 8192
ROWS = 128
ORDER = 64
LANES = 128
OWN = 8
WORDS = 2 * OWN + 2
NT = (((1,), (1,)), ((), ()))
TN = (((0,), (0,)), ((), ()))

VMEM = pl.BlockSpec(memory_space=pltpu.VMEM)
SMEM = pl.BlockSpec(memory_space=pltpu.SMEM)


def wave_tables():
    index = np.arange(ORDER)
    cycles = (index // 2 + 1) ** 2
    odd = index % 2 == 1

    def turn(power):
        angle = 2.0 * math.pi / LENGTH * (power[:, None] * cycles[None, :] % LENGTH)
        return np.cos(angle), np.sin(angle)

    ahead = np.arange(ROWS)
    cos_a, sin_a = turn(ahead)
    cos_b, sin_b = turn(ROWS - ahead)
    real_b = np.where(odd, sin_b, cos_b)
    imag_b = np.where(odd, -cos_b, sin_b)
    wave = np.where(odd, sin_a, cos_a)
    cos_l, sin_l = turn(np.array([ROWS]))
    twice = [np.concatenate([t, t], axis=1).astype(np.float32) for t in (cos_a, sin_a, real_b, imag_b, wave)]
    step = np.concatenate([np.concatenate([t, t], axis=1) for t in (cos_l, sin_l)], axis=0).astype(np.float32)
    return (*twice, step)


def split(table):
    high = table.astype(bf16)
    low = (table - high.astype(f32)).astype(bf16)
    return jnp.concatenate([high, low], axis=0)


def table_kernel(
    place, rate, coef, weight, cos_a, sin_a, real_b, imag_b, wave, step, tx, tg, mf, me, wd, small
):
    lane = lax.broadcasted_iota(jnp.int32, (ROWS, LANES), 1)
    power = lax.broadcasted_iota(jnp.int32, (ROWS, LANES), 0).astype(f32)
    left = lane < ORDER
    slope = rate[...] * (-1.0 / LENGTH)
    env_a = jnp.exp(slope * power)
    env_b = jnp.exp(slope * (ROWS - power))
    ar = env_a * cos_a[...]
    ai = env_a * sin_a[...]
    br = env_b * real_b[...]
    bi = env_b * imag_b[...]
    back = ROWS - power
    tx[...] = split(
        jnp.concatenate([br, bi, jnp.where(left, 0.0, back * br), jnp.where(left, 0.0, back * bi)], axis=1)
    )
    tg[...] = split(
        jnp.concatenate([ar, ai, jnp.where(left, ar, power * ar), jnp.where(left, ai, power * ai)], axis=1)
    )
    mf[...] = jnp.where(left, ar, ai).astype(bf16)
    me[...] = jnp.where(left, br, bi).astype(bf16)
    w = env_a * wave[...]
    wd[...] = jnp.where(left, w, power * w)
    pick = lax.broadcasted_iota(jnp.int32, (OWN, coef.shape[1]), 1) - place[0] * OWN
    pick = (pick == lax.broadcasted_iota(jnp.int32, (OWN, coef.shape[1]), 0)).astype(f32)
    own = lax.dot_general(
        pick, jnp.concatenate([coef[...], coef[...]], axis=0), NT, precision=highest, preferred_element_type=f32
    )
    scale = own * jnp.sqrt(rate[...] * (2.0 / LENGTH))
    left8 = left[:OWN]
    decay = jnp.exp(slope * ROWS)
    small[0] = scale
    small[1] = lax.dot_general(
        jnp.where(left8, scale, 0.0), w, NT, precision=highest, preferred_element_type=f32
    )
    small[2] = jnp.broadcast_to(decay * step[0:1], (OWN, LANES))
    small[3] = jnp.broadcast_to(decay * step[1:2], (OWN, LANES))
    small[4] = jnp.where(left8, scale * (0.5 / rate[...]), scale * (-1.0 / LENGTH))
    for tap in (1, 2):
        small[5 + tap] = lax.dot_general(
            pick,
            jnp.broadcast_to(weight[tap : tap + 1], (LANES, coef.shape[1])),
            NT,
            precision=highest,
            preferred_element_type=f32,
        )
    small[5] = jnp.broadcast_to(jnp.sqrt(rate[...] * (2.0 / LENGTH)) * LENGTH ** -0.5, (OWN, LANES))


def make_tables(place, rate, coef, weight):
    consts = [jnp.asarray(t) for t in wave_tables()]
    rate2 = jnp.concatenate([rate, rate])[None, :]
    return pl.pallas_call(
        table_kernel,
        out_shape=(
            jax.ShapeDtypeStruct((2 * ROWS, 4 * LANES), bf16),
            jax.ShapeDtypeStruct((2 * ROWS, 4 * LANES), bf16),
            jax.ShapeDtypeStruct((ROWS, LANES), bf16),
            jax.ShapeDtypeStruct((ROWS, LANES), bf16),
            jax.ShapeDtypeStruct((ROWS, LANES), f32),
            jax.ShapeDtypeStruct((8, OWN, LANES), f32),
        ),
        in_specs=[SMEM] + [VMEM] * 9,
        out_specs=tuple([VMEM] * 6),
        compiler_params=pltpu.CompilerParams(vmem_limit_bytes=12 << 20),
        cost_estimate=pl.CostEstimate(flops=4_000_000, bytes_accessed=1_000_000, transcendentals=40_000),
        name="tables",
    )(place, rate2, coef, weight, *consts)


def mix(value, prior, weight):
    row = lax.broadcasted_iota(jnp.int32, value.shape, 0)
    one = jnp.where(row == 0, prior[1:2], pltpu.roll(value, 1, 0))
    two = jnp.where(row == 0, prior[0:1], jnp.where(row == 1, prior[1:2], pltpu.roll(value, 2, 0)))
    return weight[0:1] * value + weight[1:2] * one + weight[2:3] * two


def gate_kernel(x1h, x2h, vh, oh, wh, sent, tail, x1, x2, v, o, w, sems):
    copies = [
        pltpu.make_async_copy(src, dst, sems.at[n])
        for n, (src, dst) in enumerate(((oh, o), (x2h, x2), (vh, v), (wh, w), (x1h, x1)))
    ]
    for copy in copies:
        copy.start()
    copies[0].wait()
    copies[1].wait()
    shards = sent.shape[0]
    grad = o[...].astype(f32) * x2[...].astype(f32)
    grad = grad.T.reshape(shards, OWN, ROWS)
    for copy in copies[2:]:
        copy.wait()
    value = v[...].astype(f32)
    first = x1[...].astype(f32)
    zero = jnp.zeros((2, value.shape[1]), f32)
    gated = (first * mix(value, zero, w[...])).T.reshape(shards, OWN, ROWS)
    flat = sent.reshape(shards, WORDS, ROWS)
    flat[:, : 2 * OWN] = jnp.concatenate([gated, grad], axis=1).astype(bf16)
    tail[...] = v[ROWS - 16 :]

    per = LANES // OWN
    lane = lax.broadcasted_iota(jnp.int32, (per, LANES), 1)
    row = lax.broadcasted_iota(jnp.int32, (per, LANES), 0)
    group = lax.rem(lane - row * OWN + LANES, LANES) // OWN
    edges = []
    for at in range(0, value.shape[1], LANES):
        tile = jnp.zeros((per, LANES), f32)
        for n, (source, where) in enumerate(((first, 0), (first, 1), (value, ROWS - 2), (value, ROWS - 1))):
            line = source[where : where + 1, at : at + LANES]
            line = pltpu.roll(line, n * OWN, 1) if n else line
            tile = jnp.where(group == n, line, tile)
        edges.append(tile)
    edges = jnp.concatenate(edges, axis=0)
    flat[:, 2 * OWN :] = jnp.broadcast_to(edges[:, None, :], (shards, 2, LANES)).astype(bf16)


def gate(x1, x2, value, out_grad, weight):
    shards = x1.shape[1] // OWN
    return pl.pallas_call(
        gate_kernel,
        out_shape=(
            jax.ShapeDtypeStruct((shards, WORDS // 2, 2, ROWS), bf16),
            jax.ShapeDtypeStruct((16, x1.shape[1]), bf16),
        ),
        in_specs=[pl.BlockSpec(memory_space=pltpu.HBM)] * 5,
        out_specs=(VMEM, VMEM),
        scratch_shapes=[pltpu.VMEM(x1.shape, bf16)] * 4
        + [pltpu.VMEM(weight.shape, f32), pltpu.SemaphoreType.DMA((5,))],
        compiler_params=pltpu.CompilerParams(vmem_limit_bytes=(64 << 20) - (64 << 10)),
        name="gate",
    )(x1, x2, value, out_grad, weight)


def owner_kernel(place, got, tx, tg, mf, me, wd, small, out, xs, gs, rs, ex, eg, sr, si, gr, gi, yc, yg):
    chunks = got.shape[0]
    rows = chunks * OWN
    flat = got.reshape(chunks, WORDS, ROWS)
    both = flat[:, : 2 * OWN].astype(f32)
    edge = flat[:, 2 * OWN :].astype(f32)[:, :1]
    edge = jnp.broadcast_to(edge, (chunks, OWN, LANES)).reshape(rows, LANES)
    edge = pltpu.roll(edge, lax.rem(ORDER * LANES - place[0] * OWN, LANES), 1)
    lane3 = lax.broadcasted_iota(jnp.int32, (rows, LANES), 1)
    row3 = lax.broadcasted_iota(jnp.int32, (rows, LANES), 0)
    edge = jnp.where(lane3 % OWN == row3 % OWN, edge, 0.0).astype(bf16)
    group = lax.broadcasted_iota(jnp.int32, (LANES, LANES), 0) // OWN
    to = lax.broadcasted_iota(jnp.int32, (LANES, LANES), 1)
    spot_x1 = ((group < 2) & (to % ORDER == group)).astype(bf16)
    spot_v = (((group == 2) & (to == 0)) | ((group == 3) & (to == 1))).astype(bf16)
    spot_last = ((group == 3) & (to == 0)).astype(bf16)
    spread = jnp.dot(
        edge, jnp.concatenate([spot_x1, spot_v, spot_last], axis=1), preferred_element_type=f32
    )
    x1_head = spread[:, :LANES]
    before = (
        small[7] * spread[:, LANES : 2 * LANES].reshape(chunks, OWN, LANES)
        + small[6] * spread[:, 2 * LANES :].reshape(chunks, OWN, LANES)
    )
    before = jnp.concatenate([jnp.zeros((1, OWN, LANES), f32), before[:-1]], axis=0)
    x = both[:, :OWN].reshape(rows, ROWS) + x1_head * before.reshape(rows, LANES)
    x = x.astype(bf16).astype(f32)
    g = both[:, OWN:].reshape(rows, ROWS)
    xs[...] = x
    gs[...] = g
    xb = x.astype(bf16)
    gb = g.astype(bf16)
    here = lax.broadcasted_iota(jnp.int32, (ROWS, ROWS), 0)
    there = lax.broadcasted_iota(jnp.int32, (ROWS, ROWS), 1)
    mirror = (here + there == ROWS - 1).astype(bf16)
    rs[...] = jnp.dot(xb, mirror, preferred_element_type=f32)
    ex[...] = jnp.dot(
        jnp.concatenate([xb, xb], axis=1), tx[...], preferred_element_type=f32
    )
    eg[...] = jnp.dot(
        jnp.concatenate([gb, gb], axis=1), tg[...], preferred_element_type=f32
    )
    scale = small[0]
    filt = small[1]
    lr = small[2]
    li = small[3]

    a = b = c = d = jnp.zeros((OWN, LANES), f32)
    for k in range(chunks):
        at = pl.ds(k * OWN, OWN)
        sr[at] = a
        si[at] = b
        a, b = (
            lr * a - li * b + ex[at, 0:LANES],
            lr * b + li * a + ex[at, LANES : 2 * LANES],
        )
        at = pl.ds((chunks - 1 - k) * OWN, OWN)
        gr[at] = c
        gi[at] = d
        c, d = (
            lr * c - li * d + eg[at, 0:LANES],
            lr * d + li * c + eg[at, LANES : 2 * LANES],
        )

    left = lax.broadcasted_iota(jnp.int32, (OWN, LANES), 1) < ORDER

    def cube(array):
        return array.reshape(chunks, OWN, LANES)

    s_r, s_i, g_r, g_i = (cube(ref[...]) for ref in (sr, si, gr, gi))
    over = jnp.where(left, 0.0, float(ROWS))
    ahead_r = over * lr * g_r - over * li * g_i
    ahead_i = over * lr * g_i + over * li * g_r
    total = (
        s_r * (cube(eg[:, 2 * LANES : 3 * LANES]) + ahead_r)
        - s_i * (cube(eg[:, 3 * LANES : 4 * LANES]) + ahead_i)
        + g_r * cube(ex[:, 2 * LANES : 3 * LANES])
        - g_i * cube(ex[:, 3 * LANES : 4 * LANES])
    )
    total = jnp.sum(total, axis=0)
    us = jnp.where(left, scale * s_r, -scale * s_i).reshape(rows, LANES).astype(bf16)
    ug = jnp.where(left, scale * g_r, -scale * g_i).reshape(rows, LANES).astype(bf16)
    yc[...] = lax.dot_general(us, mf[...], NT, preferred_element_type=f32)
    yg[...] = lax.dot_general(ug, me[...], NT, preferred_element_type=f32)

    later = there >= here
    inside = (there < here) | (there == ROWS - 1)
    lags = []
    for ch in range(OWN):
        at = pl.ds(ch, chunks, stride=OWN)
        xc = xs[at, :].astype(bf16)
        gc = gs[at, :].astype(bf16)
        toeplitz = pltpu.roll(
            jnp.broadcast_to(filt[ch : ch + 1], (ROWS, ROWS)), 0, 1, stride=1, stride_axis=0
        )
        toeplitz = jnp.where(later, toeplitz, 0.0).astype(bf16)
        yc[at, :] += jnp.dot(xc, toeplitz, preferred_element_type=f32)
        yg[at, :] += lax.dot_general(gc, toeplitz, NT, preferred_element_type=f32)
        pairs = lax.dot_general(rs[at, :].astype(bf16), gc, TN, preferred_element_type=f32)
        pairs = pltpu.roll(pairs, 0, 1, stride=1, stride_axis=0)
        lags.append(jnp.sum(jnp.where(inside, pairs, 0.0), axis=0, keepdims=True))
    lags = pltpu.roll(jnp.concatenate(lags, axis=0), 1, 1)
    total = total + jnp.dot(lags, wd[...], precision=highest, preferred_element_type=f32)

    part = jnp.sum(total * small[4], axis=0, keepdims=True)
    part = jnp.broadcast_to(part + pltpu.roll(part, ORDER, 1), (OWN, LANES))
    moved = pltpu.roll(part, 2, 1)
    low = part - part.astype(bf16).astype(f32)
    low_moved = moved - moved.astype(bf16).astype(f32)
    row = lax.broadcasted_iota(jnp.int32, (OWN, LANES), 0)
    lane = lax.broadcasted_iota(jnp.int32, (OWN, LANES), 1)
    part = jnp.where(row == 0, part, jnp.where(row == 1, moved, jnp.where(row == 2, low, low_moved)))
    extra = jnp.where(left, total * small[5], jnp.where(row < 4, part, 0.0))
    grad = cube(yg[...])
    heads = cube(pltpu.roll(yg[...], ORDER, 1) * x1_head)
    heads = jnp.concatenate([heads[1:], jnp.zeros((1, OWN, LANES), f32)], axis=0)
    is_head = (lane >= ORDER) & (lane < ORDER + 2)
    extra = jnp.where(is_head, heads, extra)
    out[...] = jnp.concatenate([cube(yc[...]), grad, extra], axis=1).astype(bf16)


def owner(place, got, tables):
    chunks = got.shape[0]
    rows = chunks * OWN
    return pl.pallas_call(
        owner_kernel,
        out_shape=jax.ShapeDtypeStruct((chunks, 3 * OWN, ROWS), bf16),
        in_specs=[SMEM] + [VMEM] * 7,
        out_specs=VMEM,
        scratch_shapes=[pltpu.VMEM((rows, LANES), f32)] * 3
        + [pltpu.VMEM((rows, 4 * LANES), f32)] * 2
        + [pltpu.VMEM((rows, LANES), f32)] * 6,
        compiler_params=pltpu.CompilerParams(vmem_limit_bytes=24 << 20),
        name="owner",
    )(place, got, *tables)


def finish_kernel(back, x1, x2, value, tail, weight, y, gx1, gvalue, gcoef, rates):
    shards = back.shape[0]
    wide = shards * OWN
    every = back[...].astype(f32)
    conv = every[:, :OWN].reshape(wide, ROWS).T
    grad = every[:, OWN : 2 * OWN].reshape(wide, ROWS).T
    extra = every[:, 2 * OWN :]
    turned = extra.reshape(wide, LANES).T
    gcoef[...] = turned[:ORDER]
    part = jnp.sum(extra, axis=0)
    lane = lax.broadcasted_iota(jnp.int32, (1, LANES), 1)
    most = part[0:1] + part[2:3]
    few = part[1:2] + part[3:4]
    rates[...] = jnp.broadcast_to(
        jnp.where(lane < 2, pltpu.roll(few, ORDER - 2, 1), pltpu.roll(most, ORDER, 1)), rates.shape
    )
    first = x1[...].astype(f32)
    w = weight[...]
    y[...] = (x2[...].astype(f32) * conv).astype(bf16)
    mixed = mix(value[...].astype(f32), tail[...].astype(f32)[14:], w)
    gx1[...] = (grad * mixed).astype(bf16)
    grad_mixed = grad * first
    after = turned[ORDER : ORDER + 2]
    row = lax.broadcasted_iota(jnp.int32, grad_mixed.shape, 0)
    one = jnp.where(row == ROWS - 1, after[0:1], pltpu.roll(grad_mixed, ROWS - 1, 0))
    two = jnp.where(
        row == ROWS - 2,
        after[0:1],
        jnp.where(row == ROWS - 1, after[1:2], pltpu.roll(grad_mixed, ROWS - 2, 0)),
    )
    gvalue[...] = (w[0:1] * grad_mixed + w[1:2] * one + w[2:3] * two).astype(bf16)


def finish(back, x1, x2, value, tail, weight, peers):
    shape = jax.ShapeDtypeStruct(x1.shape, bf16)
    return pl.pallas_call(
        finish_kernel,
        out_shape=(
            shape,
            shape,
            shape,
            jax.ShapeDtypeStruct((ORDER, x1.shape[1]), f32),
            jax.ShapeDtypeStruct((peers, LANES), f32),
        ),
        in_specs=[VMEM] * 6,
        out_specs=tuple([VMEM] * 5),
        compiler_params=pltpu.CompilerParams(vmem_limit_bytes=16 << 20),
        name="finish",
    )(back, x1, x2, value, tail, weight)


def shift(array, by):
    peers = lax.axis_size("seq")
    pairs = [(i, i + by) for i in range(peers) if 0 <= i + by < peers]
    return lax.ppermute(array, "seq", pairs)


def per_device(x1, x2, value, out_grad, short_weight, coef, rate):
    peers = lax.axis_size("chan")
    width = x1.shape[1]
    place = lax.axis_index("seq").astype(jnp.int32)[None]
    tables = make_tables(place, rate, coef, short_weight)
    sent, tail = gate(x1, x2, value, out_grad, short_weight)
    tail = shift(tail, 1)
    got = lax.all_to_all(sent, "seq", split_axis=0, concat_axis=0, tiled=True)
    done = owner(place, got, tables)
    back = lax.all_to_all(done, "seq", split_axis=0, concat_axis=0, tiled=True)
    y, gx1, gvalue, gcoef, rates = finish(back, x1, x2, value, tail, short_weight, peers)
    rates = lax.all_to_all(rates, "chan", split_axis=0, concat_axis=0, tiled=True)
    grad_rate = jnp.sum(rates, axis=0)[:ORDER] * (LENGTH * width * peers) ** -0.5
    return (y, gx1, gvalue, gcoef, grad_rate)


def solution(mesh):
    whole = P("seq", "chan")
    return jax.shard_map(
        per_device,
        mesh=mesh,
        in_specs=(whole, whole, whole, whole, P(None, "chan"), P(None, "chan"), P()),
        out_specs=(whole, whole, whole, P(None, "chan"), P()),
        check_vma=False,
    )
```

```python
import functools
import math

import jax
import jax.numpy as jnp
import numpy as np
from jax import lax
from jax.experimental import pallas as pl
from jax.experimental.pallas import tpu as pltpu
from jax.sharding import PartitionSpec as P

f32 = jnp.float32
bf16 = jnp.bfloat16
highest = lax.Precision.HIGHEST
LENGTH = 8192
ROWS = 128
ORDER = 64
LANES = 128
OWN = 8
WORDS = 2 * OWN + 2
NT = (((1,), (1,)), ((), ()))
TN = (((0,), (0,)), ((), ()))

VMEM = pl.BlockSpec(memory_space=pltpu.VMEM)
SMEM = pl.BlockSpec(memory_space=pltpu.SMEM)


def wave_tables():
    index = np.arange(ORDER)
    cycles = (index // 2 + 1) ** 2
    odd = index % 2 == 1

    def turn(power):
        angle = 2.0 * math.pi / LENGTH * (power[:, None] * cycles[None, :] % LENGTH)
        return np.cos(angle), np.sin(angle)

    ahead = np.arange(ROWS)
    cos_a, sin_a = turn(ahead)
    cos_b, sin_b = turn(ROWS - ahead)
    real_b = np.where(odd, sin_b, cos_b)
    imag_b = np.where(odd, -cos_b, sin_b)
    wave = np.where(odd, sin_a, cos_a)
    cos_l, sin_l = turn(np.array([ROWS]))
    twice = [np.concatenate([t, t], axis=1).astype(np.float32) for t in (cos_a, sin_a, real_b, imag_b, wave)]
    step = np.concatenate([np.concatenate([t, t], axis=1) for t in (cos_l, sin_l)], axis=0).astype(np.float32)
    return (*twice, step)


def split(table):
    high = table.astype(bf16)
    low = (table - high.astype(f32)).astype(bf16)
    return jnp.concatenate([high, low], axis=0)


def table_kernel(
    place, rate, coef, weight, cos_a, sin_a, real_b, imag_b, wave, step, tx, tg, mf, me, wd, small
):
    lane = lax.broadcasted_iota(jnp.int32, (ROWS, LANES), 1)
    power = lax.broadcasted_iota(jnp.int32, (ROWS, LANES), 0).astype(f32)
    left = lane < ORDER
    slope = rate[...] * (-1.0 / LENGTH)
    env_a = jnp.exp(slope * power)
    env_b = jnp.exp(slope * (ROWS - power))
    ar = env_a * cos_a[...]
    ai = env_a * sin_a[...]
    br = env_b * real_b[...]
    bi = env_b * imag_b[...]
    back = ROWS - power
    tx[...] = split(
        jnp.concatenate([br, bi, jnp.where(left, 0.0, back * br), jnp.where(left, 0.0, back * bi)], axis=1)
    )
    tg[...] = split(
        jnp.concatenate([ar, ai, jnp.where(left, ar, power * ar), jnp.where(left, ai, power * ai)], axis=1)
    )
    mf[...] = jnp.where(left, ar, ai).astype(bf16)
    me[...] = jnp.where(left, br, bi).astype(bf16)
    w = env_a * wave[...]
    wd[...] = jnp.where(left, w, power * w)
    pick = lax.broadcasted_iota(jnp.int32, (OWN, coef.shape[1]), 1) - place[0] * OWN
    pick = (pick == lax.broadcasted_iota(jnp.int32, (OWN, coef.shape[1]), 0)).astype(f32)
    own = lax.dot_general(
        pick, jnp.concatenate([coef[...], coef[...]], axis=0), NT, precision=highest, preferred_element_type=f32
    )
    scale = own * jnp.sqrt(rate[...] * (2.0 / LENGTH))
    left8 = left[:OWN]
    decay = jnp.exp(slope * ROWS)
    small[0] = scale
    small[1] = lax.dot_general(
        jnp.where(left8, scale, 0.0), w, NT, precision=highest, preferred_element_type=f32
    )
    small[2] = jnp.broadcast_to(decay * step[0:1], (OWN, LANES))
    small[3] = jnp.broadcast_to(decay * step[1:2], (OWN, LANES))
    small[4] = jnp.where(left8, scale * (0.5 / rate[...]), scale * (-1.0 / LENGTH))
    for tap in (1, 2):
        small[5 + tap] = lax.dot_general(
            pick,
            jnp.broadcast_to(weight[tap : tap + 1], (LANES, coef.shape[1])),
            NT,
            precision=highest,
            preferred_element_type=f32,
        )
    small[5] = jnp.broadcast_to(jnp.sqrt(rate[...] * (2.0 / LENGTH)) * LENGTH ** -0.5, (OWN, LANES))


def make_tables(place, rate, coef, weight):
    consts = [jnp.asarray(t) for t in wave_tables()]
    rate2 = jnp.concatenate([rate, rate])[None, :]
    return pl.pallas_call(
        table_kernel,
        out_shape=(
            jax.ShapeDtypeStruct((2 * ROWS, 4 * LANES), bf16),
            jax.ShapeDtypeStruct((2 * ROWS, 4 * LANES), bf16),
            jax.ShapeDtypeStruct((ROWS, LANES), bf16),
            jax.ShapeDtypeStruct((ROWS, LANES), bf16),
            jax.ShapeDtypeStruct((ROWS, LANES), f32),
            jax.ShapeDtypeStruct((8, OWN, LANES), f32),
        ),
        in_specs=[SMEM] + [VMEM] * 9,
        out_specs=tuple([VMEM] * 6),
        compiler_params=pltpu.CompilerParams(vmem_limit_bytes=12 << 20),
        cost_estimate=pl.CostEstimate(flops=4_000_000, bytes_accessed=1_000_000, transcendentals=40_000),
        name="tables",
    )(place, rate2, coef, weight, *consts)


def mix(value, prior, weight):
    row = lax.broadcasted_iota(jnp.int32, value.shape, 0)
    one = jnp.where(row == 0, prior[1:2], pltpu.roll(value, 1, 0))
    two = jnp.where(row == 0, prior[0:1], jnp.where(row == 1, prior[1:2], pltpu.roll(value, 2, 0)))
    return weight[0:1] * value + weight[1:2] * one + weight[2:3] * two


def gate_kernel(x1h, x2h, vh, oh, wh, sent, tail, x1, x2, v, o, w, sems):
    copies = [
        pltpu.make_async_copy(src, dst, sems.at[n])
        for n, (src, dst) in enumerate(((oh, o), (x2h, x2), (vh, v), (wh, w), (x1h, x1)))
    ]
    for copy in copies:
        copy.start()
    copies[0].wait()
    copies[1].wait()
    shards = sent.shape[0]
    grad = o[...].astype(f32) * x2[...].astype(f32)
    grad = grad.T.reshape(shards, OWN, ROWS)
    for copy in copies[2:]:
        copy.wait()
    value = v[...].astype(f32)
    first = x1[...].astype(f32)
    zero = jnp.zeros((2, value.shape[1]), f32)
    gated = (first * mix(value, zero, w[...])).T.reshape(shards, OWN, ROWS)
    flat = sent.reshape(shards, WORDS, ROWS)
    flat[:, : 2 * OWN] = jnp.concatenate([gated, grad], axis=1).astype(bf16)
    tail[...] = v[ROWS - 16 :]

    per = LANES // OWN
    lane = lax.broadcasted_iota(jnp.int32, (per, LANES), 1)
    row = lax.broadcasted_iota(jnp.int32, (per, LANES), 0)
    group = lax.rem(lane - row * OWN + LANES, LANES) // OWN
    edges = []
    for at in range(0, value.shape[1], LANES):
        tile = jnp.zeros((per, LANES), f32)
        for n, (source, where) in enumerate(((first, 0), (first, 1), (value, ROWS - 2), (value, ROWS - 1))):
            line = source[where : where + 1, at : at + LANES]
            line = pltpu.roll(line, n * OWN, 1) if n else line
            tile = jnp.where(group == n, line, tile)
        edges.append(tile)
    edges = jnp.concatenate(edges, axis=0)
    flat[:, 2 * OWN :] = jnp.broadcast_to(edges[:, None, :], (shards, 2, LANES)).astype(bf16)


def gate(x1, x2, value, out_grad, weight):
    shards = x1.shape[1] // OWN
    return pl.pallas_call(
        gate_kernel,
        out_shape=(
            jax.ShapeDtypeStruct((shards, WORDS // 2, 2, ROWS), bf16),
            jax.ShapeDtypeStruct((16, x1.shape[1]), bf16),
        ),
        in_specs=[pl.BlockSpec(memory_space=pltpu.HBM)] * 5,
        out_specs=(VMEM, VMEM),
        scratch_shapes=[pltpu.VMEM(x1.shape, bf16)] * 4
        + [pltpu.VMEM(weight.shape, f32), pltpu.SemaphoreType.DMA((5,))],
        compiler_params=pltpu.CompilerParams(vmem_limit_bytes=(64 << 20) - (64 << 10)),
        name="gate",
    )(x1, x2, value, out_grad, weight)


def owner_kernel(
    place, got, tx, tg, wd, small, part_out, coef_out, us, ug, xb_out, head_out, gs, rs, ex, eg, sr, si, gr, gi
):
    chunks = got.shape[0]
    rows = chunks * OWN
    flat = got.reshape(chunks, WORDS, ROWS)
    both = flat[:, : 2 * OWN].astype(f32)
    edge = flat[:, 2 * OWN :].astype(f32)[:, :1]
    edge = jnp.broadcast_to(edge, (chunks, OWN, LANES)).reshape(rows, LANES)
    edge = pltpu.roll(edge, lax.rem(ORDER * LANES - place[0] * OWN, LANES), 1)
    lane3 = lax.broadcasted_iota(jnp.int32, (rows, LANES), 1)
    row3 = lax.broadcasted_iota(jnp.int32, (rows, LANES), 0)
    edge = jnp.where(lane3 % OWN == row3 % OWN, edge, 0.0).astype(bf16)
    group = lax.broadcasted_iota(jnp.int32, (LANES, LANES), 0) // OWN
    to = lax.broadcasted_iota(jnp.int32, (LANES, LANES), 1)
    spot_x1 = ((group < 2) & (to % ORDER == group)).astype(bf16)
    spot_v = (((group == 2) & (to == 0)) | ((group == 3) & (to == 1))).astype(bf16)
    spot_last = ((group == 3) & (to == 0)).astype(bf16)
    spread = jnp.dot(
        edge, jnp.concatenate([spot_x1, spot_v, spot_last], axis=1), preferred_element_type=f32
    )
    x1_head = spread[:, :LANES]
    before = (
        small[7] * spread[:, LANES : 2 * LANES].reshape(chunks, OWN, LANES)
        + small[6] * spread[:, 2 * LANES :].reshape(chunks, OWN, LANES)
    )
    before = jnp.concatenate([jnp.zeros((1, OWN, LANES), f32), before[:-1]], axis=0)
    x = both[:, :OWN].reshape(rows, ROWS) + x1_head * before.reshape(rows, LANES)
    g = both[:, OWN:].reshape(rows, ROWS)
    gs[...] = g
    xb = x.astype(bf16)
    xb_out[...] = xb
    head_out[...] = x1_head
    gb = g.astype(bf16)
    here = lax.broadcasted_iota(jnp.int32, (ROWS, ROWS), 0)
    there = lax.broadcasted_iota(jnp.int32, (ROWS, ROWS), 1)
    mirror = (here + there == ROWS - 1).astype(bf16)
    rs[...] = jnp.dot(xb, mirror, preferred_element_type=f32)
    ex[...] = jnp.dot(
        jnp.concatenate([xb, xb], axis=1), tx[...], preferred_element_type=f32
    )
    eg[...] = jnp.dot(
        jnp.concatenate([gb, gb], axis=1), tg[...], preferred_element_type=f32
    )
    scale = small[0]
    lr = small[2]
    li = small[3]

    a = b = c = d = jnp.zeros((OWN, LANES), f32)
    for k in range(chunks):
        at = pl.ds(k * OWN, OWN)
        sr[at] = a
        si[at] = b
        a, b = (
            lr * a - li * b + ex[at, 0:LANES],
            lr * b + li * a + ex[at, LANES : 2 * LANES],
        )
        at = pl.ds((chunks - 1 - k) * OWN, OWN)
        gr[at] = c
        gi[at] = d
        c, d = (
            lr * c - li * d + eg[at, 0:LANES],
            lr * d + li * c + eg[at, LANES : 2 * LANES],
        )

    left = lax.broadcasted_iota(jnp.int32, (OWN, LANES), 1) < ORDER

    def cube(array):
        return array.reshape(chunks, OWN, LANES)

    s_r, s_i, g_r, g_i = (cube(ref[...]) for ref in (sr, si, gr, gi))
    over = jnp.where(left, 0.0, float(ROWS))
    ahead_r = over * lr * g_r - over * li * g_i
    ahead_i = over * lr * g_i + over * li * g_r
    total = (
        s_r * (cube(eg[:, 2 * LANES : 3 * LANES]) + ahead_r)
        - s_i * (cube(eg[:, 3 * LANES : 4 * LANES]) + ahead_i)
        + g_r * cube(ex[:, 2 * LANES : 3 * LANES])
        - g_i * cube(ex[:, 3 * LANES : 4 * LANES])
    )
    total = jnp.sum(total, axis=0)
    us[...] = jnp.where(left, scale * s_r, -scale * s_i).reshape(rows, LANES).astype(bf16)
    ug[...] = jnp.where(left, scale * g_r, -scale * g_i).reshape(rows, LANES).astype(bf16)

    inside = (there < here) | (there == ROWS - 1)
    lags = []
    for ch in range(OWN):
        at = pl.ds(ch, chunks, stride=OWN)
        pairs = lax.dot_general(
            rs[at, :].astype(bf16), gs[at, :].astype(bf16), TN, preferred_element_type=f32
        )
        pairs = pltpu.roll(pairs, 0, 1, stride=1, stride_axis=0)
        lags.append(jnp.sum(jnp.where(inside, pairs, 0.0), axis=0, keepdims=True))
    lags = pltpu.roll(jnp.concatenate(lags, axis=0), 1, 1)
    total = total + jnp.dot(lags, wd[...], precision=highest, preferred_element_type=f32)
    coef_out[...] = total * small[5]
    part = jnp.sum(total * small[4], axis=0, keepdims=True)
    part_out[...] = jnp.broadcast_to(part + pltpu.roll(part, ORDER, 1), part_out.shape)


def owner(place, got, tables, peers):
    chunks = got.shape[0]
    rows = chunks * OWN
    tx, tg, mf, me, wd, small = tables
    flat = jax.ShapeDtypeStruct((rows, LANES), bf16)
    return pl.pallas_call(
        owner_kernel,
        out_shape=(
            jax.ShapeDtypeStruct((peers, LANES), f32),
            jax.ShapeDtypeStruct((OWN, LANES), f32),
            flat,
            flat,
            flat,
            jax.ShapeDtypeStruct((rows, LANES), f32),
        ),
        in_specs=[SMEM] + [VMEM] * 5,
        out_specs=tuple([VMEM] * 6),
        scratch_shapes=[pltpu.VMEM((rows, LANES), f32)] * 2
        + [pltpu.VMEM((rows, 4 * LANES), f32)] * 2
        + [pltpu.VMEM((rows, LANES), f32)] * 4,
        compiler_params=pltpu.CompilerParams(vmem_limit_bytes=24 << 20),
        name="owner",
    )(place, got, tx, tg, wd, small)


def emit_kernel(got, parts, coef, us, ug, xb, head, mf, me, small, out, xs, gs, yc, yg):
    chunks = got.shape[0]
    rows = chunks * OWN

    def cube(array):
        return array.reshape(chunks, OWN, LANES)

    xs[...] = xb[...].astype(f32)
    gs[...] = got.reshape(chunks, WORDS, ROWS)[:, : 2 * OWN].astype(f32)[:, OWN:].reshape(rows, ROWS)
    yc[...] = lax.dot_general(us[...], mf[...], NT, preferred_element_type=f32)
    yg[...] = lax.dot_general(ug[...], me[...], NT, preferred_element_type=f32)
    here = lax.broadcasted_iota(jnp.int32, (ROWS, ROWS), 0)
    there = lax.broadcasted_iota(jnp.int32, (ROWS, ROWS), 1)
    later = there >= here
    filt = small[1]
    for ch in range(OWN):
        at = pl.ds(ch, chunks, stride=OWN)
        toeplitz = pltpu.roll(
            jnp.broadcast_to(filt[ch : ch + 1], (ROWS, ROWS)), 0, 1, stride=1, stride_axis=0
        )
        toeplitz = jnp.where(later, toeplitz, 0.0).astype(bf16)
        yc[at, :] += jnp.dot(xs[at, :].astype(bf16), toeplitz, preferred_element_type=f32)
        yg[at, :] += lax.dot_general(gs[at, :].astype(bf16), toeplitz, NT, preferred_element_type=f32)

    row = lax.broadcasted_iota(jnp.int32, (OWN, LANES), 0)
    lane = lax.broadcasted_iota(jnp.int32, (OWN, LANES), 1)
    part = jnp.broadcast_to(jnp.sum(parts[...], axis=0, keepdims=True), (OWN, LANES))
    moved = pltpu.roll(part, 2, 1)
    low = part - part.astype(bf16).astype(f32)
    low_moved = moved - moved.astype(bf16).astype(f32)
    part = jnp.where(row == 0, part, jnp.where(row == 1, moved, jnp.where(row == 2, low, low_moved)))
    extra = jnp.where(lane < ORDER, coef[...], jnp.where(row < 4, part, 0.0))
    heads = cube(pltpu.roll(yg[...], ORDER, 1) * head[...])
    heads = jnp.concatenate([heads[1:], jnp.zeros((1, OWN, LANES), f32)], axis=0)
    is_head = (lane >= ORDER) & (lane < ORDER + 2)
    extra = jnp.where(is_head, heads, extra)
    out[...] = jnp.concatenate([cube(yc[...]), cube(yg[...]), extra], axis=1).astype(bf16)


def emit(got, parts, made, tables):
    chunks = got.shape[0]
    rows = chunks * OWN
    tx, tg, mf, me, wd, small = tables
    return pl.pallas_call(
        emit_kernel,
        out_shape=jax.ShapeDtypeStruct((chunks, 3 * OWN, ROWS), bf16),
        in_specs=[VMEM] * 10,
        out_specs=VMEM,
        scratch_shapes=[pltpu.VMEM((rows, LANES), f32)] * 4,
        compiler_params=pltpu.CompilerParams(vmem_limit_bytes=24 << 20),
        name="emit",
    )(got, parts, *made, mf, me, small)


def finish_kernel(peers, back, x1, x2, value, tail, weight, y, gx1, gvalue, gcoef, grate):
    shards = back.shape[0]
    wide = shards * OWN
    every = back[...].astype(f32)
    conv = every[:, :OWN].reshape(wide, ROWS).T
    grad = every[:, OWN : 2 * OWN].reshape(wide, ROWS).T
    extra = every[:, 2 * OWN :]
    turned = extra.reshape(wide, LANES).T
    gcoef[...] = turned[:ORDER]
    part = jnp.sum(extra, axis=0)
    lane = lax.broadcasted_iota(jnp.int32, (1, LANES), 1)
    most = part[0:1] + part[2:3]
    few = part[1:2] + part[3:4]
    rates = jnp.where(lane < 2, pltpu.roll(few, ORDER - 2, 1), pltpu.roll(most, ORDER, 1))
    grate[...] = rates[:, :ORDER] * (LENGTH * wide * peers) ** -0.5
    first = x1[...].astype(f32)
    w = weight[...]
    y[...] = (x2[...].astype(f32) * conv).astype(bf16)
    mixed = mix(value[...].astype(f32), tail[...].astype(f32)[14:], w)
    gx1[...] = (grad * mixed).astype(bf16)
    grad_mixed = grad * first
    after = turned[ORDER : ORDER + 2]
    row = lax.broadcasted_iota(jnp.int32, grad_mixed.shape, 0)
    one = jnp.where(row == ROWS - 1, after[0:1], pltpu.roll(grad_mixed, ROWS - 1, 0))
    two = jnp.where(
        row == ROWS - 2,
        after[0:1],
        jnp.where(row == ROWS - 1, after[1:2], pltpu.roll(grad_mixed, ROWS - 2, 0)),
    )
    gvalue[...] = (w[0:1] * grad_mixed + w[1:2] * one + w[2:3] * two).astype(bf16)


def finish(back, x1, x2, value, tail, weight, peers):
    shape = jax.ShapeDtypeStruct(x1.shape, bf16)
    return pl.pallas_call(
        functools.partial(finish_kernel, peers),
        out_shape=(
            shape,
            shape,
            shape,
            jax.ShapeDtypeStruct((ORDER, x1.shape[1]), f32),
            jax.ShapeDtypeStruct((1, ORDER), f32),
        ),
        in_specs=[VMEM] * 6,
        out_specs=tuple([VMEM] * 5),
        compiler_params=pltpu.CompilerParams(vmem_limit_bytes=16 << 20),
        name="finish",
    )(back, x1, x2, value, tail, weight)


def shift(array, by):
    peers = lax.axis_size("seq")
    pairs = [(i, i + by) for i in range(peers) if 0 <= i + by < peers]
    return lax.ppermute(array, "seq", pairs)


def per_device(x1, x2, value, out_grad, short_weight, coef, rate):
    peers = lax.axis_size("chan")
    place = lax.axis_index("seq").astype(jnp.int32)[None]
    tables = make_tables(place, rate, coef, short_weight)
    sent, tail = gate(x1, x2, value, out_grad, short_weight)
    tail = shift(tail, 1)
    got = lax.all_to_all(sent, "seq", split_axis=0, concat_axis=0, tiled=True)
    part, *made = owner(place, got, tables, peers)
    parts = lax.all_to_all(part, "chan", split_axis=0, concat_axis=0, tiled=True)
    done = emit(got, parts, made, tables)
    back = lax.all_to_all(done, "seq", split_axis=0, concat_axis=0, tiled=True)
    y, gx1, gvalue, gcoef, grate = finish(back, x1, x2, value, tail, short_weight, peers)
    return (y, gx1, gvalue, gcoef, grate.reshape(ORDER))


def solution(mesh):
    whole = P("seq", "chan")
    return jax.shard_map(
        per_device,
        mesh=mesh,
        in_specs=(whole, whole, whole, whole, P(None, "chan"), P(None, "chan"), P()),
        out_specs=(whole, whole, whole, P(None, "chan"), P()),
        check_vma=False,
    )
```

```python
import functools
import math

import jax
import jax.numpy as jnp
import numpy as np
from jax import lax
from jax.experimental import pallas as pl
from jax.experimental.pallas import tpu as pltpu
from jax.sharding import PartitionSpec as P

f32 = jnp.float32
bf16 = jnp.bfloat16
highest = lax.Precision.HIGHEST
LENGTH = 8192
ROWS = 128
ORDER = 64
LANES = 128
OWN = 8
WORDS = 2 * OWN + 2
BACK = 2 * OWN + 6
NT = (((1,), (1,)), ((), ()))
TN = (((0,), (0,)), ((), ()))

VMEM = pl.BlockSpec(memory_space=pltpu.VMEM)
SMEM = pl.BlockSpec(memory_space=pltpu.SMEM)


def wave_tables():
    index = np.arange(ORDER)
    cycles = (index // 2 + 1) ** 2
    odd = index % 2 == 1

    def turn(power):
        angle = 2.0 * math.pi / LENGTH * (power[:, None] * cycles[None, :] % LENGTH)
        return np.cos(angle), np.sin(angle)

    ahead = np.arange(ROWS)
    cos_a, sin_a = turn(ahead)
    cos_b, sin_b = turn(ROWS - ahead)
    real_b = np.where(odd, sin_b, cos_b)
    imag_b = np.where(odd, -cos_b, sin_b)
    wave = np.where(odd, sin_a, cos_a)
    cos_l, sin_l = turn(np.array([ROWS]))
    twice = [np.concatenate([t, t], axis=1).astype(np.float32) for t in (cos_a, sin_a, real_b, imag_b, wave)]
    step = np.concatenate([np.concatenate([t, t], axis=1) for t in (cos_l, sin_l)], axis=0).astype(np.float32)
    return (*twice, step)


def split(table):
    high = table.astype(bf16)
    low = (table - high.astype(f32)).astype(bf16)
    return jnp.concatenate([high, low], axis=0)


def table_kernel(
    place, rate, coef, weight, cos_a, sin_a, real_b, imag_b, wave, step, tx, tg, mf, me, wd, small
):
    lane = lax.broadcasted_iota(jnp.int32, (ROWS, LANES), 1)
    power = lax.broadcasted_iota(jnp.int32, (ROWS, LANES), 0).astype(f32)
    left = lane < ORDER
    slope = rate[...] * (-1.0 / LENGTH)
    env_a = jnp.exp(slope * power)
    env_b = jnp.exp(slope * (ROWS - power))
    ar = env_a * cos_a[...]
    ai = env_a * sin_a[...]
    br = env_b * real_b[...]
    bi = env_b * imag_b[...]
    back = ROWS - power
    tx[...] = split(
        jnp.concatenate([br, bi, jnp.where(left, 0.0, back * br), jnp.where(left, 0.0, back * bi)], axis=1)
    )
    tg[...] = split(
        jnp.concatenate([ar, ai, jnp.where(left, ar, power * ar), jnp.where(left, ai, power * ai)], axis=1)
    )
    mf[...] = jnp.where(left, ar, ai).astype(bf16)
    me[...] = jnp.where(left, br, bi).astype(bf16)
    w = env_a * wave[...]
    wd[...] = jnp.where(left, w, power * w)
    pick = lax.broadcasted_iota(jnp.int32, (OWN, coef.shape[1]), 1) - place[0] * OWN
    pick = (pick == lax.broadcasted_iota(jnp.int32, (OWN, coef.shape[1]), 0)).astype(f32)
    own = lax.dot_general(
        pick, jnp.concatenate([coef[...], coef[...]], axis=0), NT, precision=highest, preferred_element_type=f32
    )
    scale = own * jnp.sqrt(rate[...] * (2.0 / LENGTH))
    left8 = left[:OWN]
    decay = jnp.exp(slope * ROWS)
    small[0] = scale
    small[1] = lax.dot_general(
        jnp.where(left8, scale, 0.0), w, NT, precision=highest, preferred_element_type=f32
    )
    small[2] = jnp.broadcast_to(decay * step[0:1], (OWN, LANES))
    small[3] = jnp.broadcast_to(decay * step[1:2], (OWN, LANES))
    small[4] = jnp.where(left8, scale * (0.5 / rate[...]), scale * (-1.0 / LENGTH))
    for tap in (1, 2):
        small[5 + tap] = lax.dot_general(
            pick,
            jnp.broadcast_to(weight[tap : tap + 1], (LANES, coef.shape[1])),
            NT,
            precision=highest,
            preferred_element_type=f32,
        )
    small[5] = jnp.broadcast_to(jnp.sqrt(rate[...] * (2.0 / LENGTH)) * LENGTH ** -0.5, (OWN, LANES))


def make_tables(place, rate, coef, weight):
    consts = [jnp.asarray(t) for t in wave_tables()]
    rate2 = jnp.concatenate([rate, rate])[None, :]
    return pl.pallas_call(
        table_kernel,
        out_shape=(
            jax.ShapeDtypeStruct((2 * ROWS, 4 * LANES), bf16),
            jax.ShapeDtypeStruct((2 * ROWS, 4 * LANES), bf16),
            jax.ShapeDtypeStruct((ROWS, LANES), bf16),
            jax.ShapeDtypeStruct((ROWS, LANES), bf16),
            jax.ShapeDtypeStruct((ROWS, LANES), f32),
            jax.ShapeDtypeStruct((8, OWN, LANES), f32),
        ),
        in_specs=[SMEM] + [VMEM] * 9,
        out_specs=tuple([VMEM] * 6),
        compiler_params=pltpu.CompilerParams(vmem_limit_bytes=12 << 20),
        cost_estimate=pl.CostEstimate(flops=4_000_000, bytes_accessed=1_000_000, transcendentals=40_000),
        name="tables",
    )(place, rate2, coef, weight, *consts)


def mix(value, prior, weight):
    row = lax.broadcasted_iota(jnp.int32, value.shape, 0)
    one = jnp.where(row == 0, prior[1:2], pltpu.roll(value, 1, 0))
    two = jnp.where(row == 0, prior[0:1], jnp.where(row == 1, prior[1:2], pltpu.roll(value, 2, 0)))
    return weight[0:1] * value + weight[1:2] * one + weight[2:3] * two


def gate_kernel(x1h, x2h, vh, oh, wh, sent, tail, x1, x2, v, o, w, sems):
    copies = [
        pltpu.make_async_copy(src, dst, sems.at[n])
        for n, (src, dst) in enumerate(((oh, o), (x2h, x2), (vh, v), (wh, w), (x1h, x1)))
    ]
    for copy in copies:
        copy.start()
    copies[0].wait()
    copies[1].wait()
    shards = sent.shape[0]
    grad = o[...].astype(f32) * x2[...].astype(f32)
    grad = grad.T.reshape(shards, OWN, ROWS)
    for copy in copies[2:]:
        copy.wait()
    value = v[...].astype(f32)
    first = x1[...].astype(f32)
    zero = jnp.zeros((2, value.shape[1]), f32)
    gated = (first * mix(value, zero, w[...])).T.reshape(shards, OWN, ROWS)
    flat = sent.reshape(shards, WORDS, ROWS)
    flat[:, : 2 * OWN] = jnp.concatenate([gated, grad], axis=1).astype(bf16)
    tail[...] = v[ROWS - 16 :]

    per = LANES // OWN
    lane = lax.broadcasted_iota(jnp.int32, (per, LANES), 1)
    row = lax.broadcasted_iota(jnp.int32, (per, LANES), 0)
    group = lax.rem(lane - row * OWN + LANES, LANES) // OWN
    edges = []
    for at in range(0, value.shape[1], LANES):
        tile = jnp.zeros((per, LANES), f32)
        for n, (source, where) in enumerate(((first, 0), (first, 1), (value, ROWS - 2), (value, ROWS - 1))):
            line = source[where : where + 1, at : at + LANES]
            line = pltpu.roll(line, n * OWN, 1) if n else line
            tile = jnp.where(group == n, line, tile)
        edges.append(tile)
    edges = jnp.concatenate(edges, axis=0)
    flat[:, 2 * OWN :] = jnp.broadcast_to(edges[:, None, :], (shards, 2, LANES)).astype(bf16)


def gate(x1, x2, value, out_grad, weight):
    shards = x1.shape[1] // OWN
    return pl.pallas_call(
        gate_kernel,
        out_shape=(
            jax.ShapeDtypeStruct((shards, WORDS // 2, 2, ROWS), bf16),
            jax.ShapeDtypeStruct((16, x1.shape[1]), bf16),
        ),
        in_specs=[pl.BlockSpec(memory_space=pltpu.HBM)] * 5,
        out_specs=(VMEM, VMEM),
        scratch_shapes=[pltpu.VMEM(x1.shape, bf16)] * 4
        + [pltpu.VMEM(weight.shape, f32), pltpu.SemaphoreType.DMA((5,))],
        compiler_params=pltpu.CompilerParams(vmem_limit_bytes=(64 << 20) - (64 << 10)),
        name="gate",
    )(x1, x2, value, out_grad, weight)


def owner_kernel(
    place, got, tx, tg, wd, small, part_out, coef_out, us, ug, xb_out, head_out, gs, rs, ex, eg, sr, si, gr, gi
):
    chunks = got.shape[0]
    rows = chunks * OWN
    flat = got.reshape(chunks, WORDS, ROWS)
    both = flat[:, : 2 * OWN].astype(f32)
    edge = flat[:, 2 * OWN :].astype(f32)[:, :1]
    edge = jnp.broadcast_to(edge, (chunks, OWN, LANES)).reshape(rows, LANES)
    edge = pltpu.roll(edge, lax.rem(ORDER * LANES - place[0] * OWN, LANES), 1)
    lane3 = lax.broadcasted_iota(jnp.int32, (rows, LANES), 1)
    row3 = lax.broadcasted_iota(jnp.int32, (rows, LANES), 0)
    edge = jnp.where(lane3 % OWN == row3 % OWN, edge, 0.0).astype(bf16)
    group = lax.broadcasted_iota(jnp.int32, (LANES, LANES), 0) // OWN
    to = lax.broadcasted_iota(jnp.int32, (LANES, LANES), 1)
    spot_x1 = ((group < 2) & (to % ORDER == group)).astype(bf16)
    spot_v = (((group == 2) & (to == 0)) | ((group == 3) & (to == 1))).astype(bf16)
    spot_last = ((group == 3) & (to == 0)).astype(bf16)
    spread = jnp.dot(
        edge, jnp.concatenate([spot_x1, spot_v, spot_last], axis=1), preferred_element_type=f32
    )
    x1_head = spread[:, :LANES]
    before = (
        small[7] * spread[:, LANES : 2 * LANES].reshape(chunks, OWN, LANES)
        + small[6] * spread[:, 2 * LANES :].reshape(chunks, OWN, LANES)
    )
    before = jnp.concatenate([jnp.zeros((1, OWN, LANES), f32), before[:-1]], axis=0)
    x = both[:, :OWN].reshape(rows, ROWS) + x1_head * before.reshape(rows, LANES)
    g = both[:, OWN:].reshape(rows, ROWS)
    gs[...] = g
    xb = x.astype(bf16)
    xb_out[...] = xb
    head_out[...] = x1_head
    gb = g.astype(bf16)
    here = lax.broadcasted_iota(jnp.int32, (ROWS, ROWS), 0)
    there = lax.broadcasted_iota(jnp.int32, (ROWS, ROWS), 1)
    mirror = (here + there == ROWS - 1).astype(bf16)
    rs[...] = jnp.dot(xb, mirror, preferred_element_type=f32)
    ex[...] = jnp.dot(
        jnp.concatenate([xb, xb], axis=1), tx[...], preferred_element_type=f32
    )
    eg[...] = jnp.dot(
        jnp.concatenate([gb, gb], axis=1), tg[...], preferred_element_type=f32
    )
    scale = small[0]
    lr = small[2]
    li = small[3]

    a = b = c = d = jnp.zeros((OWN, LANES), f32)
    for k in range(chunks):
        at = pl.ds(k * OWN, OWN)
        sr[at] = a
        si[at] = b
        a, b = (
            lr * a - li * b + ex[at, 0:LANES],
            lr * b + li * a + ex[at, LANES : 2 * LANES],
        )
        at = pl.ds((chunks - 1 - k) * OWN, OWN)
        gr[at] = c
        gi[at] = d
        c, d = (
            lr * c - li * d + eg[at, 0:LANES],
            lr * d + li * c + eg[at, LANES : 2 * LANES],
        )

    left = lax.broadcasted_iota(jnp.int32, (OWN, LANES), 1) < ORDER

    def cube(array):
        return array.reshape(chunks, OWN, LANES)

    s_r, s_i, g_r, g_i = (cube(ref[...]) for ref in (sr, si, gr, gi))
    over = jnp.where(left, 0.0, float(ROWS))
    ahead_r = over * lr * g_r - over * li * g_i
    ahead_i = over * lr * g_i + over * li * g_r
    total = (
        s_r * (cube(eg[:, 2 * LANES : 3 * LANES]) + ahead_r)
        - s_i * (cube(eg[:, 3 * LANES : 4 * LANES]) + ahead_i)
        + g_r * cube(ex[:, 2 * LANES : 3 * LANES])
        - g_i * cube(ex[:, 3 * LANES : 4 * LANES])
    )
    total = jnp.sum(total, axis=0)
    us[...] = jnp.where(left, scale * s_r, -scale * s_i).reshape(rows, LANES).astype(bf16)
    ug[...] = jnp.where(left, scale * g_r, -scale * g_i).reshape(rows, LANES).astype(bf16)

    inside = (there < here) | (there == ROWS - 1)
    lags = []
    for ch in range(OWN):
        at = pl.ds(ch, chunks, stride=OWN)
        pairs = lax.dot_general(
            rs[at, :].astype(bf16), gs[at, :].astype(bf16), TN, preferred_element_type=f32
        )
        pairs = pltpu.roll(pairs, 0, 1, stride=1, stride_axis=0)
        lags.append(jnp.sum(jnp.where(inside, pairs, 0.0), axis=0, keepdims=True))
    lags = pltpu.roll(jnp.concatenate(lags, axis=0), 1, 1)
    total = total + jnp.dot(lags, wd[...], precision=highest, preferred_element_type=f32)
    coef_out[...] = total * small[5]
    part = jnp.sum(total * small[4], axis=0, keepdims=True)
    part_out[...] = jnp.broadcast_to(part + pltpu.roll(part, ORDER, 1), part_out.shape)


def owner(place, got, tables, peers):
    chunks = got.shape[0]
    rows = chunks * OWN
    tx, tg, mf, me, wd, small = tables
    flat = jax.ShapeDtypeStruct((rows, LANES), bf16)
    return pl.pallas_call(
        owner_kernel,
        out_shape=(
            jax.ShapeDtypeStruct((peers, LANES), f32),
            jax.ShapeDtypeStruct((OWN, LANES), f32),
            flat,
            flat,
            flat,
            jax.ShapeDtypeStruct((rows, LANES), f32),
        ),
        in_specs=[SMEM] + [VMEM] * 5,
        out_specs=tuple([VMEM] * 6),
        scratch_shapes=[pltpu.VMEM((rows, LANES), f32)] * 2
        + [pltpu.VMEM((rows, 4 * LANES), f32)] * 2
        + [pltpu.VMEM((rows, LANES), f32)] * 4,
        compiler_params=pltpu.CompilerParams(vmem_limit_bytes=24 << 20),
        name="owner",
    )(place, got, tx, tg, wd, small)


def emit_kernel(got, parts, coef, us, ug, xb, head, mf, me, small, out, xs, gs, yc, yg):
    chunks = got.shape[0]
    rows = chunks * OWN

    def cube(array):
        return array.reshape(chunks, OWN, LANES)

    xs[...] = xb[...].astype(f32)
    gs[...] = got.reshape(chunks, WORDS, ROWS)[:, : 2 * OWN].astype(f32)[:, OWN:].reshape(rows, ROWS)
    yc[...] = lax.dot_general(us[...], mf[...], NT, preferred_element_type=f32)
    yg[...] = lax.dot_general(ug[...], me[...], NT, preferred_element_type=f32)
    here = lax.broadcasted_iota(jnp.int32, (ROWS, ROWS), 0)
    there = lax.broadcasted_iota(jnp.int32, (ROWS, ROWS), 1)
    later = there >= here
    filt = small[1]
    for ch in range(OWN):
        at = pl.ds(ch, chunks, stride=OWN)
        toeplitz = pltpu.roll(
            jnp.broadcast_to(filt[ch : ch + 1], (ROWS, ROWS)), 0, 1, stride=1, stride_axis=0
        )
        toeplitz = jnp.where(later, toeplitz, 0.0).astype(bf16)
        yc[at, :] += jnp.dot(xs[at, :].astype(bf16), toeplitz, preferred_element_type=f32)
        yg[at, :] += lax.dot_general(gs[at, :].astype(bf16), toeplitz, NT, preferred_element_type=f32)

    flat = out.reshape(chunks, BACK, ROWS)
    flat[:, : 2 * OWN] = jnp.concatenate([cube(yc[...]), cube(yg[...])], axis=1).astype(bf16)
    lane = lax.broadcasted_iota(jnp.int32, (OWN, LANES), 1)
    row = lax.broadcasted_iota(jnp.int32, (OWN, LANES), 0)
    both = jnp.where(lane < ORDER, coef[...], pltpu.roll(pltpu.roll(coef[...], ORDER, 1), OWN // 2, 0))
    flat[:, 2 * OWN : 2 * OWN + 4] = jnp.broadcast_to(both[: OWN // 2], (chunks, OWN // 2, LANES)).astype(bf16)
    heads = (pltpu.roll(yg[...], ORDER, 1) * head[...]).astype(bf16)
    heads = cube(jnp.dot(heads, head_spots(False), preferred_element_type=f32))
    heads = jnp.sum(jnp.where((lane - ORDER) // 2 == row, heads, 0.0), axis=1, keepdims=True)
    heads = jnp.concatenate([heads[1:], jnp.zeros((1, 1, LANES), f32)], axis=0)
    part = jnp.sum(parts[...], axis=0, keepdims=True)
    low = part - part.astype(bf16).astype(f32)
    left = lane[:1] < ORDER
    high = jnp.where(left, part, heads)
    low = jnp.broadcast_to(jnp.where(left, low, 0.0), (chunks, 1, LANES))
    flat[:, 2 * OWN + 4 :] = jnp.concatenate([high, low], axis=1).astype(bf16)


def head_spots(turned):
    few = lax.broadcasted_iota(jnp.int32, (LANES, LANES), 1 if turned else 0)
    many = lax.broadcasted_iota(jnp.int32, (LANES, LANES), 0 if turned else 1)
    hit = (few // 2 == ORDER // 2) & (many >= ORDER) & (many < ORDER + 2 * OWN) & (few % 2 == many % 2)
    return hit.astype(bf16)


def emit(got, parts, made, tables):
    chunks = got.shape[0]
    rows = chunks * OWN
    tx, tg, mf, me, wd, small = tables
    return pl.pallas_call(
        emit_kernel,
        out_shape=jax.ShapeDtypeStruct((chunks, BACK // 2, 2, ROWS), bf16),
        in_specs=[VMEM] * 10,
        out_specs=VMEM,
        scratch_shapes=[pltpu.VMEM((rows, LANES), f32)] * 4,
        compiler_params=pltpu.CompilerParams(vmem_limit_bytes=24 << 20),
        name="emit",
    )(got, parts, *made, mf, me, small)


def finish_kernel(peers, back, x1, x2, value, tail, weight, y, gx1, gvalue, gcoef, grate):
    shards = back.shape[0]
    wide = shards * OWN
    every = back.reshape(shards, BACK, ROWS)
    both = every[:, : 2 * OWN].astype(f32)
    conv = both[:, :OWN].reshape(wide, ROWS).T
    grad = both[:, OWN:].reshape(wide, ROWS).T
    both = every[:, 2 * OWN : 2 * OWN + 4].astype(f32)
    both = jnp.concatenate([both, pltpu.roll(both, ORDER, 2)], axis=1).reshape(wide, LANES)
    rest = every[:, 2 * OWN + 4 :].astype(f32)
    rates = jnp.sum(jnp.sum(rest, axis=0), axis=0, keepdims=True)
    grate[...] = rates[:, :ORDER] * (LENGTH * wide * peers) ** -0.5
    lane = lax.broadcasted_iota(jnp.int32, (shards, OWN, LANES), 2)
    row = lax.broadcasted_iota(jnp.int32, (shards, OWN, LANES), 1)
    heads = jnp.where((lane - ORDER) // 2 == row, jnp.broadcast_to(rest[:, :1], lane.shape), 0.0)
    heads = jnp.dot(heads.reshape(wide, LANES).astype(bf16), head_spots(True), preferred_element_type=f32)
    lane = lax.broadcasted_iota(jnp.int32, (wide, LANES), 1)
    turned = jnp.where(lane < ORDER, both, heads).T
    gcoef[...] = turned[:ORDER]
    first = x1[...].astype(f32)
    w = weight[...]
    y[...] = (x2[...].astype(f32) * conv).astype(bf16)
    mixed = mix(value[...].astype(f32), tail[...].astype(f32)[14:], w)
    gx1[...] = (grad * mixed).astype(bf16)
    grad_mixed = grad * first
    after = turned[ORDER : ORDER + 2]
    row = lax.broadcasted_iota(jnp.int32, grad_mixed.shape, 0)
    one = jnp.where(row == ROWS - 1, after[0:1], pltpu.roll(grad_mixed, ROWS - 1, 0))
    two = jnp.where(
        row == ROWS - 2,
        after[0:1],
        jnp.where(row == ROWS - 1, after[1:2], pltpu.roll(grad_mixed, ROWS - 2, 0)),
    )
    gvalue[...] = (w[0:1] * grad_mixed + w[1:2] * one + w[2:3] * two).astype(bf16)


def finish(back, x1, x2, value, tail, weight, peers):
    shape = jax.ShapeDtypeStruct(x1.shape, bf16)
    return pl.pallas_call(
        functools.partial(finish_kernel, peers),
        out_shape=(
            shape,
            shape,
            shape,
            jax.ShapeDtypeStruct((ORDER, x1.shape[1]), f32),
            jax.ShapeDtypeStruct((1, ORDER), f32),
        ),
        in_specs=[VMEM] * 6,
        out_specs=tuple([VMEM] * 5),
        compiler_params=pltpu.CompilerParams(vmem_limit_bytes=16 << 20),
        name="finish",
    )(back, x1, x2, value, tail, weight)


def shift(array, by):
    peers = lax.axis_size("seq")
    pairs = [(i, i + by) for i in range(peers) if 0 <= i + by < peers]
    return lax.ppermute(array, "seq", pairs)


def per_device(x1, x2, value, out_grad, short_weight, coef, rate):
    peers = lax.axis_size("chan")
    place = lax.axis_index("seq").astype(jnp.int32)[None]
    tables = make_tables(place, rate, coef, short_weight)
    sent, tail = gate(x1, x2, value, out_grad, short_weight)
    tail = shift(tail, 1)
    got = lax.all_to_all(sent, "seq", split_axis=0, concat_axis=0, tiled=True)
    part, *made = owner(place, got, tables, peers)
    parts = lax.all_to_all(part, "chan", split_axis=0, concat_axis=0, tiled=True)
    done = emit(got, parts, made, tables)
    back = lax.all_to_all(done, "seq", split_axis=0, concat_axis=0, tiled=True)
    y, gx1, gvalue, gcoef, grate = finish(back, x1, x2, value, tail, short_weight, peers)
    return (y, gx1, gvalue, gcoef, grate.reshape(ORDER))


def solution(mesh):
    whole = P("seq", "chan")
    return jax.shard_map(
        per_device,
        mesh=mesh,
        in_specs=(whole, whole, whole, whole, P(None, "chan"), P(None, "chan"), P()),
        out_specs=(whole, whole, whole, P(None, "chan"), P()),
        check_vma=False,
    )
```

```python
import functools
import math

import jax
import jax.numpy as jnp
import numpy as np
from jax import lax
from jax.experimental import pallas as pl
from jax.experimental.pallas import tpu as pltpu
from jax.sharding import PartitionSpec as P

f32 = jnp.float32
bf16 = jnp.bfloat16
highest = lax.Precision.HIGHEST
LENGTH = 8192
ROWS = 128
ORDER = 64
LANES = 128
OWN = 8
WORDS = 2 * OWN + 2
BACK = 2 * OWN + 6
NT = (((1,), (1,)), ((), ()))
TN = (((0,), (0,)), ((), ()))

VMEM = pl.BlockSpec(memory_space=pltpu.VMEM)
SMEM = pl.BlockSpec(memory_space=pltpu.SMEM)


def wave_tables():
    index = np.arange(ORDER)
    cycles = (index // 2 + 1) ** 2
    odd = index % 2 == 1

    def turn(power):
        angle = 2.0 * math.pi / LENGTH * (power[:, None] * cycles[None, :] % LENGTH)
        return np.cos(angle), np.sin(angle)

    ahead = np.arange(ROWS)
    cos_a, sin_a = turn(ahead)
    cos_b, sin_b = turn(ROWS - ahead)
    real_b = np.where(odd, sin_b, cos_b)
    imag_b = np.where(odd, -cos_b, sin_b)
    wave = np.where(odd, sin_a, cos_a)
    cos_l, sin_l = turn(np.array([ROWS]))
    twice = [np.concatenate([t, t], axis=1).astype(np.float32) for t in (cos_a, sin_a, real_b, imag_b, wave)]
    step = np.concatenate([np.concatenate([t, t], axis=1) for t in (cos_l, sin_l)], axis=0).astype(np.float32)
    return (*twice, step)


def split(table):
    high = table.astype(bf16)
    low = (table - high.astype(f32)).astype(bf16)
    return jnp.concatenate([high, low], axis=0)


def table_kernel(
    place, rate, coef, weight, cos_a, sin_a, real_b, imag_b, wave, step, tx, tg, mf, me, wd, small
):
    lane = lax.broadcasted_iota(jnp.int32, (ROWS, LANES), 1)
    power = lax.broadcasted_iota(jnp.int32, (ROWS, LANES), 0).astype(f32)
    left = lane < ORDER
    slope = rate[...] * (-1.0 / LENGTH)
    env_a = jnp.exp(slope * power)
    env_b = jnp.exp(slope * (ROWS - power))
    ar = env_a * cos_a[...]
    ai = env_a * sin_a[...]
    br = env_b * real_b[...]
    bi = env_b * imag_b[...]
    back = ROWS - power
    tx[...] = split(
        jnp.concatenate([br, bi, jnp.where(left, 0.0, back * br), jnp.where(left, 0.0, back * bi)], axis=1)
    )
    tg[...] = split(
        jnp.concatenate([ar, ai, jnp.where(left, ar, power * ar), jnp.where(left, ai, power * ai)], axis=1)
    )
    mf[...] = jnp.where(left, ar, ai).astype(bf16)
    me[...] = jnp.where(left, br, bi).astype(bf16)
    w = env_a * wave[...]
    wd[...] = jnp.where(left, w, power * w)
    pick = lax.broadcasted_iota(jnp.int32, (OWN, coef.shape[1]), 1) - place[0] * OWN
    pick = (pick == lax.broadcasted_iota(jnp.int32, (OWN, coef.shape[1]), 0)).astype(f32)
    own = lax.dot_general(
        pick, jnp.concatenate([coef[...], coef[...]], axis=0), NT, precision=highest, preferred_element_type=f32
    )
    scale = own * jnp.sqrt(rate[...] * (2.0 / LENGTH))
    left8 = left[:OWN]
    decay = jnp.exp(slope * ROWS)
    small[0] = scale
    small[1] = lax.dot_general(
        jnp.where(left8, scale, 0.0), w, NT, precision=highest, preferred_element_type=f32
    )
    small[2] = jnp.broadcast_to(decay * step[0:1], (OWN, LANES))
    small[3] = jnp.broadcast_to(decay * step[1:2], (OWN, LANES))
    small[4] = jnp.where(left8, scale * (0.5 / rate[...]), scale * (-1.0 / LENGTH))
    for tap in (1, 2):
        small[5 + tap] = lax.dot_general(
            pick,
            jnp.broadcast_to(weight[tap : tap + 1], (LANES, coef.shape[1])),
            NT,
            precision=highest,
            preferred_element_type=f32,
        )
    small[5] = jnp.broadcast_to(jnp.sqrt(rate[...] * (2.0 / LENGTH)) * LENGTH ** -0.5, (OWN, LANES))


def make_tables(place, rate, coef, weight):
    consts = [jnp.asarray(t) for t in wave_tables()]
    rate2 = jnp.concatenate([rate, rate])[None, :]
    return pl.pallas_call(
        table_kernel,
        out_shape=(
            jax.ShapeDtypeStruct((2 * ROWS, 4 * LANES), bf16),
            jax.ShapeDtypeStruct((2 * ROWS, 4 * LANES), bf16),
            jax.ShapeDtypeStruct((ROWS, LANES), bf16),
            jax.ShapeDtypeStruct((ROWS, LANES), bf16),
            jax.ShapeDtypeStruct((ROWS, LANES), f32),
            jax.ShapeDtypeStruct((8, OWN, LANES), f32),
        ),
        in_specs=[SMEM] + [VMEM] * 9,
        out_specs=tuple([VMEM] * 6),
        compiler_params=pltpu.CompilerParams(vmem_limit_bytes=12 << 20),
        cost_estimate=pl.CostEstimate(flops=4_000_000, bytes_accessed=1_000_000, transcendentals=40_000),
        name="tables",
    )(place, rate2, coef, weight, *consts)


def mix(value, prior, weight):
    row = lax.broadcasted_iota(jnp.int32, value.shape, 0)
    one = jnp.where(row == 0, prior[1:2], pltpu.roll(value, 1, 0))
    two = jnp.where(row == 0, prior[0:1], jnp.where(row == 1, prior[1:2], pltpu.roll(value, 2, 0)))
    return weight[0:1] * value + weight[1:2] * one + weight[2:3] * two


def gate_kernel(x1h, x2h, vh, oh, wh, sent, x1, x2, v, o, w, sems):
    copies = [
        pltpu.make_async_copy(src, dst, sems.at[n])
        for n, (src, dst) in enumerate(((oh, o), (x2h, x2), (vh, v), (wh, w), (x1h, x1)))
    ]
    for copy in copies:
        copy.start()
    copies[0].wait()
    copies[1].wait()
    shards = sent.shape[0]
    grad = o[...].astype(f32) * x2[...].astype(f32)
    grad = grad.T.reshape(shards, OWN, ROWS)
    for copy in copies[2:]:
        copy.wait()
    value = v[...].astype(f32)
    first = x1[...].astype(f32)
    zero = jnp.zeros((2, value.shape[1]), f32)
    gated = (first * mix(value, zero, w[...])).T.reshape(shards, OWN, ROWS)
    flat = sent.reshape(shards, WORDS, ROWS)
    flat[:, : 2 * OWN] = jnp.concatenate([gated, grad], axis=1).astype(bf16)

    per = LANES // OWN
    lane = lax.broadcasted_iota(jnp.int32, (per, LANES), 1)
    row = lax.broadcasted_iota(jnp.int32, (per, LANES), 0)
    group = lax.rem(lane - row * OWN + LANES, LANES) // OWN
    edges = []
    for at in range(0, value.shape[1], LANES):
        tile = jnp.zeros((per, LANES), f32)
        for n, (source, where) in enumerate(((first, 0), (first, 1), (value, ROWS - 2), (value, ROWS - 1))):
            line = source[where : where + 1, at : at + LANES]
            line = pltpu.roll(line, n * OWN, 1) if n else line
            tile = jnp.where(group == n, line, tile)
        edges.append(tile)
    edges = jnp.concatenate(edges, axis=0)
    flat[:, 2 * OWN :] = jnp.broadcast_to(edges[:, None, :], (shards, 2, LANES)).astype(bf16)


def gate(x1, x2, value, out_grad, weight):
    shards = x1.shape[1] // OWN
    return pl.pallas_call(
        gate_kernel,
        out_shape=jax.ShapeDtypeStruct((shards, WORDS // 2, 2, ROWS), bf16),
        in_specs=[pl.BlockSpec(memory_space=pltpu.HBM)] * 5,
        out_specs=VMEM,
        scratch_shapes=[pltpu.VMEM(x1.shape, bf16)] * 4
        + [pltpu.VMEM(weight.shape, f32), pltpu.SemaphoreType.DMA((5,))],
        compiler_params=pltpu.CompilerParams(vmem_limit_bytes=(64 << 20) - (64 << 10)),
        name="gate",
    )(x1, x2, value, out_grad, weight)


def owner_kernel(
    place, got, tx, tg, wd, small, part_out, coef_out, us, ug, xb_out, head_out, gs, rs, ex, eg, sr, si, gr, gi
):
    chunks = got.shape[0]
    rows = chunks * OWN
    flat = got.reshape(chunks, WORDS, ROWS)
    both = flat[:, : 2 * OWN].astype(f32)
    edge = flat[:, 2 * OWN :].astype(f32)[:, :1]
    edge = jnp.broadcast_to(edge, (chunks, OWN, LANES)).reshape(rows, LANES)
    edge = pltpu.roll(edge, lax.rem(ORDER * LANES - place[0] * OWN, LANES), 1)
    lane3 = lax.broadcasted_iota(jnp.int32, (rows, LANES), 1)
    row3 = lax.broadcasted_iota(jnp.int32, (rows, LANES), 0)
    edge = jnp.where(lane3 % OWN == row3 % OWN, edge, 0.0).astype(bf16)
    group = lax.broadcasted_iota(jnp.int32, (LANES, LANES), 0) // OWN
    to = lax.broadcasted_iota(jnp.int32, (LANES, LANES), 1)
    spot_x1 = ((group < 2) & (to % ORDER == group)).astype(bf16)
    spot_v = (((group == 2) & (to == 0)) | ((group == 3) & (to == 1))).astype(bf16)
    spot_last = ((group == 3) & (to == 0)).astype(bf16)
    spread = jnp.dot(
        edge, jnp.concatenate([spot_x1, spot_v, spot_last], axis=1), preferred_element_type=f32
    )
    x1_head = spread[:, :LANES]
    before = (
        small[7] * spread[:, LANES : 2 * LANES].reshape(chunks, OWN, LANES)
        + small[6] * spread[:, 2 * LANES :].reshape(chunks, OWN, LANES)
    )
    before = jnp.concatenate([jnp.zeros((1, OWN, LANES), f32), before[:-1]], axis=0)
    x = both[:, :OWN].reshape(rows, ROWS) + x1_head * before.reshape(rows, LANES)
    g = both[:, OWN:].reshape(rows, ROWS)
    gs[...] = g
    xb = x.astype(bf16)
    xb_out[...] = xb
    head_out[...] = jnp.where(lane3 < ORDER, spread[:, LANES : 2 * LANES], x1_head)
    gb = g.astype(bf16)
    here = lax.broadcasted_iota(jnp.int32, (ROWS, ROWS), 0)
    there = lax.broadcasted_iota(jnp.int32, (ROWS, ROWS), 1)
    mirror = (here + there == ROWS - 1).astype(bf16)
    rs[...] = jnp.dot(xb, mirror, preferred_element_type=f32)
    ex[...] = jnp.dot(
        jnp.concatenate([xb, xb], axis=1), tx[...], preferred_element_type=f32
    )
    eg[...] = jnp.dot(
        jnp.concatenate([gb, gb], axis=1), tg[...], preferred_element_type=f32
    )
    scale = small[0]
    lr = small[2]
    li = small[3]

    a = b = c = d = jnp.zeros((OWN, LANES), f32)
    for k in range(chunks):
        at = pl.ds(k * OWN, OWN)
        sr[at] = a
        si[at] = b
        a, b = (
            lr * a - li * b + ex[at, 0:LANES],
            lr * b + li * a + ex[at, LANES : 2 * LANES],
        )
        at = pl.ds((chunks - 1 - k) * OWN, OWN)
        gr[at] = c
        gi[at] = d
        c, d = (
            lr * c - li * d + eg[at, 0:LANES],
            lr * d + li * c + eg[at, LANES : 2 * LANES],
        )

    left = lax.broadcasted_iota(jnp.int32, (OWN, LANES), 1) < ORDER

    def cube(array):
        return array.reshape(chunks, OWN, LANES)

    s_r, s_i, g_r, g_i = (cube(ref[...]) for ref in (sr, si, gr, gi))
    over = jnp.where(left, 0.0, float(ROWS))
    ahead_r = over * lr * g_r - over * li * g_i
    ahead_i = over * lr * g_i + over * li * g_r
    total = (
        s_r * (cube(eg[:, 2 * LANES : 3 * LANES]) + ahead_r)
        - s_i * (cube(eg[:, 3 * LANES : 4 * LANES]) + ahead_i)
        + g_r * cube(ex[:, 2 * LANES : 3 * LANES])
        - g_i * cube(ex[:, 3 * LANES : 4 * LANES])
    )
    total = jnp.sum(total, axis=0)
    us[...] = jnp.where(left, scale * s_r, -scale * s_i).reshape(rows, LANES).astype(bf16)
    ug[...] = jnp.where(left, scale * g_r, -scale * g_i).reshape(rows, LANES).astype(bf16)

    inside = (there < here) | (there == ROWS - 1)
    lags = []
    for ch in range(OWN):
        at = pl.ds(ch, chunks, stride=OWN)
        pairs = lax.dot_general(
            rs[at, :].astype(bf16), gs[at, :].astype(bf16), TN, preferred_element_type=f32
        )
        pairs = pltpu.roll(pairs, 0, 1, stride=1, stride_axis=0)
        lags.append(jnp.sum(jnp.where(inside, pairs, 0.0), axis=0, keepdims=True))
    lags = pltpu.roll(jnp.concatenate(lags, axis=0), 1, 1)
    total = total + jnp.dot(lags, wd[...], precision=highest, preferred_element_type=f32)
    coef_out[...] = total * small[5]
    part = jnp.sum(total * small[4], axis=0, keepdims=True)
    part_out[...] = jnp.broadcast_to(part + pltpu.roll(part, ORDER, 1), part_out.shape)


def owner(place, got, tables, peers):
    chunks = got.shape[0]
    rows = chunks * OWN
    tx, tg, mf, me, wd, small = tables
    flat = jax.ShapeDtypeStruct((rows, LANES), bf16)
    return pl.pallas_call(
        owner_kernel,
        out_shape=(
            jax.ShapeDtypeStruct((peers, LANES), f32),
            jax.ShapeDtypeStruct((OWN, LANES), f32),
            flat,
            flat,
            flat,
            jax.ShapeDtypeStruct((rows, LANES), f32),
        ),
        in_specs=[SMEM] + [VMEM] * 5,
        out_specs=tuple([VMEM] * 6),
        scratch_shapes=[pltpu.VMEM((rows, LANES), f32)] * 2
        + [pltpu.VMEM((rows, 4 * LANES), f32)] * 2
        + [pltpu.VMEM((rows, LANES), f32)] * 4,
        compiler_params=pltpu.CompilerParams(vmem_limit_bytes=24 << 20),
        name="owner",
    )(place, got, tx, tg, wd, small)


def emit_kernel(got, parts, coef, us, ug, xb, head, mf, me, small, out, xs, gs, yc, yg):
    chunks = got.shape[0]
    rows = chunks * OWN

    def cube(array):
        return array.reshape(chunks, OWN, LANES)

    xs[...] = xb[...].astype(f32)
    gs[...] = got.reshape(chunks, WORDS, ROWS)[:, : 2 * OWN].astype(f32)[:, OWN:].reshape(rows, ROWS)
    yc[...] = lax.dot_general(us[...], mf[...], NT, preferred_element_type=f32)
    yg[...] = lax.dot_general(ug[...], me[...], NT, preferred_element_type=f32)
    here = lax.broadcasted_iota(jnp.int32, (ROWS, ROWS), 0)
    there = lax.broadcasted_iota(jnp.int32, (ROWS, ROWS), 1)
    later = there >= here
    filt = small[1]
    for ch in range(OWN):
        at = pl.ds(ch, chunks, stride=OWN)
        toeplitz = pltpu.roll(
            jnp.broadcast_to(filt[ch : ch + 1], (ROWS, ROWS)), 0, 1, stride=1, stride_axis=0
        )
        toeplitz = jnp.where(later, toeplitz, 0.0).astype(bf16)
        yc[at, :] += jnp.dot(xs[at, :].astype(bf16), toeplitz, preferred_element_type=f32)
        yg[at, :] += lax.dot_general(gs[at, :].astype(bf16), toeplitz, NT, preferred_element_type=f32)

    flat = out.reshape(chunks, BACK, ROWS)
    flat[:, : 2 * OWN] = jnp.concatenate([cube(yc[...]), cube(yg[...])], axis=1).astype(bf16)
    lane = lax.broadcasted_iota(jnp.int32, (OWN, LANES), 1)
    row = lax.broadcasted_iota(jnp.int32, (OWN, LANES), 0)
    both = jnp.where(lane < ORDER, coef[...], pltpu.roll(pltpu.roll(coef[...], ORDER, 1), OWN // 2, 0))
    flat[:, 2 * OWN : 2 * OWN + 4] = jnp.broadcast_to(both[: OWN // 2], (chunks, OWN // 2, LANES)).astype(bf16)
    lane2 = lax.broadcasted_iota(jnp.int32, (rows, LANES), 1)
    ends = jnp.where(lane2 < ORDER, head[...], pltpu.roll(yg[...], ORDER, 1) * head[...]).astype(bf16)
    ends = cube(jnp.dot(ends, end_spots(False), preferred_element_type=f32))
    ends = jnp.sum(jnp.where(lane % ORDER // 2 == row, ends, 0.0), axis=1, keepdims=True)
    none = jnp.zeros((1, 1, LANES), f32)
    part = jnp.sum(parts[...], axis=0, keepdims=True)
    low = part - part.astype(bf16).astype(f32)
    left = lane[:1] < ORDER
    high = jnp.where(left, part, jnp.concatenate([ends[1:], none], axis=0))
    ends = pltpu.roll(jnp.concatenate([none, ends[:-1]], axis=0), ORDER, 2)
    low = jnp.where(left, low, ends)
    flat[:, 2 * OWN + 4 :] = jnp.concatenate([high, low], axis=1).astype(bf16)


def end_spots(turned):
    few = lax.broadcasted_iota(jnp.int32, (LANES, LANES), 1 if turned else 0)
    many = lax.broadcasted_iota(jnp.int32, (LANES, LANES), 0 if turned else 1)
    hit = (many % ORDER < 2 * OWN) & (few % 2 == many % 2)
    if turned:
        hit &= few // 2 == jnp.where(many < ORDER, ORDER // 2 + 1, ORDER // 2)
    else:
        hit &= few // 2 == many // ORDER * (ORDER // 2)
    return hit.astype(bf16)


def emit(got, parts, made, tables):
    chunks = got.shape[0]
    rows = chunks * OWN
    tx, tg, mf, me, wd, small = tables
    return pl.pallas_call(
        emit_kernel,
        out_shape=jax.ShapeDtypeStruct((chunks, BACK // 2, 2, ROWS), bf16),
        in_specs=[VMEM] * 10,
        out_specs=VMEM,
        scratch_shapes=[pltpu.VMEM((rows, LANES), f32)] * 4,
        compiler_params=pltpu.CompilerParams(vmem_limit_bytes=24 << 20),
        name="emit",
    )(got, parts, *made, mf, me, small)


def finish_kernel(peers, back, x1, x2, value, weight, y, gx1, gvalue, gcoef, grate):
    shards = back.shape[0]
    wide = shards * OWN
    every = back.reshape(shards, BACK, ROWS)
    both = every[:, : 2 * OWN].astype(f32)
    conv = both[:, :OWN].reshape(wide, ROWS).T
    grad = both[:, OWN:].reshape(wide, ROWS).T
    both = every[:, 2 * OWN : 2 * OWN + 4].astype(f32)
    both = jnp.concatenate([both, pltpu.roll(both, ORDER, 2)], axis=1).reshape(wide, LANES)
    rest = every[:, 2 * OWN + 4 :].astype(f32)
    rates = jnp.sum(jnp.sum(rest, axis=0), axis=0, keepdims=True)
    grate[...] = rates[:, :ORDER] * (LENGTH * wide * peers) ** -0.5
    lane = lax.broadcasted_iota(jnp.int32, (shards, OWN, LANES), 2)
    row = lax.broadcasted_iota(jnp.int32, (shards, OWN, LANES), 1)
    ends = jnp.where(lane[:, :1] < ORDER, pltpu.roll(rest[:, 1:], ORDER, 2), rest[:, :1])
    ends = jnp.where(lane % ORDER // 2 == row, jnp.broadcast_to(ends, lane.shape), 0.0)
    ends = jnp.dot(ends.reshape(wide, LANES).astype(bf16), end_spots(True), preferred_element_type=f32)
    lane = lax.broadcasted_iota(jnp.int32, (wide, LANES), 1)
    turned = jnp.where(lane < ORDER, both, ends).T
    gcoef[...] = turned[:ORDER]
    first = x1[...].astype(f32)
    w = weight[...]
    y[...] = (x2[...].astype(f32) * conv).astype(bf16)
    mixed = mix(value[...].astype(f32), turned[ORDER + 2 : ORDER + 4], w)
    gx1[...] = (grad * mixed).astype(bf16)
    grad_mixed = grad * first
    after = turned[ORDER : ORDER + 2]
    row = lax.broadcasted_iota(jnp.int32, grad_mixed.shape, 0)
    one = jnp.where(row == ROWS - 1, after[0:1], pltpu.roll(grad_mixed, ROWS - 1, 0))
    two = jnp.where(
        row == ROWS - 2,
        after[0:1],
        jnp.where(row == ROWS - 1, after[1:2], pltpu.roll(grad_mixed, ROWS - 2, 0)),
    )
    gvalue[...] = (w[0:1] * grad_mixed + w[1:2] * one + w[2:3] * two).astype(bf16)


def finish(back, x1, x2, value, weight, peers):
    shape = jax.ShapeDtypeStruct(x1.shape, bf16)
    return pl.pallas_call(
        functools.partial(finish_kernel, peers),
        out_shape=(
            shape,
            shape,
            shape,
            jax.ShapeDtypeStruct((ORDER, x1.shape[1]), f32),
            jax.ShapeDtypeStruct((1, ORDER), f32),
        ),
        in_specs=[VMEM] * 5,
        out_specs=tuple([VMEM] * 5),
        compiler_params=pltpu.CompilerParams(vmem_limit_bytes=16 << 20),
        name="finish",
    )(back, x1, x2, value, weight)


def per_device(x1, x2, value, out_grad, short_weight, coef, rate):
    peers = lax.axis_size("chan")
    place = lax.axis_index("seq").astype(jnp.int32)[None]
    tables = make_tables(place, rate, coef, short_weight)
    sent = gate(x1, x2, value, out_grad, short_weight)
    got = lax.all_to_all(sent, "seq", split_axis=0, concat_axis=0, tiled=True)
    part, *made = owner(place, got, tables, peers)
    parts = lax.all_to_all(part, "chan", split_axis=0, concat_axis=0, tiled=True)
    done = emit(got, parts, made, tables)
    back = lax.all_to_all(done, "seq", split_axis=0, concat_axis=0, tiled=True)
    y, gx1, gvalue, gcoef, grate = finish(back, x1, x2, value, short_weight, peers)
    return (y, gx1, gvalue, gcoef, grate.reshape(ORDER))


def solution(mesh):
    whole = P("seq", "chan")
    return jax.shard_map(
        per_device,
        mesh=mesh,
        in_specs=(whole, whole, whole, whole, P(None, "chan"), P(None, "chan"), P()),
        out_specs=(whole, whole, whole, P(None, "chan"), P()),
        check_vma=False,
    )
```

```python
import math

import jax
import jax.numpy as jnp
import numpy as np
from jax import lax
from jax.experimental import pallas as pl
from jax.experimental.pallas import tpu as pltpu
from jax.sharding import PartitionSpec as P

f32 = jnp.float32
bf16 = jnp.bfloat16
highest = lax.Precision.HIGHEST
LENGTH = 8192
ROWS = 128
ORDER = 64
LANES = 128
OWN = 8
WORDS = 2 * OWN + 2
BACK = 2 * OWN + 6
NT = (((1,), (1,)), ((), ()))
TN = (((0,), (0,)), ((), ()))

VMEM = pl.BlockSpec(memory_space=pltpu.VMEM)
SMEM = pl.BlockSpec(memory_space=pltpu.SMEM)


def wave_tables():
    index = np.arange(ORDER)
    cycles = (index // 2 + 1) ** 2
    odd = index % 2 == 1

    def turn(power):
        angle = 2.0 * math.pi / LENGTH * (power[:, None] * cycles[None, :] % LENGTH)
        return np.cos(angle), np.sin(angle)

    ahead = np.arange(ROWS)
    cos_a, sin_a = turn(ahead)
    cos_b, sin_b = turn(ROWS - ahead)
    real_b = np.where(odd, sin_b, cos_b)
    imag_b = np.where(odd, -cos_b, sin_b)
    wave = np.where(odd, sin_a, cos_a)
    cos_l, sin_l = turn(np.array([ROWS]))
    twice = [np.concatenate([t, t], axis=1).astype(np.float32) for t in (cos_a, sin_a, real_b, imag_b, wave)]
    step = np.concatenate([np.concatenate([t, t], axis=1) for t in (cos_l, sin_l)], axis=0).astype(np.float32)
    return (*twice, step)


def split(table):
    high = table.astype(bf16)
    low = (table - high.astype(f32)).astype(bf16)
    return jnp.concatenate([high, low], axis=0)


def table_kernel(
    place, rate, coef, weight, cos_a, sin_a, real_b, imag_b, wave, step, tx, tg, mf, me, wd, small
):
    lane = lax.broadcasted_iota(jnp.int32, (ROWS, LANES), 1)
    power = lax.broadcasted_iota(jnp.int32, (ROWS, LANES), 0).astype(f32)
    left = lane < ORDER
    slope = rate[...] * (-1.0 / LENGTH)
    env_a = jnp.exp(slope * power)
    env_b = jnp.exp(slope * (ROWS - power))
    ar = env_a * cos_a[...]
    ai = env_a * sin_a[...]
    br = env_b * real_b[...]
    bi = env_b * imag_b[...]
    back = ROWS - power
    tx[...] = split(
        jnp.concatenate([br, bi, jnp.where(left, 0.0, back * br), jnp.where(left, 0.0, back * bi)], axis=1)
    )
    tg[...] = split(
        jnp.concatenate([ar, ai, jnp.where(left, ar, power * ar), jnp.where(left, ai, power * ai)], axis=1)
    )
    mf[...] = jnp.where(left, ar, ai).astype(bf16)
    me[...] = jnp.where(left, br, bi).astype(bf16)
    w = env_a * wave[...]
    wd[...] = jnp.where(left, w, power * w)
    pick = lax.broadcasted_iota(jnp.int32, (OWN, coef.shape[1]), 1) - place[0] * OWN
    pick = (pick == lax.broadcasted_iota(jnp.int32, (OWN, coef.shape[1]), 0)).astype(f32)
    own = lax.dot_general(
        pick, jnp.concatenate([coef[...], coef[...]], axis=0), NT, precision=highest, preferred_element_type=f32
    )
    scale = own * jnp.sqrt(rate[...] * (2.0 / LENGTH))
    left8 = left[:OWN]
    decay = jnp.exp(slope * ROWS)
    small[0] = scale
    small[1] = lax.dot_general(
        jnp.where(left8, scale, 0.0), w, NT, precision=highest, preferred_element_type=f32
    )
    small[2] = jnp.broadcast_to(decay * step[0:1], (OWN, LANES))
    small[3] = jnp.broadcast_to(decay * step[1:2], (OWN, LANES))
    small[4] = jnp.where(left8, scale * (0.5 / rate[...]), scale * (-1.0 / LENGTH))
    for tap in (1, 2):
        small[5 + tap] = lax.dot_general(
            pick,
            jnp.broadcast_to(weight[tap : tap + 1], (LANES, coef.shape[1])),
            NT,
            precision=highest,
            preferred_element_type=f32,
        )
    small[5] = jnp.broadcast_to(jnp.sqrt(rate[...] * (2.0 / LENGTH)) * LENGTH ** -0.5, (OWN, LANES))


def make_tables(place, rate, coef, weight):
    consts = [jnp.asarray(t) for t in wave_tables()]
    rate2 = jnp.concatenate([rate, rate])[None, :]
    return pl.pallas_call(
        table_kernel,
        out_shape=(
            jax.ShapeDtypeStruct((2 * ROWS, 4 * LANES), bf16),
            jax.ShapeDtypeStruct((2 * ROWS, 4 * LANES), bf16),
            jax.ShapeDtypeStruct((ROWS, LANES), bf16),
            jax.ShapeDtypeStruct((ROWS, LANES), bf16),
            jax.ShapeDtypeStruct((ROWS, LANES), f32),
            jax.ShapeDtypeStruct((8, OWN, LANES), f32),
        ),
        in_specs=[SMEM] + [VMEM] * 9,
        out_specs=tuple([VMEM] * 6),
        compiler_params=pltpu.CompilerParams(vmem_limit_bytes=12 << 20),
        cost_estimate=pl.CostEstimate(flops=4_000_000, bytes_accessed=1_000_000, transcendentals=40_000),
        name="tables",
    )(place, rate2, coef, weight, *consts)


def mix(value, prior, weight):
    row = lax.broadcasted_iota(jnp.int32, value.shape, 0)
    one = jnp.where(row == 0, prior[1:2], pltpu.roll(value, 1, 0))
    two = jnp.where(row == 0, prior[0:1], jnp.where(row == 1, prior[1:2], pltpu.roll(value, 2, 0)))
    return weight[0:1] * value + weight[1:2] * one + weight[2:3] * two


def gate_kernel(x1h, x2h, vh, oh, wh, sent, x1, x2, v, o, w, sems):
    copies = [
        pltpu.make_async_copy(src, dst, sems.at[n])
        for n, (src, dst) in enumerate(((oh, o), (x2h, x2), (vh, v), (wh, w), (x1h, x1)))
    ]
    for copy in copies:
        copy.start()
    copies[0].wait()
    copies[1].wait()
    shards = sent.shape[0]
    grad = o[...].astype(f32) * x2[...].astype(f32)
    grad = grad.T.reshape(shards, OWN, ROWS)
    for copy in copies[2:]:
        copy.wait()
    value = v[...].astype(f32)
    first = x1[...].astype(f32)
    zero = jnp.zeros((2, value.shape[1]), f32)
    gated = (first * mix(value, zero, w[...])).T.reshape(shards, OWN, ROWS)
    flat = sent.reshape(shards, WORDS, ROWS)
    flat[:, : 2 * OWN] = jnp.concatenate([gated, grad], axis=1).astype(bf16)

    per = LANES // OWN
    lane = lax.broadcasted_iota(jnp.int32, (per, LANES), 1)
    row = lax.broadcasted_iota(jnp.int32, (per, LANES), 0)
    group = lax.rem(lane - row * OWN + LANES, LANES) // OWN
    edges = []
    for at in range(0, value.shape[1], LANES):
        tile = jnp.zeros((per, LANES), f32)
        for n, (source, where) in enumerate(((first, 0), (first, 1), (value, ROWS - 2), (value, ROWS - 1))):
            line = source[where : where + 1, at : at + LANES]
            line = pltpu.roll(line, n * OWN, 1) if n else line
            tile = jnp.where(group == n, line, tile)
        edges.append(tile)
    edges = jnp.concatenate(edges, axis=0)
    flat[:, 2 * OWN :] = jnp.broadcast_to(edges[:, None, :], (shards, 2, LANES)).astype(bf16)


def gate(x1, x2, value, out_grad, weight):
    shards = x1.shape[1] // OWN
    return pl.pallas_call(
        gate_kernel,
        out_shape=jax.ShapeDtypeStruct((shards, WORDS // 2, 2, ROWS), bf16),
        in_specs=[pl.BlockSpec(memory_space=pltpu.HBM)] * 5,
        out_specs=VMEM,
        scratch_shapes=[pltpu.VMEM(x1.shape, bf16)] * 4
        + [pltpu.VMEM(weight.shape, f32), pltpu.SemaphoreType.DMA((5,))],
        compiler_params=pltpu.CompilerParams(vmem_limit_bytes=(64 << 20) - (64 << 10)),
        name="gate",
    )(x1, x2, value, out_grad, weight)


def owner_kernel(
    place, got, tx, tg, wd, small, part_out, coef_out, us, ug, xb_out, head_out, gs, rs, ex, eg, sr, si, gr, gi
):
    chunks = got.shape[0]
    rows = chunks * OWN
    flat = got.reshape(chunks, WORDS, ROWS)
    both = flat[:, : 2 * OWN].astype(f32)
    edge = flat[:, 2 * OWN :].astype(f32)[:, :1]
    edge = jnp.broadcast_to(edge, (chunks, OWN, LANES)).reshape(rows, LANES)
    edge = pltpu.roll(edge, lax.rem(ORDER * LANES - place[0] * OWN, LANES), 1)
    lane3 = lax.broadcasted_iota(jnp.int32, (rows, LANES), 1)
    row3 = lax.broadcasted_iota(jnp.int32, (rows, LANES), 0)
    edge = jnp.where(lane3 % OWN == row3 % OWN, edge, 0.0).astype(bf16)
    group = lax.broadcasted_iota(jnp.int32, (LANES, LANES), 0) // OWN
    to = lax.broadcasted_iota(jnp.int32, (LANES, LANES), 1)
    spot_x1 = ((group < 2) & (to % ORDER == group)).astype(bf16)
    spot_v = (((group == 2) & (to == 0)) | ((group == 3) & (to == 1))).astype(bf16)
    spot_last = ((group == 3) & (to == 0)).astype(bf16)
    spread = jnp.dot(
        edge, jnp.concatenate([spot_x1, spot_v, spot_last], axis=1), preferred_element_type=f32
    )
    x1_head = spread[:, :LANES]
    before = (
        small[7] * spread[:, LANES : 2 * LANES].reshape(chunks, OWN, LANES)
        + small[6] * spread[:, 2 * LANES :].reshape(chunks, OWN, LANES)
    )
    before = jnp.concatenate([jnp.zeros((1, OWN, LANES), f32), before[:-1]], axis=0)
    x = both[:, :OWN].reshape(rows, ROWS) + x1_head * before.reshape(rows, LANES)
    g = both[:, OWN:].reshape(rows, ROWS)
    gs[...] = g
    xb = x.astype(bf16)
    xb_out[...] = xb
    head_out[...] = jnp.where(lane3 < ORDER, spread[:, LANES : 2 * LANES], x1_head)
    gb = g.astype(bf16)
    here = lax.broadcasted_iota(jnp.int32, (ROWS, ROWS), 0)
    there = lax.broadcasted_iota(jnp.int32, (ROWS, ROWS), 1)
    mirror = (here + there == ROWS - 1).astype(bf16)
    rs[...] = jnp.dot(xb, mirror, preferred_element_type=f32)
    ex[...] = jnp.dot(
        jnp.concatenate([xb, xb], axis=1), tx[...], preferred_element_type=f32
    )
    eg[...] = jnp.dot(
        jnp.concatenate([gb, gb], axis=1), tg[...], preferred_element_type=f32
    )
    scale = small[0]
    lr = small[2]
    li = small[3]

    a = b = c = d = jnp.zeros((OWN, LANES), f32)
    for k in range(chunks):
        at = pl.ds(k * OWN, OWN)
        sr[at] = a
        si[at] = b
        a, b = (
            lr * a - li * b + ex[at, 0:LANES],
            lr * b + li * a + ex[at, LANES : 2 * LANES],
        )
        at = pl.ds((chunks - 1 - k) * OWN, OWN)
        gr[at] = c
        gi[at] = d
        c, d = (
            lr * c - li * d + eg[at, 0:LANES],
            lr * d + li * c + eg[at, LANES : 2 * LANES],
        )

    left = lax.broadcasted_iota(jnp.int32, (OWN, LANES), 1) < ORDER

    def cube(array):
        return array.reshape(chunks, OWN, LANES)

    s_r, s_i, g_r, g_i = (cube(ref[...]) for ref in (sr, si, gr, gi))
    over = jnp.where(left, 0.0, float(ROWS))
    ahead_r = over * lr * g_r - over * li * g_i
    ahead_i = over * lr * g_i + over * li * g_r
    total = (
        s_r * (cube(eg[:, 2 * LANES : 3 * LANES]) + ahead_r)
        - s_i * (cube(eg[:, 3 * LANES : 4 * LANES]) + ahead_i)
        + g_r * cube(ex[:, 2 * LANES : 3 * LANES])
        - g_i * cube(ex[:, 3 * LANES : 4 * LANES])
    )
    total = jnp.sum(total, axis=0)
    us[...] = jnp.where(left, scale * s_r, -scale * s_i).reshape(rows, LANES).astype(bf16)
    ug[...] = jnp.where(left, scale * g_r, -scale * g_i).reshape(rows, LANES).astype(bf16)

    inside = (there < here) | (there == ROWS - 1)
    lags = []
    for ch in range(OWN):
        at = pl.ds(ch, chunks, stride=OWN)
        pairs = lax.dot_general(
            rs[at, :].astype(bf16), gs[at, :].astype(bf16), TN, preferred_element_type=f32
        )
        pairs = pltpu.roll(pairs, 0, 1, stride=1, stride_axis=0)
        lags.append(jnp.sum(jnp.where(inside, pairs, 0.0), axis=0, keepdims=True))
    lags = pltpu.roll(jnp.concatenate(lags, axis=0), 1, 1)
    total = total + jnp.dot(lags, wd[...], precision=highest, preferred_element_type=f32)
    coef_out[...] = total * small[5]
    part = jnp.sum(total * small[4], axis=0, keepdims=True)
    part_out[...] = jnp.broadcast_to(part + pltpu.roll(part, ORDER, 1), part_out.shape)


def emit_kernel(got, parts, coef, us, ug, xb, head, mf, me, small, out, xs, gs, yc, yg):
    chunks = got.shape[0]
    rows = chunks * OWN

    def cube(array):
        return array.reshape(chunks, OWN, LANES)

    xs[...] = xb[...].astype(f32)
    gs[...] = got.reshape(chunks, WORDS, ROWS)[:, : 2 * OWN].astype(f32)[:, OWN:].reshape(rows, ROWS)
    yc[...] = lax.dot_general(us[...], mf[...], NT, preferred_element_type=f32)
    yg[...] = lax.dot_general(ug[...], me[...], NT, preferred_element_type=f32)
    here = lax.broadcasted_iota(jnp.int32, (ROWS, ROWS), 0)
    there = lax.broadcasted_iota(jnp.int32, (ROWS, ROWS), 1)
    later = there >= here
    filt = small[1]
    for ch in range(OWN):
        at = pl.ds(ch, chunks, stride=OWN)
        toeplitz = pltpu.roll(
            jnp.broadcast_to(filt[ch : ch + 1], (ROWS, ROWS)), 0, 1, stride=1, stride_axis=0
        )
        toeplitz = jnp.where(later, toeplitz, 0.0).astype(bf16)
        yc[at, :] += jnp.dot(xs[at, :].astype(bf16), toeplitz, preferred_element_type=f32)
        yg[at, :] += lax.dot_general(gs[at, :].astype(bf16), toeplitz, NT, preferred_element_type=f32)

    flat = out.reshape(chunks, BACK, ROWS)
    flat[:, : 2 * OWN] = jnp.concatenate([cube(yc[...]), cube(yg[...])], axis=1).astype(bf16)
    lane = lax.broadcasted_iota(jnp.int32, (OWN, LANES), 1)
    row = lax.broadcasted_iota(jnp.int32, (OWN, LANES), 0)
    both = jnp.where(lane < ORDER, coef[...], pltpu.roll(pltpu.roll(coef[...], ORDER, 1), OWN // 2, 0))
    flat[:, 2 * OWN : 2 * OWN + 4] = jnp.broadcast_to(both[: OWN // 2], (chunks, OWN // 2, LANES)).astype(bf16)
    lane2 = lax.broadcasted_iota(jnp.int32, (rows, LANES), 1)
    ends = jnp.where(lane2 < ORDER, head[...], pltpu.roll(yg[...], ORDER, 1) * head[...]).astype(bf16)
    ends = cube(jnp.dot(ends, end_spots(False), preferred_element_type=f32))
    ends = jnp.sum(jnp.where(lane % ORDER // 2 == row, ends, 0.0), axis=1, keepdims=True)
    none = jnp.zeros((1, 1, LANES), f32)
    part = jnp.sum(parts[...], axis=0, keepdims=True)
    low = part - part.astype(bf16).astype(f32)
    left = lane[:1] < ORDER
    high = jnp.where(left, part, jnp.concatenate([ends[1:], none], axis=0))
    ends = pltpu.roll(jnp.concatenate([none, ends[:-1]], axis=0), ORDER, 2)
    low = jnp.where(left, low, ends)
    flat[:, 2 * OWN + 4 :] = jnp.concatenate([high, low], axis=1).astype(bf16)


def end_spots(turned):
    few = lax.broadcasted_iota(jnp.int32, (LANES, LANES), 1 if turned else 0)
    many = lax.broadcasted_iota(jnp.int32, (LANES, LANES), 0 if turned else 1)
    hit = (many % ORDER < 2 * OWN) & (few % 2 == many % 2)
    if turned:
        hit &= few // 2 == jnp.where(many < ORDER, ORDER // 2 + 1, ORDER // 2)
    else:
        hit &= few // 2 == many // ORDER * (ORDER // 2)
    return hit.astype(bf16)


def owner_emit_kernel(
    place, got, tx, tg, mf, me, wd, small, out, part, coef, us, ug, xb, head, gs, rs, ex, eg, sr, si, gr, gi, xs, yc, yg
):
    owner_kernel(place, got, tx, tg, wd, small, part, coef, us, ug, xb, head, gs, rs, ex, eg, sr, si, gr, gi)
    emit_kernel(got, part, coef, us, ug, xb, head, mf, me, small, out, xs, gs, yc, yg)


def owner_emit(place, got, tables):
    chunks = got.shape[0]
    rows = chunks * OWN
    wide = pltpu.VMEM((rows, LANES), f32)
    flat = pltpu.VMEM((rows, LANES), bf16)
    tall = pltpu.VMEM((rows, 4 * LANES), f32)
    return pl.pallas_call(
        owner_emit_kernel,
        out_shape=jax.ShapeDtypeStruct((chunks, BACK // 2, 2, ROWS), bf16),
        in_specs=[SMEM] + [VMEM] * 7,
        out_specs=VMEM,
        scratch_shapes=[pltpu.VMEM((1, LANES), f32), pltpu.VMEM((OWN, LANES), f32)]
        + [flat] * 3
        + [wide] * 3
        + [tall] * 2
        + [wide] * 7,
        compiler_params=pltpu.CompilerParams(vmem_limit_bytes=24 << 20),
        name="owner",
    )(place, got, *tables)


def rate_kernel(back, parts):
    flat = back.reshape(back.shape[0], BACK, ROWS)
    rates = jnp.sum(jnp.sum(flat[:, 2 * OWN + 4 :].astype(f32), axis=0), axis=0, keepdims=True)
    parts[...] = jnp.broadcast_to(rates, parts.shape)


def rate_parts(back, peers):
    return pl.pallas_call(
        rate_kernel,
        out_shape=jax.ShapeDtypeStruct((peers, LANES), f32),
        in_specs=[VMEM],
        out_specs=VMEM,
        compiler_params=pltpu.CompilerParams(vmem_limit_bytes=8 << 20),
        name="rates",
    )(back)


def finish_kernel(back, x1, x2, value, weight, y, gx1, gvalue, gcoef):
    shards = back.shape[0]
    wide = shards * OWN
    every = back.reshape(shards, BACK, ROWS)
    both = every[:, : 2 * OWN].astype(f32)
    conv = both[:, :OWN].reshape(wide, ROWS).T
    grad = both[:, OWN:].reshape(wide, ROWS).T
    both = every[:, 2 * OWN : 2 * OWN + 4].astype(f32)
    both = jnp.concatenate([both, pltpu.roll(both, ORDER, 2)], axis=1).reshape(wide, LANES)
    rest = every[:, 2 * OWN + 4 :].astype(f32)
    lane = lax.broadcasted_iota(jnp.int32, (shards, OWN, LANES), 2)
    row = lax.broadcasted_iota(jnp.int32, (shards, OWN, LANES), 1)
    ends = jnp.where(lane[:, :1] < ORDER, pltpu.roll(rest[:, 1:], ORDER, 2), rest[:, :1])
    ends = jnp.where(lane % ORDER // 2 == row, jnp.broadcast_to(ends, lane.shape), 0.0)
    ends = jnp.dot(ends.reshape(wide, LANES).astype(bf16), end_spots(True), preferred_element_type=f32)
    lane = lax.broadcasted_iota(jnp.int32, (wide, LANES), 1)
    turned = jnp.where(lane < ORDER, both, ends).T
    gcoef[...] = turned[:ORDER]
    first = x1[...].astype(f32)
    w = weight[...]
    y[...] = (x2[...].astype(f32) * conv).astype(bf16)
    mixed = mix(value[...].astype(f32), turned[ORDER + 2 : ORDER + 4], w)
    gx1[...] = (grad * mixed).astype(bf16)
    grad_mixed = grad * first
    after = turned[ORDER : ORDER + 2]
    row = lax.broadcasted_iota(jnp.int32, grad_mixed.shape, 0)
    one = jnp.where(row == ROWS - 1, after[0:1], pltpu.roll(grad_mixed, ROWS - 1, 0))
    two = jnp.where(
        row == ROWS - 2,
        after[0:1],
        jnp.where(row == ROWS - 1, after[1:2], pltpu.roll(grad_mixed, ROWS - 2, 0)),
    )
    gvalue[...] = (w[0:1] * grad_mixed + w[1:2] * one + w[2:3] * two).astype(bf16)


def finish(back, x1, x2, value, weight):
    shape = jax.ShapeDtypeStruct(x1.shape, bf16)
    return pl.pallas_call(
        finish_kernel,
        out_shape=(
            shape,
            shape,
            shape,
            jax.ShapeDtypeStruct((ORDER, x1.shape[1]), f32),
        ),
        in_specs=[VMEM] * 5,
        out_specs=tuple([VMEM] * 4),
        compiler_params=pltpu.CompilerParams(vmem_limit_bytes=16 << 20),
        cost_estimate=pl.CostEstimate(flops=4_000_000, bytes_accessed=4_000_000, transcendentals=0),
        name="finish",
    )(back, x1, x2, value, weight)


def per_device(x1, x2, value, out_grad, short_weight, coef, rate):
    peers = lax.axis_size("chan")
    place = lax.axis_index("seq").astype(jnp.int32)[None]
    tables = make_tables(place, rate, coef, short_weight)
    sent = gate(x1, x2, value, out_grad, short_weight)
    got = lax.all_to_all(sent, "seq", split_axis=0, concat_axis=0, tiled=True)
    done = owner_emit(place, got, tables)
    back = lax.all_to_all(done, "seq", split_axis=0, concat_axis=0, tiled=True)
    parts = rate_parts(back, peers)
    parts = lax.all_to_all(parts, "chan", split_axis=0, concat_axis=0, tiled=True)
    y, gx1, gvalue, gcoef = finish(back, x1, x2, value, short_weight)
    grate = jnp.sum(parts[:, :ORDER], axis=0) * (LENGTH * x1.shape[1] * peers) ** -0.5
    return (y, gx1, gvalue, gcoef, grate)


def solution(mesh):
    whole = P("seq", "chan")
    return jax.shard_map(
        per_device,
        mesh=mesh,
        in_specs=(whole, whole, whole, whole, P(None, "chan"), P(None, "chan"), P()),
        out_specs=(whole, whole, whole, P(None, "chan"), P()),
        check_vma=False,
    )
```

```python
import math

import jax
import jax.numpy as jnp
import numpy as np
from jax import lax
from jax.experimental import pallas as pl
from jax.experimental.pallas import tpu as pltpu
from jax.sharding import PartitionSpec as P

f32 = jnp.float32
bf16 = jnp.bfloat16
highest = lax.Precision.HIGHEST
LENGTH = 8192
ROWS = 128
ORDER = 64
LANES = 128
OWN = 8
WORDS = 2 * OWN + 2
BACK = 2 * OWN + 6
NT = (((1,), (1,)), ((), ()))
TN = (((0,), (0,)), ((), ()))

VMEM = pl.BlockSpec(memory_space=pltpu.VMEM)
SMEM = pl.BlockSpec(memory_space=pltpu.SMEM)


def wave_tables():
    index = np.arange(ORDER)
    cycles = (index // 2 + 1) ** 2
    odd = index % 2 == 1

    def turn(power):
        angle = 2.0 * math.pi / LENGTH * (power[:, None] * cycles[None, :] % LENGTH)
        return np.cos(angle), np.sin(angle)

    ahead = np.arange(ROWS)
    cos_a, sin_a = turn(ahead)
    cos_b, sin_b = turn(ROWS - ahead)
    real_b = np.where(odd, sin_b, cos_b)
    imag_b = np.where(odd, -cos_b, sin_b)
    wave = np.where(odd, sin_a, cos_a)
    cos_l, sin_l = turn(np.array([ROWS]))
    twice = [np.concatenate([t, t], axis=1).astype(np.float32) for t in (cos_a, sin_a, real_b, imag_b, wave)]
    step = np.concatenate([np.concatenate([t, t], axis=1) for t in (cos_l, sin_l)], axis=0).astype(np.float32)
    return (*twice, step)


def split(table):
    high = table.astype(bf16)
    low = (table - high.astype(f32)).astype(bf16)
    return jnp.concatenate([high, low], axis=0)


def table_kernel(
    place, rate, coef, weight, cos_a, sin_a, real_b, imag_b, wave, step, tx, tg, mf, me, wd, small
):
    lane = lax.broadcasted_iota(jnp.int32, (ROWS, LANES), 1)
    power = lax.broadcasted_iota(jnp.int32, (ROWS, LANES), 0).astype(f32)
    left = lane < ORDER
    slope = rate[...] * (-1.0 / LENGTH)
    env_a = jnp.exp(slope * power)
    env_b = jnp.exp(slope * (ROWS - power))
    ar = env_a * cos_a[...]
    ai = env_a * sin_a[...]
    br = env_b * real_b[...]
    bi = env_b * imag_b[...]
    back = ROWS - power
    tx[...] = split(
        jnp.concatenate([br, bi, jnp.where(left, 0.0, back * br), jnp.where(left, 0.0, back * bi)], axis=1)
    )
    tg[...] = split(
        jnp.concatenate([ar, ai, jnp.where(left, ar, power * ar), jnp.where(left, ai, power * ai)], axis=1)
    )
    mf[...] = jnp.where(left, ar, ai).astype(bf16)
    me[...] = jnp.where(left, br, bi).astype(bf16)
    w = env_a * wave[...]
    wd[...] = jnp.where(left, w, power * w)
    pick = lax.broadcasted_iota(jnp.int32, (OWN, coef.shape[1]), 1) - place[0] * OWN
    pick = (pick == lax.broadcasted_iota(jnp.int32, (OWN, coef.shape[1]), 0)).astype(f32)
    own = lax.dot_general(
        pick, jnp.concatenate([coef[...], coef[...]], axis=0), NT, precision=highest, preferred_element_type=f32
    )
    scale = own * jnp.sqrt(rate[...] * (2.0 / LENGTH))
    left8 = left[:OWN]
    decay = jnp.exp(slope * ROWS)
    small[0] = scale
    small[1] = lax.dot_general(
        jnp.where(left8, scale, 0.0), w, NT, precision=highest, preferred_element_type=f32
    )
    small[2] = jnp.broadcast_to(decay * step[0:1], (OWN, LANES))
    small[3] = jnp.broadcast_to(decay * step[1:2], (OWN, LANES))
    small[4] = jnp.where(left8, scale * (0.5 / rate[...]), scale * (-1.0 / LENGTH))
    for tap in (1, 2):
        small[5 + tap] = lax.dot_general(
            pick,
            jnp.broadcast_to(weight[tap : tap + 1], (LANES, coef.shape[1])),
            NT,
            precision=highest,
            preferred_element_type=f32,
        )
    small[5] = jnp.broadcast_to(jnp.sqrt(rate[...] * (2.0 / LENGTH)) * LENGTH ** -0.5, (OWN, LANES))


def make_tables(place, rate, coef, weight):
    consts = [jnp.asarray(t) for t in wave_tables()]
    rate2 = jnp.concatenate([rate, rate])[None, :]
    return pl.pallas_call(
        table_kernel,
        out_shape=(
            jax.ShapeDtypeStruct((2 * ROWS, 4 * LANES), bf16),
            jax.ShapeDtypeStruct((2 * ROWS, 4 * LANES), bf16),
            jax.ShapeDtypeStruct((ROWS, LANES), bf16),
            jax.ShapeDtypeStruct((ROWS, LANES), bf16),
            jax.ShapeDtypeStruct((ROWS, LANES), f32),
            jax.ShapeDtypeStruct((8, OWN, LANES), f32),
        ),
        in_specs=[SMEM] + [VMEM] * 9,
        out_specs=tuple([VMEM] * 6),
        compiler_params=pltpu.CompilerParams(vmem_limit_bytes=12 << 20),
        cost_estimate=pl.CostEstimate(flops=4_000_000, bytes_accessed=1_000_000, transcendentals=40_000),
        name="tables",
    )(place, rate2, coef, weight, *consts)


def mix(value, prior, weight):
    row = lax.broadcasted_iota(jnp.int32, value.shape, 0)
    one = jnp.where(row == 0, prior[1:2], pltpu.roll(value, 1, 0))
    two = jnp.where(row == 0, prior[0:1], jnp.where(row == 1, prior[1:2], pltpu.roll(value, 2, 0)))
    return weight[0:1] * value + weight[1:2] * one + weight[2:3] * two


def gate_kernel(x1h, x2h, vh, oh, wh, sent, x1, x2, v, o, w, sems):
    copies = [
        pltpu.make_async_copy(src, dst, sems.at[n])
        for n, (src, dst) in enumerate(((oh, o), (x2h, x2), (vh, v), (wh, w), (x1h, x1)))
    ]
    for copy in copies:
        copy.start()
    copies[0].wait()
    copies[1].wait()
    shards = sent.shape[0]
    grad = o[...].astype(f32) * x2[...].astype(f32)
    grad = grad.T.reshape(shards, OWN, ROWS)
    for copy in copies[2:]:
        copy.wait()
    value = v[...].astype(f32)
    first = x1[...].astype(f32)
    zero = jnp.zeros((2, value.shape[1]), f32)
    gated = (first * mix(value, zero, w[...])).T.reshape(shards, OWN, ROWS)
    flat = sent.reshape(shards, WORDS, ROWS)
    flat[:, : 2 * OWN] = jnp.concatenate([gated, grad], axis=1).astype(bf16)

    per = LANES // OWN
    lane = lax.broadcasted_iota(jnp.int32, (per, LANES), 1)
    row = lax.broadcasted_iota(jnp.int32, (per, LANES), 0)
    group = lax.rem(lane - row * OWN + LANES, LANES) // OWN
    edges = []
    for at in range(0, value.shape[1], LANES):
        tile = jnp.zeros((per, LANES), f32)
        for n, (source, where) in enumerate(((first, 0), (first, 1), (value, ROWS - 2), (value, ROWS - 1))):
            line = source[where : where + 1, at : at + LANES]
            line = pltpu.roll(line, n * OWN, 1) if n else line
            tile = jnp.where(group == n, line, tile)
        edges.append(tile)
    edges = jnp.concatenate(edges, axis=0)
    flat[:, 2 * OWN :] = jnp.broadcast_to(edges[:, None, :], (shards, 2, LANES)).astype(bf16)


def gate(x1, x2, value, out_grad, weight):
    shards = x1.shape[1] // OWN
    return pl.pallas_call(
        gate_kernel,
        out_shape=jax.ShapeDtypeStruct((shards, WORDS // 2, 2, ROWS), bf16),
        in_specs=[pl.BlockSpec(memory_space=pltpu.HBM)] * 5,
        out_specs=VMEM,
        scratch_shapes=[pltpu.VMEM(x1.shape, bf16)] * 4
        + [pltpu.VMEM(weight.shape, f32), pltpu.SemaphoreType.DMA((5,))],
        compiler_params=pltpu.CompilerParams(vmem_limit_bytes=(64 << 20) - (64 << 10)),
        name="gate",
    )(x1, x2, value, out_grad, weight)


def owner_kernel(
    place, got, tx, tg, wd, small, part_out, coef_out, us, ug, xb_out, head_out, gs, rs, ex, eg, sr, si, gr, gi
):
    chunks = got.shape[0]
    rows = chunks * OWN
    flat = got.reshape(chunks, WORDS, ROWS)
    both = flat[:, : 2 * OWN].astype(f32)
    edge = flat[:, 2 * OWN :].astype(f32)[:, :1]
    edge = jnp.broadcast_to(edge, (chunks, OWN, LANES)).reshape(rows, LANES)
    edge = pltpu.roll(edge, lax.rem(ORDER * LANES - place[0] * OWN, LANES), 1)
    lane3 = lax.broadcasted_iota(jnp.int32, (rows, LANES), 1)
    row3 = lax.broadcasted_iota(jnp.int32, (rows, LANES), 0)
    edge = jnp.where(lane3 % OWN == row3 % OWN, edge, 0.0).astype(bf16)
    group = lax.broadcasted_iota(jnp.int32, (LANES, LANES), 0) // OWN
    to = lax.broadcasted_iota(jnp.int32, (LANES, LANES), 1)
    spot_x1 = ((group < 2) & (to % ORDER == group)).astype(bf16)
    spot_v = (((group == 2) & (to == 0)) | ((group == 3) & (to == 1))).astype(bf16)
    spot_last = ((group == 3) & (to == 0)).astype(bf16)
    spread = jnp.dot(
        edge, jnp.concatenate([spot_x1, spot_v, spot_last], axis=1), preferred_element_type=f32
    )
    x1_head = spread[:, :LANES]
    before = (
        small[7] * spread[:, LANES : 2 * LANES].reshape(chunks, OWN, LANES)
        + small[6] * spread[:, 2 * LANES :].reshape(chunks, OWN, LANES)
    )
    before = jnp.concatenate([jnp.zeros((1, OWN, LANES), f32), before[:-1]], axis=0)
    x = both[:, :OWN].reshape(rows, ROWS) + x1_head * before.reshape(rows, LANES)
    g = both[:, OWN:].reshape(rows, ROWS)
    gs[...] = g
    xb = x.astype(bf16)
    xb_out[...] = xb
    head_out[...] = jnp.where(lane3 < ORDER, spread[:, LANES : 2 * LANES], x1_head)
    gb = g.astype(bf16)
    here = lax.broadcasted_iota(jnp.int32, (ROWS, ROWS), 0)
    there = lax.broadcasted_iota(jnp.int32, (ROWS, ROWS), 1)
    mirror = (here + there == ROWS - 1).astype(bf16)
    rs[...] = jnp.dot(xb, mirror, preferred_element_type=f32)
    ex[...] = jnp.dot(
        jnp.concatenate([xb, xb], axis=1), tx[...], preferred_element_type=f32
    )
    eg[...] = jnp.dot(
        jnp.concatenate([gb, gb], axis=1), tg[...], preferred_element_type=f32
    )
    scale = small[0]
    lr = small[2]
    li = small[3]

    a = b = c = d = jnp.zeros((OWN, LANES), f32)
    for k in range(chunks):
        at = pl.ds(k * OWN, OWN)
        sr[at] = a
        si[at] = b
        a, b = (
            lr * a - li * b + ex[at, 0:LANES],
            lr * b + li * a + ex[at, LANES : 2 * LANES],
        )
        at = pl.ds((chunks - 1 - k) * OWN, OWN)
        gr[at] = c
        gi[at] = d
        c, d = (
            lr * c - li * d + eg[at, 0:LANES],
            lr * d + li * c + eg[at, LANES : 2 * LANES],
        )

    left = lax.broadcasted_iota(jnp.int32, (OWN, LANES), 1) < ORDER

    def cube(array):
        return array.reshape(chunks, OWN, LANES)

    s_r, s_i, g_r, g_i = (cube(ref[...]) for ref in (sr, si, gr, gi))
    over = jnp.where(left, 0.0, float(ROWS))
    ahead_r = over * lr * g_r - over * li * g_i
    ahead_i = over * lr * g_i + over * li * g_r
    total = (
        s_r * (cube(eg[:, 2 * LANES : 3 * LANES]) + ahead_r)
        - s_i * (cube(eg[:, 3 * LANES : 4 * LANES]) + ahead_i)
        + g_r * cube(ex[:, 2 * LANES : 3 * LANES])
        - g_i * cube(ex[:, 3 * LANES : 4 * LANES])
    )
    total = jnp.sum(total, axis=0)
    us[...] = jnp.where(left, scale * s_r, -scale * s_i).reshape(rows, LANES).astype(bf16)
    ug[...] = jnp.where(left, scale * g_r, -scale * g_i).reshape(rows, LANES).astype(bf16)

    inside = (there < here) | (there == ROWS - 1)
    lags = []
    for ch in range(OWN):
        at = pl.ds(ch, chunks, stride=OWN)
        pairs = lax.dot_general(
            rs[at, :].astype(bf16), gs[at, :].astype(bf16), TN, preferred_element_type=f32
        )
        pairs = pltpu.roll(pairs, 0, 1, stride=1, stride_axis=0)
        lags.append(jnp.sum(jnp.where(inside, pairs, 0.0), axis=0, keepdims=True))
    lags = pltpu.roll(jnp.concatenate(lags, axis=0), 1, 1)
    total = total + jnp.dot(lags, wd[...], precision=highest, preferred_element_type=f32)
    coef_out[...] = total * small[5]
    part = jnp.sum(total * small[4], axis=0, keepdims=True)
    part_out[...] = jnp.broadcast_to(part + pltpu.roll(part, ORDER, 1), part_out.shape)


def emit_kernel(got, parts, coef, us, ug, xb, head, mf, me, small, out, xs, gs, yc, yg):
    chunks = got.shape[0]
    rows = chunks * OWN

    def cube(array):
        return array.reshape(chunks, OWN, LANES)

    xs[...] = xb[...].astype(f32)
    gs[...] = got.reshape(chunks, WORDS, ROWS)[:, : 2 * OWN].astype(f32)[:, OWN:].reshape(rows, ROWS)
    yc[...] = lax.dot_general(us[...], mf[...], NT, preferred_element_type=f32)
    yg[...] = lax.dot_general(ug[...], me[...], NT, preferred_element_type=f32)
    here = lax.broadcasted_iota(jnp.int32, (ROWS, ROWS), 0)
    there = lax.broadcasted_iota(jnp.int32, (ROWS, ROWS), 1)
    later = there >= here
    filt = small[1]
    for ch in range(OWN):
        at = pl.ds(ch, chunks, stride=OWN)
        toeplitz = pltpu.roll(
            jnp.broadcast_to(filt[ch : ch + 1], (ROWS, ROWS)), 0, 1, stride=1, stride_axis=0
        )
        toeplitz = jnp.where(later, toeplitz, 0.0).astype(bf16)
        yc[at, :] += jnp.dot(xs[at, :].astype(bf16), toeplitz, preferred_element_type=f32)
        yg[at, :] += lax.dot_general(gs[at, :].astype(bf16), toeplitz, NT, preferred_element_type=f32)

    flat = out.reshape(chunks, BACK, ROWS)
    flat[:, : 2 * OWN] = jnp.concatenate([cube(yc[...]), cube(yg[...])], axis=1).astype(bf16)
    lane = lax.broadcasted_iota(jnp.int32, (OWN, LANES), 1)
    row = lax.broadcasted_iota(jnp.int32, (OWN, LANES), 0)
    both = jnp.where(lane < ORDER, coef[...], pltpu.roll(pltpu.roll(coef[...], ORDER, 1), OWN // 2, 0))
    flat[:, 2 * OWN : 2 * OWN + 4] = jnp.broadcast_to(both[: OWN // 2], (chunks, OWN // 2, LANES)).astype(bf16)
    lane2 = lax.broadcasted_iota(jnp.int32, (rows, LANES), 1)
    ends = jnp.where(lane2 < ORDER, head[...], pltpu.roll(yg[...], ORDER, 1) * head[...]).astype(bf16)
    ends = cube(jnp.dot(ends, end_spots(False), preferred_element_type=f32))
    ends = jnp.sum(jnp.where(lane % ORDER // 2 == row, ends, 0.0), axis=1, keepdims=True)
    none = jnp.zeros((1, 1, LANES), f32)
    part = jnp.sum(parts[...], axis=0, keepdims=True)
    low = part - part.astype(bf16).astype(f32)
    left = lane[:1] < ORDER
    high = jnp.where(left, part, jnp.concatenate([ends[1:], none], axis=0))
    ends = pltpu.roll(jnp.concatenate([none, ends[:-1]], axis=0), ORDER, 2)
    low = jnp.where(left, low, ends)
    flat[:, 2 * OWN + 4 :] = jnp.concatenate([high, low], axis=1).astype(bf16)


def end_spots(turned):
    few = lax.broadcasted_iota(jnp.int32, (LANES, LANES), 1 if turned else 0)
    many = lax.broadcasted_iota(jnp.int32, (LANES, LANES), 0 if turned else 1)
    hit = (many % ORDER < 2 * OWN) & (few % 2 == many % 2)
    if turned:
        hit &= few // 2 == jnp.where(many < ORDER, ORDER // 2 + 1, ORDER // 2)
    else:
        hit &= few // 2 == many // ORDER * (ORDER // 2)
    return hit.astype(bf16)


def owner_emit_kernel(
    place, got, tx, tg, mf, me, wd, small, out, part, coef, us, ug, xb, head, gs, rs, ex, eg, sr, si, gr, gi, xs, yc, yg
):
    owner_kernel(place, got, tx, tg, wd, small, part, coef, us, ug, xb, head, gs, rs, ex, eg, sr, si, gr, gi)
    emit_kernel(got, part, coef, us, ug, xb, head, mf, me, small, out, xs, gs, yc, yg)


def owner_emit(place, got, tables):
    chunks = got.shape[0]
    rows = chunks * OWN
    wide = pltpu.VMEM((rows, LANES), f32)
    flat = pltpu.VMEM((rows, LANES), bf16)
    tall = pltpu.VMEM((rows, 4 * LANES), f32)
    return pl.pallas_call(
        owner_emit_kernel,
        out_shape=jax.ShapeDtypeStruct((chunks, BACK // 2, 2, ROWS), bf16),
        in_specs=[SMEM] + [VMEM] * 7,
        out_specs=VMEM,
        scratch_shapes=[pltpu.VMEM((1, LANES), f32), pltpu.VMEM((OWN, LANES), f32)]
        + [flat] * 3
        + [wide] * 3
        + [tall] * 2
        + [wide] * 7,
        compiler_params=pltpu.CompilerParams(vmem_limit_bytes=24 << 20),
        name="owner",
    )(place, got, *tables)


def rate_kernel(back, parts):
    flat = back.reshape(back.shape[0], BACK, ROWS)
    rates = jnp.sum(jnp.sum(flat[:, 2 * OWN + 4 :].astype(f32), axis=0), axis=0, keepdims=True)
    scale = (LENGTH * back.shape[0] * OWN * parts.shape[0]) ** -0.5
    parts[...] = jnp.broadcast_to(rates * scale, parts.shape)


def rate_parts(back, peers):
    return pl.pallas_call(
        rate_kernel,
        out_shape=jax.ShapeDtypeStruct((peers, LANES), f32),
        in_specs=[VMEM],
        out_specs=VMEM,
        compiler_params=pltpu.CompilerParams(vmem_limit_bytes=8 << 20),
        name="rates",
    )(back)


def finish_kernel(back, x1, x2, value, weight, y, gx1, gvalue, gcoef):
    shards = back.shape[0]
    wide = shards * OWN
    every = back.reshape(shards, BACK, ROWS)
    both = every[:, : 2 * OWN].astype(f32)
    conv = both[:, :OWN].reshape(wide, ROWS).T
    grad = both[:, OWN:].reshape(wide, ROWS).T
    both = every[:, 2 * OWN : 2 * OWN + 4].astype(f32)
    both = jnp.concatenate([both, pltpu.roll(both, ORDER, 2)], axis=1).reshape(wide, LANES)
    rest = every[:, 2 * OWN + 4 :].astype(f32)
    lane = lax.broadcasted_iota(jnp.int32, (shards, OWN, LANES), 2)
    row = lax.broadcasted_iota(jnp.int32, (shards, OWN, LANES), 1)
    ends = jnp.where(lane[:, :1] < ORDER, pltpu.roll(rest[:, 1:], ORDER, 2), rest[:, :1])
    ends = jnp.where(lane % ORDER // 2 == row, jnp.broadcast_to(ends, lane.shape), 0.0)
    ends = jnp.dot(ends.reshape(wide, LANES).astype(bf16), end_spots(True), preferred_element_type=f32)
    lane = lax.broadcasted_iota(jnp.int32, (wide, LANES), 1)
    turned = jnp.where(lane < ORDER, both, ends).T
    gcoef[...] = turned[:ORDER]
    first = x1[...].astype(f32)
    w = weight[...]
    y[...] = (x2[...].astype(f32) * conv).astype(bf16)
    mixed = mix(value[...].astype(f32), turned[ORDER + 2 : ORDER + 4], w)
    gx1[...] = (grad * mixed).astype(bf16)
    grad_mixed = grad * first
    after = turned[ORDER : ORDER + 2]
    row = lax.broadcasted_iota(jnp.int32, grad_mixed.shape, 0)
    one = jnp.where(row == ROWS - 1, after[0:1], pltpu.roll(grad_mixed, ROWS - 1, 0))
    two = jnp.where(
        row == ROWS - 2,
        after[0:1],
        jnp.where(row == ROWS - 1, after[1:2], pltpu.roll(grad_mixed, ROWS - 2, 0)),
    )
    gvalue[...] = (w[0:1] * grad_mixed + w[1:2] * one + w[2:3] * two).astype(bf16)


def finish(back, x1, x2, value, weight):
    shape = jax.ShapeDtypeStruct(x1.shape, bf16)
    return pl.pallas_call(
        finish_kernel,
        out_shape=(
            shape,
            shape,
            shape,
            jax.ShapeDtypeStruct((ORDER, x1.shape[1]), f32),
        ),
        in_specs=[VMEM] * 5,
        out_specs=tuple([VMEM] * 4),
        compiler_params=pltpu.CompilerParams(vmem_limit_bytes=16 << 20),
        cost_estimate=pl.CostEstimate(flops=4_000_000, bytes_accessed=4_000_000, transcendentals=0),
        name="finish",
    )(back, x1, x2, value, weight)


def per_device(x1, x2, value, out_grad, short_weight, coef, rate):
    peers = lax.axis_size("chan")
    place = lax.axis_index("seq").astype(jnp.int32)[None]
    tables = make_tables(place, rate, coef, short_weight)
    sent = gate(x1, x2, value, out_grad, short_weight)
    got = lax.all_to_all(sent, "seq", split_axis=0, concat_axis=0, tiled=True)
    done = owner_emit(place, got, tables)
    back = lax.all_to_all(done, "seq", split_axis=0, concat_axis=0, tiled=True)
    parts = rate_parts(back, peers)
    parts = lax.all_to_all(parts, "chan", split_axis=0, concat_axis=0, tiled=True)
    y, gx1, gvalue, gcoef = finish(back, x1, x2, value, short_weight)
    grate = jnp.sum(parts[:, :ORDER], axis=0)
    return (y, gx1, gvalue, gcoef, grate)


def solution(mesh):
    whole = P("seq", "chan")
    return jax.shard_map(
        per_device,
        mesh=mesh,
        in_specs=(whole, whole, whole, whole, P(None, "chan"), P(None, "chan"), P()),
        out_specs=(whole, whole, whole, P(None, "chan"), P()),
        check_vma=False,
    )
```

```python
import math

import jax
import jax.numpy as jnp
import numpy as np
from jax import lax
from jax.experimental import pallas as pl
from jax.experimental.pallas import tpu as pltpu
from jax.sharding import PartitionSpec as P

f32 = jnp.float32
bf16 = jnp.bfloat16
highest = lax.Precision.HIGHEST
LENGTH = 8192
ROWS = 128
ORDER = 64
LANES = 128
OWN = 8
WORDS = 2 * OWN + 2
BACK = 2 * OWN + 6
NT = (((1,), (1,)), ((), ()))
TN = (((0,), (0,)), ((), ()))

VMEM = pl.BlockSpec(memory_space=pltpu.VMEM)
SMEM = pl.BlockSpec(memory_space=pltpu.SMEM)


def wave_tables():
    index = np.arange(ORDER)
    cycles = (index // 2 + 1) ** 2
    odd = index % 2 == 1

    def turn(power):
        angle = 2.0 * math.pi / LENGTH * (power[:, None] * cycles[None, :] % LENGTH)
        return np.cos(angle), np.sin(angle)

    ahead = np.arange(ROWS)
    cos_a, sin_a = turn(ahead)
    cos_b, sin_b = turn(ROWS - ahead)
    real_b = np.where(odd, sin_b, cos_b)
    imag_b = np.where(odd, -cos_b, sin_b)
    wave = np.where(odd, sin_a, cos_a)
    cos_l, sin_l = turn(np.array([ROWS]))
    twice = [np.concatenate([t, t], axis=1).astype(np.float32) for t in (cos_a, sin_a, real_b, imag_b, wave)]
    step = np.concatenate([np.concatenate([t, t], axis=1) for t in (cos_l, sin_l)], axis=0).astype(np.float32)
    return (*twice, step)


def split(table):
    high = table.astype(bf16)
    low = (table - high.astype(f32)).astype(bf16)
    return jnp.concatenate([high, low], axis=0)


def table_kernel(
    place, rate, coef, weight, cos_a, sin_a, real_b, imag_b, wave, step, tx, tg, mf, me, wd, small
):
    lane = lax.broadcasted_iota(jnp.int32, (ROWS, LANES), 1)
    power = lax.broadcasted_iota(jnp.int32, (ROWS, LANES), 0).astype(f32)
    left = lane < ORDER
    slope = rate[...] * (-1.0 / LENGTH)
    env_a = jnp.exp(slope * power)
    env_b = jnp.exp(slope * (ROWS - power))
    ar = env_a * cos_a[...]
    ai = env_a * sin_a[...]
    br = env_b * real_b[...]
    bi = env_b * imag_b[...]
    back = ROWS - power
    tx[...] = split(
        jnp.concatenate([br, bi, jnp.where(left, 0.0, back * br), jnp.where(left, 0.0, back * bi)], axis=1)
    )
    tg[...] = split(
        jnp.concatenate([ar, ai, jnp.where(left, ar, power * ar), jnp.where(left, ai, power * ai)], axis=1)
    )
    mf[...] = jnp.where(left, ar, ai).astype(bf16)
    me[...] = jnp.where(left, br, bi).astype(bf16)
    w = env_a * wave[...]
    wd[...] = jnp.where(left, w, power * w)
    pick = lax.broadcasted_iota(jnp.int32, (OWN, coef.shape[1]), 1) - place[0] * OWN
    pick = (pick == lax.broadcasted_iota(jnp.int32, (OWN, coef.shape[1]), 0)).astype(f32)
    own = lax.dot_general(
        pick, jnp.concatenate([coef[...], coef[...]], axis=0), NT, precision=highest, preferred_element_type=f32
    )
    scale = own * jnp.sqrt(rate[...] * (2.0 / LENGTH))
    left8 = left[:OWN]
    decay = jnp.exp(slope * ROWS)
    small[0] = scale
    small[1] = lax.dot_general(
        jnp.where(left8, scale, 0.0), w, NT, precision=highest, preferred_element_type=f32
    )
    small[2] = jnp.broadcast_to(decay * step[0:1], (OWN, LANES))
    small[3] = jnp.broadcast_to(decay * step[1:2], (OWN, LANES))
    small[4] = jnp.where(left8, scale * (0.5 / rate[...]), scale * (-1.0 / LENGTH))
    for tap in (1, 2):
        small[5 + tap] = lax.dot_general(
            pick,
            jnp.broadcast_to(weight[tap : tap + 1], (LANES, coef.shape[1])),
            NT,
            precision=highest,
            preferred_element_type=f32,
        )
    small[5] = jnp.broadcast_to(jnp.sqrt(rate[...] * (2.0 / LENGTH)) * LENGTH ** -0.5, (OWN, LANES))


def make_tables(place, rate, coef, weight):
    consts = [jnp.asarray(t) for t in wave_tables()]
    rate2 = jnp.concatenate([rate, rate])[None, :]
    return pl.pallas_call(
        table_kernel,
        out_shape=(
            jax.ShapeDtypeStruct((2 * ROWS, 4 * LANES), bf16),
            jax.ShapeDtypeStruct((2 * ROWS, 4 * LANES), bf16),
            jax.ShapeDtypeStruct((ROWS, LANES), bf16),
            jax.ShapeDtypeStruct((ROWS, LANES), bf16),
            jax.ShapeDtypeStruct((ROWS, LANES), f32),
            jax.ShapeDtypeStruct((8, OWN, LANES), f32),
        ),
        in_specs=[SMEM] + [VMEM] * 9,
        out_specs=tuple([VMEM] * 6),
        compiler_params=pltpu.CompilerParams(vmem_limit_bytes=12 << 20),
        cost_estimate=pl.CostEstimate(flops=4_000_000, bytes_accessed=1_000_000, transcendentals=40_000),
        name="tables",
    )(place, rate2, coef, weight, *consts)


def mix(value, prior, weight):
    row = lax.broadcasted_iota(jnp.int32, value.shape, 0)
    one = jnp.where(row == 0, prior[1:2], pltpu.roll(value, 1, 0))
    two = jnp.where(row == 0, prior[0:1], jnp.where(row == 1, prior[1:2], pltpu.roll(value, 2, 0)))
    return weight[0:1] * value + weight[1:2] * one + weight[2:3] * two


def gate_kernel(x1h, x2h, vh, oh, wh, sent, x1, x2, v, o, w, sems):
    copies = [
        pltpu.make_async_copy(src, dst, sems.at[n])
        for n, (src, dst) in enumerate(((oh, o), (x2h, x2), (vh, v), (wh, w), (x1h, x1)))
    ]
    for copy in copies:
        copy.start()
    copies[0].wait()
    copies[1].wait()
    shards = sent.shape[0]
    grad = o[...].astype(f32) * x2[...].astype(f32)
    grad = grad.T.reshape(shards, OWN, ROWS)
    for copy in copies[2:]:
        copy.wait()
    value = v[...].astype(f32)
    first = x1[...].astype(f32)
    zero = jnp.zeros((2, value.shape[1]), f32)
    gated = (first * mix(value, zero, w[...])).T.reshape(shards, OWN, ROWS)
    flat = sent.reshape(shards, WORDS, ROWS)
    flat[:, : 2 * OWN] = jnp.concatenate([gated, grad], axis=1).astype(bf16)

    per = LANES // OWN
    lane = lax.broadcasted_iota(jnp.int32, (per, LANES), 1)
    row = lax.broadcasted_iota(jnp.int32, (per, LANES), 0)
    group = lax.rem(lane - row * OWN + LANES, LANES) // OWN
    edges = []
    for at in range(0, value.shape[1], LANES):
        tile = jnp.zeros((per, LANES), f32)
        for n, (source, where) in enumerate(((first, 0), (first, 1), (value, ROWS - 2), (value, ROWS - 1))):
            line = source[where : where + 1, at : at + LANES]
            line = pltpu.roll(line, n * OWN, 1) if n else line
            tile = jnp.where(group == n, line, tile)
        edges.append(tile)
    edges = jnp.concatenate(edges, axis=0)
    flat[:, 2 * OWN :] = jnp.broadcast_to(edges[:, None, :], (shards, 2, LANES)).astype(bf16)


def gate(x1, x2, value, out_grad, weight):
    shards = x1.shape[1] // OWN
    return pl.pallas_call(
        gate_kernel,
        out_shape=jax.ShapeDtypeStruct((shards, WORDS // 2, 2, ROWS), bf16),
        in_specs=[pl.BlockSpec(memory_space=pltpu.HBM)] * 5,
        out_specs=VMEM,
        scratch_shapes=[pltpu.VMEM(x1.shape, bf16)] * 4
        + [pltpu.VMEM(weight.shape, f32), pltpu.SemaphoreType.DMA((5,))],
        compiler_params=pltpu.CompilerParams(vmem_limit_bytes=(64 << 20) - (64 << 10)),
        name="gate",
    )(x1, x2, value, out_grad, weight)


def owner_kernel(
    place, got, tx, tg, wd, small, part_out, coef_out, us, ug, xb_out, head_out, gs, rs, ex, eg, sr, si, gr, gi
):
    chunks = got.shape[0]
    rows = chunks * OWN
    flat = got.reshape(chunks, WORDS, ROWS)
    both = flat[:, : 2 * OWN].astype(f32)
    edge = flat[:, 2 * OWN :].astype(f32)[:, :1]
    edge = jnp.broadcast_to(edge, (chunks, OWN, LANES)).reshape(rows, LANES)
    edge = pltpu.roll(edge, lax.rem(ORDER * LANES - place[0] * OWN, LANES), 1)
    lane3 = lax.broadcasted_iota(jnp.int32, (rows, LANES), 1)
    row3 = lax.broadcasted_iota(jnp.int32, (rows, LANES), 0)
    edge = jnp.where(lane3 % OWN == row3 % OWN, edge, 0.0).astype(bf16)
    group = lax.broadcasted_iota(jnp.int32, (LANES, LANES), 0) // OWN
    to = lax.broadcasted_iota(jnp.int32, (LANES, LANES), 1)
    spot_x1 = ((group < 2) & (to % ORDER == group)).astype(bf16)
    spot_v = (((group == 2) & (to == 0)) | ((group == 3) & (to == 1))).astype(bf16)
    spot_last = ((group == 3) & (to == 0)).astype(bf16)
    spread = jnp.dot(
        edge, jnp.concatenate([spot_x1, spot_v, spot_last], axis=1), preferred_element_type=f32
    )
    x1_head = spread[:, :LANES]
    before = (
        small[7] * spread[:, LANES : 2 * LANES].reshape(chunks, OWN, LANES)
        + small[6] * spread[:, 2 * LANES :].reshape(chunks, OWN, LANES)
    )
    before = jnp.concatenate([jnp.zeros((1, OWN, LANES), f32), before[:-1]], axis=0)
    x = both[:, :OWN].reshape(rows, ROWS) + x1_head * before.reshape(rows, LANES)
    g = both[:, OWN:].reshape(rows, ROWS)
    gs[...] = g
    xb = x.astype(bf16)
    xb_out[...] = xb
    head_out[...] = jnp.where(lane3 < ORDER, spread[:, LANES : 2 * LANES], x1_head)
    gb = g.astype(bf16)
    here = lax.broadcasted_iota(jnp.int32, (ROWS, ROWS), 0)
    there = lax.broadcasted_iota(jnp.int32, (ROWS, ROWS), 1)
    mirror = (here + there == ROWS - 1).astype(bf16)
    rs[...] = jnp.dot(xb, mirror, preferred_element_type=f32)
    ex[...] = jnp.dot(
        jnp.concatenate([xb, xb], axis=1), tx[...], preferred_element_type=f32
    )
    eg[...] = jnp.dot(
        jnp.concatenate([gb, gb], axis=1), tg[...], preferred_element_type=f32
    )
    scale = small[0]
    lr = small[2]
    li = small[3]

    a = b = c = d = jnp.zeros((OWN, LANES), f32)
    for k in range(chunks):
        at = pl.ds(k * OWN, OWN)
        sr[at] = a
        si[at] = b
        a, b = (
            lr * a - li * b + ex[at, 0:LANES],
            lr * b + li * a + ex[at, LANES : 2 * LANES],
        )
        at = pl.ds((chunks - 1 - k) * OWN, OWN)
        gr[at] = c
        gi[at] = d
        c, d = (
            lr * c - li * d + eg[at, 0:LANES],
            lr * d + li * c + eg[at, LANES : 2 * LANES],
        )

    left = lax.broadcasted_iota(jnp.int32, (OWN, LANES), 1) < ORDER

    def cube(array):
        return array.reshape(chunks, OWN, LANES)

    s_r, s_i, g_r, g_i = (cube(ref[...]) for ref in (sr, si, gr, gi))
    over = jnp.where(left, 0.0, float(ROWS))
    ahead_r = over * lr * g_r - over * li * g_i
    ahead_i = over * lr * g_i + over * li * g_r
    total = (
        s_r * (cube(eg[:, 2 * LANES : 3 * LANES]) + ahead_r)
        - s_i * (cube(eg[:, 3 * LANES : 4 * LANES]) + ahead_i)
        + g_r * cube(ex[:, 2 * LANES : 3 * LANES])
        - g_i * cube(ex[:, 3 * LANES : 4 * LANES])
    )
    total = jnp.sum(total, axis=0)
    us[...] = jnp.where(left, scale * s_r, -scale * s_i).reshape(rows, LANES).astype(bf16)
    ug[...] = jnp.where(left, scale * g_r, -scale * g_i).reshape(rows, LANES).astype(bf16)

    inside = (there < here) | (there == ROWS - 1)
    lags = []
    for ch in range(OWN):
        at = pl.ds(ch, chunks, stride=OWN)
        pairs = lax.dot_general(
            rs[at, :].astype(bf16), gs[at, :].astype(bf16), TN, preferred_element_type=f32
        )
        pairs = pltpu.roll(pairs, 0, 1, stride=1, stride_axis=0)
        lags.append(jnp.sum(jnp.where(inside, pairs, 0.0), axis=0, keepdims=True))
    lags = pltpu.roll(jnp.concatenate(lags, axis=0), 1, 1)
    total = total + jnp.dot(lags, wd[...], precision=highest, preferred_element_type=f32)
    coef_out[...] = total * small[5]
    part = jnp.sum(total * small[4], axis=0, keepdims=True)
    part_out[...] = jnp.broadcast_to(part + pltpu.roll(part, ORDER, 1), part_out.shape)


def emit_kernel(got, parts, coef, us, ug, xb, head, mf, me, small, out, xs, gs, yc, yg):
    chunks = got.shape[0]
    rows = chunks * OWN

    def cube(array):
        return array.reshape(chunks, OWN, LANES)

    xs[...] = xb[...].astype(f32)
    gs[...] = got.reshape(chunks, WORDS, ROWS)[:, : 2 * OWN].astype(f32)[:, OWN:].reshape(rows, ROWS)
    yc[...] = lax.dot_general(us[...], mf[...], NT, preferred_element_type=f32)
    yg[...] = lax.dot_general(ug[...], me[...], NT, preferred_element_type=f32)
    here = lax.broadcasted_iota(jnp.int32, (ROWS, ROWS), 0)
    there = lax.broadcasted_iota(jnp.int32, (ROWS, ROWS), 1)
    later = there >= here
    filt = small[1]
    for ch in range(OWN):
        at = pl.ds(ch, chunks, stride=OWN)
        toeplitz = pltpu.roll(
            jnp.broadcast_to(filt[ch : ch + 1], (ROWS, ROWS)), 0, 1, stride=1, stride_axis=0
        )
        toeplitz = jnp.where(later, toeplitz, 0.0).astype(bf16)
        yc[at, :] += jnp.dot(xs[at, :].astype(bf16), toeplitz, preferred_element_type=f32)
        yg[at, :] += lax.dot_general(gs[at, :].astype(bf16), toeplitz, NT, preferred_element_type=f32)

    flat = out.reshape(chunks, BACK, ROWS)
    flat[:, : 2 * OWN] = jnp.concatenate([cube(yc[...]), cube(yg[...])], axis=1).astype(bf16)
    lane = lax.broadcasted_iota(jnp.int32, (OWN, LANES), 1)
    row = lax.broadcasted_iota(jnp.int32, (OWN, LANES), 0)
    both = jnp.where(lane < ORDER, coef[...], pltpu.roll(pltpu.roll(coef[...], ORDER, 1), OWN // 2, 0))
    flat[:, 2 * OWN : 2 * OWN + 4] = jnp.broadcast_to(both[: OWN // 2], (chunks, OWN // 2, LANES)).astype(bf16)
    lane2 = lax.broadcasted_iota(jnp.int32, (rows, LANES), 1)
    ends = jnp.where(lane2 < ORDER, head[...], pltpu.roll(yg[...], ORDER, 1) * head[...]).astype(bf16)
    ends = cube(jnp.dot(ends, end_spots(False), preferred_element_type=f32))
    ends = jnp.sum(jnp.where(lane % ORDER // 2 == row, ends, 0.0), axis=1, keepdims=True)
    none = jnp.zeros((1, 1, LANES), f32)
    part = jnp.sum(parts[...], axis=0, keepdims=True)
    low = part - part.astype(bf16).astype(f32)
    left = lane[:1] < ORDER
    high = jnp.where(left, part, jnp.concatenate([ends[1:], none], axis=0))
    ends = pltpu.roll(jnp.concatenate([none, ends[:-1]], axis=0), ORDER, 2)
    low = jnp.where(left, low, ends)
    flat[:, 2 * OWN + 4 :] = jnp.concatenate([high, low], axis=1).astype(bf16)


def end_spots(turned):
    few = lax.broadcasted_iota(jnp.int32, (LANES, LANES), 1 if turned else 0)
    many = lax.broadcasted_iota(jnp.int32, (LANES, LANES), 0 if turned else 1)
    hit = (many % ORDER < 2 * OWN) & (few % 2 == many % 2)
    if turned:
        hit &= few // 2 == jnp.where(many < ORDER, ORDER // 2 + 1, ORDER // 2)
    else:
        hit &= few // 2 == many // ORDER * (ORDER // 2)
    return hit.astype(bf16)


def owner_emit_kernel(
    place, got, tx, tg, mf, me, wd, small, out, part, coef, us, ug, xb, head, gs, rs, ex, eg, sr, si, gr, gi, xs, yc, yg
):
    owner_kernel(place, got, tx, tg, wd, small, part, coef, us, ug, xb, head, gs, rs, ex, eg, sr, si, gr, gi)
    emit_kernel(got, part, coef, us, ug, xb, head, mf, me, small, out, xs, gs, yc, yg)


def owner_emit(place, got, tables):
    chunks = got.shape[0]
    rows = chunks * OWN
    wide = pltpu.VMEM((rows, LANES), f32)
    flat = pltpu.VMEM((rows, LANES), bf16)
    tall = pltpu.VMEM((rows, 4 * LANES), f32)
    return pl.pallas_call(
        owner_emit_kernel,
        out_shape=jax.ShapeDtypeStruct((chunks, BACK // 2, 2, ROWS), bf16),
        in_specs=[SMEM] + [VMEM] * 7,
        out_specs=VMEM,
        scratch_shapes=[pltpu.VMEM((1, LANES), f32), pltpu.VMEM((OWN, LANES), f32)]
        + [flat] * 3
        + [wide] * 3
        + [tall] * 2
        + [wide] * 7,
        compiler_params=pltpu.CompilerParams(vmem_limit_bytes=24 << 20),
        name="owner",
    )(place, got, *tables)


def rate_kernel(back, early, parts):
    flat = back.reshape(back.shape[0], BACK, ROWS)
    rates = jnp.sum(jnp.sum(flat[:, 2 * OWN + 4 :].astype(f32), axis=0), axis=0, keepdims=True)
    parts[...] = jnp.broadcast_to(rates, parts.shape)


def rate_parts(back, early, peers):
    return pl.pallas_call(
        rate_kernel,
        out_shape=jax.ShapeDtypeStruct((peers, LANES), f32),
        in_specs=[VMEM, pl.BlockSpec(memory_space=pl.ANY)],
        out_specs=VMEM,
        compiler_params=pltpu.CompilerParams(vmem_limit_bytes=8 << 20),
        name="rates",
    )(back, early)


def mix_kernel(value, weight, early):
    early[...] = mix(value[...].astype(f32), jnp.zeros((2, value.shape[1]), f32), weight[...])


def mix_early(value, weight):
    return pl.pallas_call(
        mix_kernel,
        out_shape=jax.ShapeDtypeStruct(value.shape, f32),
        in_specs=[VMEM] * 2,
        out_specs=VMEM,
        compiler_params=pltpu.CompilerParams(vmem_limit_bytes=12 << 20),
        cost_estimate=pl.CostEstimate(flops=1_000_000, bytes_accessed=2_000_000, transcendentals=0),
        name="mix",
    )(value, weight)


def finish_kernel(back, x1, x2, early, weight, y, gx1, gvalue, gcoef):
    shards = back.shape[0]
    wide = shards * OWN
    every = back.reshape(shards, BACK, ROWS)
    both = every[:, : 2 * OWN].astype(f32)
    conv = both[:, :OWN].reshape(wide, ROWS).T
    grad = both[:, OWN:].reshape(wide, ROWS).T
    both = every[:, 2 * OWN : 2 * OWN + 4].astype(f32)
    both = jnp.concatenate([both, pltpu.roll(both, ORDER, 2)], axis=1).reshape(wide, LANES)
    rest = every[:, 2 * OWN + 4 :].astype(f32)
    lane = lax.broadcasted_iota(jnp.int32, (shards, OWN, LANES), 2)
    row = lax.broadcasted_iota(jnp.int32, (shards, OWN, LANES), 1)
    ends = jnp.where(lane[:, :1] < ORDER, pltpu.roll(rest[:, 1:], ORDER, 2), rest[:, :1])
    ends = jnp.where(lane % ORDER // 2 == row, jnp.broadcast_to(ends, lane.shape), 0.0)
    ends = jnp.dot(ends.reshape(wide, LANES).astype(bf16), end_spots(True), preferred_element_type=f32)
    lane = lax.broadcasted_iota(jnp.int32, (wide, LANES), 1)
    turned = jnp.where(lane < ORDER, both, ends).T
    gcoef[...] = turned[:ORDER]
    first = x1[...].astype(f32)
    w = weight[...]
    y[...] = (x2[...].astype(f32) * conv).astype(bf16)
    prior = turned[ORDER + 2 : ORDER + 4]
    position = lax.broadcasted_iota(jnp.int32, early.shape, 0)
    mixed = early[...]
    mixed = jnp.where(
        position == 0,
        mixed + w[1:2] * prior[1:2] + w[2:3] * prior[0:1],
        jnp.where(position == 1, mixed + w[2:3] * prior[1:2], mixed),
    )
    gx1[...] = (grad * mixed).astype(bf16)
    grad_mixed = grad * first
    after = turned[ORDER : ORDER + 2]
    row = lax.broadcasted_iota(jnp.int32, grad_mixed.shape, 0)
    one = jnp.where(row == ROWS - 1, after[0:1], pltpu.roll(grad_mixed, ROWS - 1, 0))
    two = jnp.where(
        row == ROWS - 2,
        after[0:1],
        jnp.where(row == ROWS - 1, after[1:2], pltpu.roll(grad_mixed, ROWS - 2, 0)),
    )
    gvalue[...] = (w[0:1] * grad_mixed + w[1:2] * one + w[2:3] * two).astype(bf16)


def finish(back, x1, x2, early, weight):
    shape = jax.ShapeDtypeStruct(x1.shape, bf16)
    return pl.pallas_call(
        finish_kernel,
        out_shape=(
            shape,
            shape,
            shape,
            jax.ShapeDtypeStruct((ORDER, x1.shape[1]), f32),
        ),
        in_specs=[VMEM] * 5,
        out_specs=tuple([VMEM] * 4),
        compiler_params=pltpu.CompilerParams(vmem_limit_bytes=16 << 20),
        cost_estimate=pl.CostEstimate(flops=4_000_000, bytes_accessed=4_000_000, transcendentals=0),
        name="finish",
    )(back, x1, x2, early, weight)


def per_device(x1, x2, value, out_grad, short_weight, coef, rate):
    peers = lax.axis_size("chan")
    place = lax.axis_index("seq").astype(jnp.int32)[None]
    tables = make_tables(place, rate, coef, short_weight)
    sent = gate(x1, x2, value, out_grad, short_weight)
    got = lax.all_to_all(sent, "seq", split_axis=0, concat_axis=0, tiled=True)
    done = owner_emit(place, got, tables)
    late, done = lax.optimization_barrier((value, done))
    early = mix_early(late, short_weight)
    back = lax.all_to_all(done, "seq", split_axis=0, concat_axis=0, tiled=True)
    parts = rate_parts(back, early, peers)
    parts = lax.all_to_all(parts, "chan", split_axis=0, concat_axis=0, tiled=True)
    y, gx1, gvalue, gcoef = finish(back, x1, x2, early, short_weight)
    grate = jnp.sum(parts[:, :ORDER], axis=0) * (LENGTH * x1.shape[1] * peers) ** -0.5
    return (y, gx1, gvalue, gcoef, grate)


def solution(mesh):
    whole = P("seq", "chan")
    return jax.shard_map(
        per_device,
        mesh=mesh,
        in_specs=(whole, whole, whole, whole, P(None, "chan"), P(None, "chan"), P()),
        out_specs=(whole, whole, whole, P(None, "chan"), P()),
        check_vma=False,
    )
```

```python
import math

import jax
import jax.numpy as jnp
import numpy as np
from jax import lax
from jax.experimental import pallas as pl
from jax.experimental.pallas import tpu as pltpu
from jax.sharding import PartitionSpec as P

f32 = jnp.float32
bf16 = jnp.bfloat16
highest = lax.Precision.HIGHEST
LENGTH = 8192
ROWS = 128
ORDER = 64
LANES = 128
OWN = 8
WORDS = 2 * OWN + 2
BACK = 2 * OWN + 6
NT = (((1,), (1,)), ((), ()))
TN = (((0,), (0,)), ((), ()))

VMEM = pl.BlockSpec(memory_space=pltpu.VMEM)
SMEM = pl.BlockSpec(memory_space=pltpu.SMEM)


def wave_tables():
    index = np.arange(ORDER)
    cycles = (index // 2 + 1) ** 2
    odd = index % 2 == 1

    def turn(power):
        angle = 2.0 * math.pi / LENGTH * (power[:, None] * cycles[None, :] % LENGTH)
        return np.cos(angle), np.sin(angle)

    ahead = np.arange(ROWS)
    cos_a, sin_a = turn(ahead)
    cos_b, sin_b = turn(ROWS - ahead)
    real_b = np.where(odd, sin_b, cos_b)
    imag_b = np.where(odd, -cos_b, sin_b)
    wave = np.where(odd, sin_a, cos_a)
    cos_l, sin_l = turn(np.array([ROWS]))
    twice = [np.concatenate([t, t], axis=1).astype(np.float32) for t in (cos_a, sin_a, real_b, imag_b, wave)]
    step = np.concatenate([np.concatenate([t, t], axis=1) for t in (cos_l, sin_l)], axis=0).astype(np.float32)
    return (*twice, step)


def split(table):
    high = table.astype(bf16)
    low = (table - high.astype(f32)).astype(bf16)
    return jnp.concatenate([high, low], axis=0)


def table_kernel(
    place, rate, coef, weight, cos_a, sin_a, real_b, imag_b, wave, step, tx, tg, mf, me, wd, small
):
    lane = lax.broadcasted_iota(jnp.int32, (ROWS, LANES), 1)
    power = lax.broadcasted_iota(jnp.int32, (ROWS, LANES), 0).astype(f32)
    left = lane < ORDER
    slope = rate[...] * (-1.0 / LENGTH)
    env_a = jnp.exp(slope * power)
    env_b = jnp.exp(slope * (ROWS - power))
    ar = env_a * cos_a[...]
    ai = env_a * sin_a[...]
    br = env_b * real_b[...]
    bi = env_b * imag_b[...]
    back = ROWS - power
    tx[...] = split(
        jnp.concatenate([br, bi, jnp.where(left, 0.0, back * br), jnp.where(left, 0.0, back * bi)], axis=1)
    )
    tg[...] = split(
        jnp.concatenate([ar, ai, jnp.where(left, ar, power * ar), jnp.where(left, ai, power * ai)], axis=1)
    )
    mf[...] = jnp.where(left, ar, ai).astype(bf16)
    me[...] = jnp.where(left, br, bi).astype(bf16)
    w = env_a * wave[...]
    wd[...] = jnp.where(left, w, power * w)
    pick = lax.broadcasted_iota(jnp.int32, (OWN, coef.shape[1]), 1) - place[0] * OWN
    pick = (pick == lax.broadcasted_iota(jnp.int32, (OWN, coef.shape[1]), 0)).astype(f32)
    own = lax.dot_general(
        pick, jnp.concatenate([coef[...], coef[...]], axis=0), NT, precision=highest, preferred_element_type=f32
    )
    scale = own * jnp.sqrt(rate[...] * (2.0 / LENGTH))
    left8 = left[:OWN]
    decay = jnp.exp(slope * ROWS)
    small[0] = scale
    small[1] = lax.dot_general(
        jnp.where(left8, scale, 0.0), w, NT, precision=highest, preferred_element_type=f32
    )
    small[2] = jnp.broadcast_to(decay * step[0:1], (OWN, LANES))
    small[3] = jnp.broadcast_to(decay * step[1:2], (OWN, LANES))
    small[4] = jnp.where(left8, scale * (0.5 / rate[...]), scale * (-1.0 / LENGTH))
    for tap in (1, 2):
        small[5 + tap] = lax.dot_general(
            pick,
            jnp.broadcast_to(weight[tap : tap + 1], (LANES, coef.shape[1])),
            NT,
            precision=highest,
            preferred_element_type=f32,
        )
    small[5] = jnp.broadcast_to(jnp.sqrt(rate[...] * (2.0 / LENGTH)) * LENGTH ** -0.5, (OWN, LANES))


def make_tables(place, rate, coef, weight):
    consts = [jnp.asarray(t) for t in wave_tables()]
    rate2 = jnp.concatenate([rate, rate])[None, :]
    return pl.pallas_call(
        table_kernel,
        out_shape=(
            jax.ShapeDtypeStruct((2 * ROWS, 4 * LANES), bf16),
            jax.ShapeDtypeStruct((2 * ROWS, 4 * LANES), bf16),
            jax.ShapeDtypeStruct((ROWS, LANES), bf16),
            jax.ShapeDtypeStruct((ROWS, LANES), bf16),
            jax.ShapeDtypeStruct((ROWS, LANES), f32),
            jax.ShapeDtypeStruct((8, OWN, LANES), f32),
        ),
        in_specs=[SMEM] + [VMEM] * 9,
        out_specs=tuple([VMEM] * 6),
        compiler_params=pltpu.CompilerParams(vmem_limit_bytes=12 << 20),
        cost_estimate=pl.CostEstimate(flops=4_000_000, bytes_accessed=1_000_000, transcendentals=40_000),
        name="tables",
    )(place, rate2, coef, weight, *consts)


def mix(value, prior, weight):
    row = lax.broadcasted_iota(jnp.int32, value.shape, 0)
    one = jnp.where(row == 0, prior[1:2], pltpu.roll(value, 1, 0))
    two = jnp.where(row == 0, prior[0:1], jnp.where(row == 1, prior[1:2], pltpu.roll(value, 2, 0)))
    return weight[0:1] * value + weight[1:2] * one + weight[2:3] * two


def gate_kernel(x1h, x2h, vh, oh, wh, sent, x1, x2, v, o, w, sems):
    copies = [
        pltpu.make_async_copy(src, dst, sems.at[n])
        for n, (src, dst) in enumerate(((oh, o), (x2h, x2), (vh, v), (wh, w), (x1h, x1)))
    ]
    for copy in copies:
        copy.start()
    copies[0].wait()
    copies[1].wait()
    shards = sent.shape[0]
    grad = o[...].astype(f32) * x2[...].astype(f32)
    grad = grad.T.reshape(shards, OWN, ROWS)
    for copy in copies[2:]:
        copy.wait()
    value = v[...].astype(f32)
    first = x1[...].astype(f32)
    zero = jnp.zeros((2, value.shape[1]), f32)
    gated = (first * mix(value, zero, w[...])).T.reshape(shards, OWN, ROWS)
    flat = sent.reshape(shards, WORDS, ROWS)
    flat[:, : 2 * OWN] = jnp.concatenate([gated, grad], axis=1).astype(bf16)

    per = LANES // OWN
    lane = lax.broadcasted_iota(jnp.int32, (per, LANES), 1)
    row = lax.broadcasted_iota(jnp.int32, (per, LANES), 0)
    group = lax.rem(lane - row * OWN + LANES, LANES) // OWN
    edges = []
    for at in range(0, value.shape[1], LANES):
        tile = jnp.zeros((per, LANES), f32)
        for n, (source, where) in enumerate(((first, 0), (first, 1), (value, ROWS - 2), (value, ROWS - 1))):
            line = source[where : where + 1, at : at + LANES]
            line = pltpu.roll(line, n * OWN, 1) if n else line
            tile = jnp.where(group == n, line, tile)
        edges.append(tile)
    edges = jnp.concatenate(edges, axis=0)
    flat[:, 2 * OWN :] = jnp.broadcast_to(edges[:, None, :], (shards, 2, LANES)).astype(bf16)


def gate(x1, x2, value, out_grad, weight):
    shards = x1.shape[1] // OWN
    return pl.pallas_call(
        gate_kernel,
        out_shape=jax.ShapeDtypeStruct((shards, WORDS // 2, 2, ROWS), bf16),
        in_specs=[pl.BlockSpec(memory_space=pltpu.HBM)] * 5,
        out_specs=VMEM,
        scratch_shapes=[pltpu.VMEM(x1.shape, bf16)] * 4
        + [pltpu.VMEM(weight.shape, f32), pltpu.SemaphoreType.DMA((5,))],
        compiler_params=pltpu.CompilerParams(vmem_limit_bytes=(64 << 20) - (64 << 10)),
        name="gate",
    )(x1, x2, value, out_grad, weight)


def owner_kernel(
    place, got, tx, tg, wd, small, part_out, coef_out, us, ug, xb_out, head_out, gs, rs, ex, eg, sr, si, gr, gi
):
    chunks = got.shape[0]
    rows = chunks * OWN
    flat = got.reshape(chunks, WORDS, ROWS)
    both = flat[:, : 2 * OWN].astype(f32)
    edge = flat[:, 2 * OWN :].astype(f32)[:, :1]
    edge = jnp.broadcast_to(edge, (chunks, OWN, LANES)).reshape(rows, LANES)
    edge = pltpu.roll(edge, lax.rem(ORDER * LANES - place[0] * OWN, LANES), 1)
    lane3 = lax.broadcasted_iota(jnp.int32, (rows, LANES), 1)
    row3 = lax.broadcasted_iota(jnp.int32, (rows, LANES), 0)
    edge = jnp.where(lane3 % OWN == row3 % OWN, edge, 0.0).astype(bf16)
    group = lax.broadcasted_iota(jnp.int32, (LANES, LANES), 0) // OWN
    to = lax.broadcasted_iota(jnp.int32, (LANES, LANES), 1)
    spot_x1 = ((group < 2) & (to % ORDER == group)).astype(bf16)
    spot_v = (((group == 2) & (to == 0)) | ((group == 3) & (to == 1))).astype(bf16)
    spot_last = ((group == 3) & (to == 0)).astype(bf16)
    spread = jnp.dot(
        edge, jnp.concatenate([spot_x1, spot_v, spot_last], axis=1), preferred_element_type=f32
    )
    x1_head = spread[:, :LANES]
    before = (
        small[7] * spread[:, LANES : 2 * LANES].reshape(chunks, OWN, LANES)
        + small[6] * spread[:, 2 * LANES :].reshape(chunks, OWN, LANES)
    )
    before = jnp.concatenate([jnp.zeros((1, OWN, LANES), f32), before[:-1]], axis=0)
    x = both[:, :OWN].reshape(rows, ROWS) + x1_head * before.reshape(rows, LANES)
    g = both[:, OWN:].reshape(rows, ROWS)
    gs[...] = g
    xb = x.astype(bf16)
    xb_out[...] = xb
    head_out[...] = jnp.where(lane3 < ORDER, spread[:, LANES : 2 * LANES], x1_head)
    gb = g.astype(bf16)
    here = lax.broadcasted_iota(jnp.int32, (ROWS, ROWS), 0)
    there = lax.broadcasted_iota(jnp.int32, (ROWS, ROWS), 1)
    mirror = (here + there == ROWS - 1).astype(bf16)
    rs[...] = jnp.dot(xb, mirror, preferred_element_type=f32)
    ex[...] = jnp.dot(
        jnp.concatenate([xb, xb], axis=1), tx[...], preferred_element_type=f32
    )
    eg[...] = jnp.dot(
        jnp.concatenate([gb, gb], axis=1), tg[...], preferred_element_type=f32
    )
    scale = small[0]
    lr = small[2]
    li = small[3]

    a = b = c = d = jnp.zeros((OWN, LANES), f32)
    for k in range(chunks):
        at = pl.ds(k * OWN, OWN)
        sr[at] = a
        si[at] = b
        a, b = (
            lr * a - li * b + ex[at, 0:LANES],
            lr * b + li * a + ex[at, LANES : 2 * LANES],
        )
        at = pl.ds((chunks - 1 - k) * OWN, OWN)
        gr[at] = c
        gi[at] = d
        c, d = (
            lr * c - li * d + eg[at, 0:LANES],
            lr * d + li * c + eg[at, LANES : 2 * LANES],
        )

    left = lax.broadcasted_iota(jnp.int32, (OWN, LANES), 1) < ORDER

    def cube(array):
        return array.reshape(chunks, OWN, LANES)

    s_r, s_i, g_r, g_i = (cube(ref[...]) for ref in (sr, si, gr, gi))
    over = jnp.where(left, 0.0, float(ROWS))
    ahead_r = over * lr * g_r - over * li * g_i
    ahead_i = over * lr * g_i + over * li * g_r
    total = (
        s_r * (cube(eg[:, 2 * LANES : 3 * LANES]) + ahead_r)
        - s_i * (cube(eg[:, 3 * LANES : 4 * LANES]) + ahead_i)
        + g_r * cube(ex[:, 2 * LANES : 3 * LANES])
        - g_i * cube(ex[:, 3 * LANES : 4 * LANES])
    )
    total = jnp.sum(total, axis=0)
    us[...] = jnp.where(left, scale * s_r, -scale * s_i).reshape(rows, LANES).astype(bf16)
    ug[...] = jnp.where(left, scale * g_r, -scale * g_i).reshape(rows, LANES).astype(bf16)

    inside = (there < here) | (there == ROWS - 1)
    lags = []
    for ch in range(OWN):
        at = pl.ds(ch, chunks, stride=OWN)
        pairs = lax.dot_general(
            rs[at, :].astype(bf16), gs[at, :].astype(bf16), TN, preferred_element_type=f32
        )
        pairs = pltpu.roll(pairs, 0, 1, stride=1, stride_axis=0)
        lags.append(jnp.sum(jnp.where(inside, pairs, 0.0), axis=0, keepdims=True))
    lags = pltpu.roll(jnp.concatenate(lags, axis=0), 1, 1)
    total = total + jnp.dot(lags, wd[...], precision=highest, preferred_element_type=f32)
    coef_out[...] = total * small[5]
    part = jnp.sum(total * small[4], axis=0, keepdims=True)
    part_out[...] = jnp.broadcast_to(part + pltpu.roll(part, ORDER, 1), part_out.shape)


def emit_kernel(got, parts, coef, us, ug, xb, head, mf, me, small, out, xs, gs, yc, yg):
    chunks = got.shape[0]
    rows = chunks * OWN

    def cube(array):
        return array.reshape(chunks, OWN, LANES)

    xs[...] = xb[...].astype(f32)
    yc[...] = lax.dot_general(us[...], mf[...], NT, preferred_element_type=f32)
    yg[...] = lax.dot_general(ug[...], me[...], NT, preferred_element_type=f32)
    here = lax.broadcasted_iota(jnp.int32, (ROWS, ROWS), 0)
    there = lax.broadcasted_iota(jnp.int32, (ROWS, ROWS), 1)
    later = there >= here
    filt = small[1]
    for ch in range(OWN):
        at = pl.ds(ch, chunks, stride=OWN)
        toeplitz = pltpu.roll(
            jnp.broadcast_to(filt[ch : ch + 1], (ROWS, ROWS)), 0, 1, stride=1, stride_axis=0
        )
        toeplitz = jnp.where(later, toeplitz, 0.0).astype(bf16)
        yc[at, :] += jnp.dot(xs[at, :].astype(bf16), toeplitz, preferred_element_type=f32)
        yg[at, :] += lax.dot_general(gs[at, :].astype(bf16), toeplitz, NT, preferred_element_type=f32)

    flat = out.reshape(chunks, BACK, ROWS)
    flat[:, : 2 * OWN] = jnp.concatenate([cube(yc[...]), cube(yg[...])], axis=1).astype(bf16)
    lane = lax.broadcasted_iota(jnp.int32, (OWN, LANES), 1)
    row = lax.broadcasted_iota(jnp.int32, (OWN, LANES), 0)
    both = jnp.where(lane < ORDER, coef[...], pltpu.roll(pltpu.roll(coef[...], ORDER, 1), OWN // 2, 0))
    flat[:, 2 * OWN : 2 * OWN + 4] = jnp.broadcast_to(both[: OWN // 2], (chunks, OWN // 2, LANES)).astype(bf16)
    lane2 = lax.broadcasted_iota(jnp.int32, (rows, LANES), 1)
    ends = jnp.where(lane2 < ORDER, head[...], pltpu.roll(yg[...], ORDER, 1) * head[...]).astype(bf16)
    ends = cube(jnp.dot(ends, end_spots(False), preferred_element_type=f32))
    ends = jnp.sum(jnp.where(lane % ORDER // 2 == row, ends, 0.0), axis=1, keepdims=True)
    none = jnp.zeros((1, 1, LANES), f32)
    part = jnp.sum(parts[...], axis=0, keepdims=True)
    low = part - part.astype(bf16).astype(f32)
    left = lane[:1] < ORDER
    high = jnp.where(left, part, jnp.concatenate([ends[1:], none], axis=0))
    ends = pltpu.roll(jnp.concatenate([none, ends[:-1]], axis=0), ORDER, 2)
    low = jnp.where(left, low, ends)
    flat[:, 2 * OWN + 4 :] = jnp.concatenate([high, low], axis=1).astype(bf16)


def end_spots(turned):
    few = lax.broadcasted_iota(jnp.int32, (LANES, LANES), 1 if turned else 0)
    many = lax.broadcasted_iota(jnp.int32, (LANES, LANES), 0 if turned else 1)
    hit = (many % ORDER < 2 * OWN) & (few % 2 == many % 2)
    if turned:
        hit &= few // 2 == jnp.where(many < ORDER, ORDER // 2 + 1, ORDER // 2)
    else:
        hit &= few // 2 == many // ORDER * (ORDER // 2)
    return hit.astype(bf16)


def owner_emit_kernel(
    place, got, tx, tg, mf, me, wd, small, out, part, coef, us, ug, xb, head, gs, rs, ex, eg, sr, si, gr, gi, xs, yc, yg
):
    owner_kernel(place, got, tx, tg, wd, small, part, coef, us, ug, xb, head, gs, rs, ex, eg, sr, si, gr, gi)
    emit_kernel(got, part, coef, us, ug, xb, head, mf, me, small, out, xs, gs, yc, yg)


def owner_emit(place, got, tables):
    chunks = got.shape[0]
    rows = chunks * OWN
    wide = pltpu.VMEM((rows, LANES), f32)
    flat = pltpu.VMEM((rows, LANES), bf16)
    tall = pltpu.VMEM((rows, 4 * LANES), f32)
    return pl.pallas_call(
        owner_emit_kernel,
        out_shape=jax.ShapeDtypeStruct((chunks, BACK // 2, 2, ROWS), bf16),
        in_specs=[SMEM] + [VMEM] * 7,
        out_specs=VMEM,
        scratch_shapes=[pltpu.VMEM((1, LANES), f32), pltpu.VMEM((OWN, LANES), f32)]
        + [flat] * 3
        + [wide] * 3
        + [tall] * 2
        + [wide] * 7,
        compiler_params=pltpu.CompilerParams(vmem_limit_bytes=24 << 20),
        name="owner",
    )(place, got, *tables)


def rate_kernel(back, parts):
    flat = back.reshape(back.shape[0], BACK, ROWS)
    rates = jnp.sum(jnp.sum(flat[:, 2 * OWN + 4 :].astype(f32), axis=0), axis=0, keepdims=True)
    parts[...] = jnp.broadcast_to(rates, parts.shape)


def rate_parts(back, peers):
    return pl.pallas_call(
        rate_kernel,
        out_shape=jax.ShapeDtypeStruct((peers, LANES), f32),
        in_specs=[VMEM],
        out_specs=VMEM,
        compiler_params=pltpu.CompilerParams(vmem_limit_bytes=8 << 20),
        name="rates",
    )(back)


def finish_kernel(back, x1, x2, value, weight, y, gx1, gvalue, gcoef):
    shards = back.shape[0]
    wide = shards * OWN
    every = back.reshape(shards, BACK, ROWS)
    both = every[:, : 2 * OWN].astype(f32)
    conv = both[:, :OWN].reshape(wide, ROWS).T
    grad = both[:, OWN:].reshape(wide, ROWS).T
    both = every[:, 2 * OWN : 2 * OWN + 4].astype(f32)
    both = jnp.concatenate([both, pltpu.roll(both, ORDER, 2)], axis=1).reshape(wide, LANES)
    rest = every[:, 2 * OWN + 4 :].astype(f32)
    lane = lax.broadcasted_iota(jnp.int32, (shards, OWN, LANES), 2)
    row = lax.broadcasted_iota(jnp.int32, (shards, OWN, LANES), 1)
    ends = jnp.where(lane[:, :1] < ORDER, pltpu.roll(rest[:, 1:], ORDER, 2), rest[:, :1])
    ends = jnp.where(lane % ORDER // 2 == row, jnp.broadcast_to(ends, lane.shape), 0.0)
    ends = jnp.dot(ends.reshape(wide, LANES).astype(bf16), end_spots(True), preferred_element_type=f32)
    lane = lax.broadcasted_iota(jnp.int32, (wide, LANES), 1)
    turned = jnp.where(lane < ORDER, both, ends).T
    gcoef[...] = turned[:ORDER]
    first = x1[...].astype(f32)
    w = weight[...]
    y[...] = (x2[...].astype(f32) * conv).astype(bf16)
    mixed = mix(value[...].astype(f32), turned[ORDER + 2 : ORDER + 4], w)
    gx1[...] = (grad * mixed).astype(bf16)
    grad_mixed = grad * first
    after = turned[ORDER : ORDER + 2]
    row = lax.broadcasted_iota(jnp.int32, grad_mixed.shape, 0)
    one = jnp.where(row == ROWS - 1, after[0:1], pltpu.roll(grad_mixed, ROWS - 1, 0))
    two = jnp.where(
        row == ROWS - 2,
        after[0:1],
        jnp.where(row == ROWS - 1, after[1:2], pltpu.roll(grad_mixed, ROWS - 2, 0)),
    )
    gvalue[...] = (w[0:1] * grad_mixed + w[1:2] * one + w[2:3] * two).astype(bf16)


def finish(back, x1, x2, value, weight):
    shape = jax.ShapeDtypeStruct(x1.shape, bf16)
    return pl.pallas_call(
        finish_kernel,
        out_shape=(
            shape,
            shape,
            shape,
            jax.ShapeDtypeStruct((ORDER, x1.shape[1]), f32),
        ),
        in_specs=[VMEM] * 5,
        out_specs=tuple([VMEM] * 4),
        compiler_params=pltpu.CompilerParams(vmem_limit_bytes=16 << 20),
        cost_estimate=pl.CostEstimate(flops=4_000_000, bytes_accessed=4_000_000, transcendentals=0),
        name="finish",
    )(back, x1, x2, value, weight)


def per_device(x1, x2, value, out_grad, short_weight, coef, rate):
    peers = lax.axis_size("chan")
    place = lax.axis_index("seq").astype(jnp.int32)[None]
    tables = make_tables(place, rate, coef, short_weight)
    sent = gate(x1, x2, value, out_grad, short_weight)
    got = lax.all_to_all(sent, "seq", split_axis=0, concat_axis=0, tiled=True)
    done = owner_emit(place, got, tables)
    back = lax.all_to_all(done, "seq", split_axis=0, concat_axis=0, tiled=True)
    parts = rate_parts(back, peers)
    parts = lax.all_to_all(parts, "chan", split_axis=0, concat_axis=0, tiled=True)
    y, gx1, gvalue, gcoef = finish(back, x1, x2, value, short_weight)
    grate = jnp.sum(parts[:, :ORDER], axis=0) * (LENGTH * x1.shape[1] * peers) ** -0.5
    return (y, gx1, gvalue, gcoef, grate)


def solution(mesh):
    whole = P("seq", "chan")
    return jax.shard_map(
        per_device,
        mesh=mesh,
        in_specs=(whole, whole, whole, whole, P(None, "chan"), P(None, "chan"), P()),
        out_specs=(whole, whole, whole, P(None, "chan"), P()),
        check_vma=False,
    )
```
